32 devices in a mesh: layer: 4 (over z), ex: 8 (over y, x, core).
Axes of the slice: x: 2, y: 2, z: 4, core: 2. Of those that a mesh axis runs over, the one named last changes fastest.
Arguments:
- train_grads: bfloat16 [4096, 4, 4096], P('ex', 'layer'), may hold values from -0.3984375 to 0.3984375
- query_grads: bfloat16 [512, 4, 4096], P('ex', 'layer'), may hold values from -0.3984375 to 0.3984375
- in_precond: float32 [4, 64, 64], P('layer'), as said below
- out_precond: float32 [4, 64, 64], P('layer'), as said below
- pair_blocks: int32 [48], replicated, may hold values from -1 to 31, as said below
Outputs:
- tile_out: float32 [16, 48, 512], P('layer', 'ex')
The draws below stay inside these ranges and needn't reach their ends.
Inputs may be any that keep to these rules, and one draw needn't show every extreme that they name: `pair_blocks`: slots p of training block p // 6 name query blocks (query block q holds judged examples q * 16 to q * 16 + 15 and lies on ex index q // 4), or -1 for an empty slot; the blocks named by one training block lie on distinct ex indices; empty slots come after filled ones; every training block fills at least 1 slots and some training block fills all 6. `in_precond`: each layer's factor is symmetric positive definite. `out_precond`: each layer's factor is symmetric positive definite.
All inputs are finite; a program needn't handle non-finite values.
Results may differ from the reference program's by a relative error of at most 0.0029.
Values may be sent and summed in bfloat16 or wider, within the bound.
No kernel may reach another device: no remote copies, remote signals or barrier semaphores. Data moves between devices by JAX's collectives and lax.ppermute only.
A program may use at most 64 MiB of HBM per device.

```python
import jax
import jax.numpy as jnp
from jax import lax

DIN = 64
DOUT = 64
TROWS = 512
QBLK = 16
QB_DEV = 4
F = 4096
LAYERS = 4
SLOTS = 6
TRAIN = 4096
QUERIES = 512
N_EX = 8


def factor_draw(key, width):
    noise = jax.random.normal(jax.random.fold_in(key, 1), (LAYERS, width, width), jnp.float32)
    mirror = (noise + jnp.swapaxes(noise, 1, 2)) / jnp.sqrt(2.0 * width)
    scales = jnp.exp(jax.random.uniform(jax.random.fold_in(key, 2), (LAYERS, 1, 1), jnp.float32, -0.7, 0.7))
    return scales * (jnp.eye(width, dtype=jnp.float32)[None] + 0.35 * mirror)


def draw_in_precond(key, part):
    return factor_draw(jax.random.fold_in(key, 11), DIN)


def draw_out_precond(key, part):
    return factor_draw(jax.random.fold_in(key, 12), DOUT)


def draw_pair_blocks(key, part):
    owner_keys = jax.random.split(jax.random.fold_in(key, 7), N_EX)
    sources = jax.vmap(lambda subkey: jax.random.permutation(subkey, N_EX))(owner_keys)[:, :SLOTS]
    within = jax.random.randint(jax.random.fold_in(key, 8), (N_EX, SLOTS), 0, QB_DEV)
    filled = jax.random.randint(jax.random.fold_in(key, 9), (N_EX,), SLOTS // 4, SLOTS + 1)
    full_owner = jax.random.randint(jax.random.fold_in(key, 10), (), 0, N_EX)
    filled = jnp.where(jnp.arange(N_EX) == full_owner, SLOTS, filled)
    block_ids = sources * QB_DEV + within
    block_ids = jnp.where(jnp.arange(SLOTS)[None, :] < filled[:, None], block_ids, -1)
    return block_ids.reshape(-1).astype(jnp.int32)


def block_scale(rng, extent, cuts, smallest, largest):
    factor_of = 1.0
    for position, blocks in cuts:
        draws = jax.random.uniform(jax.random.fold_in(jax.random.fold_in(rng, 6), position), (blocks,), jnp.float32, smallest / len(cuts), largest / len(cuts))
        factor_of = factor_of * jnp.repeat(jnp.exp(draws), extent[position] // blocks).reshape((-1,) + (1,) * (len(extent) - 1 - position))
    return factor_of


def normal_values(rng, dims, scale, bound, pieces=(), kind=jnp.bfloat16):
    array = jax.random.normal(rng, dims, jnp.float32) * scale
    if len(pieces) > 0:
        array = block_scale(rng, dims, pieces, -0.22, 0.18) * array
    return jnp.clip(array, min=-bound, max=bound).astype(kind)


def setup_inputs(seed: int = 0) -> dict:
    seeds = jax.random.split(jax.random.key(seed), 6)
    train_grads = normal_values(seeds[0], (TRAIN, LAYERS, F), 0.0625, 0.3984375, ((0, 8), (1, 4)))
    query_grads = normal_values(seeds[1], (QUERIES, LAYERS, F), 0.0625, 0.3984375, ((0, 8), (1, 4)))
    in_precond = draw_in_precond(jax.random.fold_in(seeds[5], 71), 0)
    out_precond = draw_out_precond(jax.random.fold_in(seeds[5], 71), 0)
    pair_blocks = draw_pair_blocks(jax.random.fold_in(seeds[5], 71), 0)
    return dict(train_grads=train_grads, query_grads=query_grads, in_precond=in_precond, out_precond=out_precond, pair_blocks=pair_blocks)


def precondition(queries, in_precond, out_precond):
    matrices = queries.astype(jnp.float32).reshape(queries.shape[0], LAYERS, DOUT, DIN)
    left_side = jnp.einsum("loj,rlji->rloi", out_precond, matrices, precision=lax.Precision.HIGHEST)
    precond = jnp.einsum("rloi,lik->rlok", left_side, in_precond, precision=lax.Precision.HIGHEST)
    return precond.reshape(queries.shape[0], LAYERS * F).astype(jnp.bfloat16)


def reference(train_grads, query_grads, in_precond, out_precond, pair_blocks):
    prepared = precondition(query_grads, in_precond, out_precond)
    train_flat = train_grads.reshape(TRAIN, LAYERS * F)

    def one_pair(pair_index):
        block_id = pair_blocks[pair_index]
        owner_id = (pair_index // SLOTS).astype(jnp.int32)
        query_start = (jnp.maximum(block_id, 0) * QBLK).astype(jnp.int32)
        query_rows = lax.dynamic_slice_in_dim(prepared, query_start, QBLK, 0)
        train_rows = lax.dynamic_slice_in_dim(train_flat, (owner_id * TROWS).astype(jnp.int32), TROWS, 0)
        tile_value = jnp.dot(query_rows, train_rows.T, preferred_element_type=jnp.float32)
        return jnp.where(block_id >= 0, tile_value, jnp.zeros_like(tile_value))

    tiles = lax.map(one_pair, jnp.arange(N_EX * SLOTS, dtype=jnp.int32))
    return jnp.transpose(tiles, (1, 0, 2))
```

```python
import functools

import jax
import jax.numpy as jnp
from jax import lax
from jax.experimental import pallas as pl
from jax.experimental.pallas import tpu as pltpu
from jax.sharding import PartitionSpec as P

QBLK = 16
LANES = 128
F32 = jnp.float32
BF16 = jnp.bfloat16

ANY = pl.BlockSpec(memory_space=pl.ANY)
VMEM = pl.BlockSpec(memory_space=pltpu.VMEM)
SMEM = pl.BlockSpec(memory_space=pltpu.SMEM)


def split_bf16(x):
    high = x.astype(BF16)
    return high, (x - high.astype(F32)).astype(BF16)


def over_slots(slots, body, init):
    if slots > 8:
        return lax.fori_loop(0, slots, body, init)
    for slot in range(slots):
        init = body(slot, init)
    return init


def pick_kernel(ex, held, slots, pairs_ref, query_ref, *rest):
    outs, sems = rest[:ex], rest[ex]
    me = lax.axis_index("ex")
    copies = []
    for k in reversed(range(ex)):
        first = (me ^ k) * slots

        def body(slot, block):
            local = pairs_ref[first + slot] - me * held
            return jnp.where((local >= 0) & (local < held), local, block)

        block = over_slots(slots, body, jnp.int32(0))
        start = pl.multiple_of(block * QBLK, QBLK)
        copy = pltpu.make_async_copy(query_ref.at[pl.ds(start, QBLK)], outs[k], sems.at[k])
        copy.start()
        copies.append(copy)
    for copy in copies:
        copy.wait()


def factor_kernel(out_ref, in_ref, left_ref, right_ref):
    width = out_ref.shape[0]
    in_width = in_ref.shape[0]
    half = left_ref.shape[2]
    span = right_ref.shape[1]
    outs = split_bf16(out_ref[...])
    ins = split_bf16(in_ref[...])
    row = lax.broadcasted_iota(jnp.int32, (half, width), 0) // QBLK
    row_o = lax.broadcasted_iota(jnp.int32, (half, width), 1)
    col = lax.broadcasted_iota(jnp.int32, (width, half), 1) // QBLK
    col_o = lax.broadcasted_iota(jnp.int32, (width, half), 0)
    same = (lax.broadcasted_iota(jnp.int32, (half, half), 0) % QBLK) == (
        lax.broadcasted_iota(jnp.int32, (half, half), 1) % QBLK
    )
    for h in range(2):
        for s in range(2):
            pick_rows = (row * 2 + s == row_o).astype(BF16)
            rows = jnp.dot(pick_rows, outs[h], preferred_element_type=F32).astype(BF16)
            for t in range(2):
                pick_cols = (col * 2 + (s ^ t) == col_o).astype(BF16)
                spread = jnp.dot(rows, pick_cols, preferred_element_type=F32)
                left_ref[h, s, :, t * half : (t + 1) * half] = jnp.where(same, spread, 0.0).astype(BF16)
        up = (
            lax.broadcasted_iota(jnp.int32, (span, in_width), 0) % in_width
            == lax.broadcasted_iota(jnp.int32, (span, in_width), 1)
        ).astype(BF16)
        down = (
            lax.broadcasted_iota(jnp.int32, (in_width, span), 1) % in_width
            == lax.broadcasted_iota(jnp.int32, (in_width, span), 0)
        ).astype(BF16)
        wide = jnp.dot(
            jnp.dot(up, ins[h], preferred_element_type=F32).astype(BF16), down, preferred_element_type=F32
        )
        block = (lax.broadcasted_iota(jnp.int32, (span, span), 0) // in_width) == (
            lax.broadcasted_iota(jnp.int32, (span, span), 1) // in_width
        )
        right_ref[h] = jnp.where(block, wide, 0.0).astype(BF16)


def prepare(blocks, left_ref, right_ref, prep_ref):
    chunks = blocks[0].shape[1] // LANES
    half = LANES // 2
    stacked = []
    for block in blocks:
        tall = jnp.concatenate([block[:, c * LANES : (c + 1) * LANES] for c in range(chunks)], axis=0)
        turned = jnp.concatenate([tall[:, half:], tall[:, :half]], axis=1)
        stacked.append(jnp.concatenate([tall, turned], axis=0))
    stacked = jnp.concatenate(stacked, axis=1)
    parts = [
        jnp.dot(left_ref[0, s], stacked, preferred_element_type=F32)
        + jnp.dot(left_ref[1, s], stacked, preferred_element_type=F32)
        for s in range(2)
    ]
    lane = lax.broadcasted_iota(jnp.int32, parts[0].shape, 1) % LANES
    high, low = split_bf16(jnp.where(lane < half, parts[0], parts[1]))
    done = (
        jnp.dot(high, right_ref[0], preferred_element_type=F32)
        + jnp.dot(low, right_ref[0], preferred_element_type=F32)
        + jnp.dot(high, right_ref[1], preferred_element_type=F32)
    ).astype(BF16)
    for b in range(len(blocks)):
        for c in range(chunks):
            prep_ref[b * QBLK : (b + 1) * QBLK, c * LANES : (c + 1) * LANES] = done[
                c * QBLK : (c + 1) * QBLK, b * LANES : (b + 1) * LANES
            ]


def tile_kernel(ex, layer, *refs):
    blocks = refs[:ex]
    train_ref, left_ref, right_ref = refs[ex : ex + 3]
    outs = refs[ex + 3 : ex + 3 + layer]
    prep_ref, tile_ref = refs[ex + 3 + layer :]
    rows = QBLK // layer
    for pair in range(ex // 2):
        prepare(
            [blocks[2 * pair][...], blocks[2 * pair + 1][...]],
            left_ref,
            right_ref,
            prep_ref.at[pl.ds(pair * 2 * QBLK, 2 * QBLK)],
        )
    tile = lax.dot_general(
        prep_ref[...], train_ref[...], (((1,), (1,)), ((), ())), preferred_element_type=F32
    )
    me = lax.axis_index("layer")
    for c in range(tile_ref.shape[0]):
        lanes = slice(c * LANES, (c + 1) * LANES)
        tile_ref[c] = tile[:, lanes]
        for m in range(layer):
            first = (me ^ m) * rows
            part = jnp.concatenate(
                [tile_ref[c, pl.ds(first + j, ex, stride=QBLK), :] for j in range(rows)], axis=0
            )
            outs[m][:, lanes] = part.astype(outs[m].dtype)


def finish_kernel(ex, layer, held, slots, pairs_ref, *refs):
    parts, out_ref, sum_ref = refs[:layer], refs[layer], refs[layer + 1]
    total = parts[0][...]
    for part in parts[1:]:
        total = total + part[...].astype(F32)
    chunks = sum_ref.shape[0]
    for c in range(chunks):
        sum_ref[c] = total[:, c * LANES : (c + 1) * LANES]
    rows = QBLK // layer
    me = lax.axis_index("ex")

    def body(slot, carry):
        q = pairs_ref[me * slots + slot]
        k = jnp.where(q >= 0, (q // held) ^ me, 0)
        for c in range(chunks):
            value = sum_ref[c, pl.ds(k, rows, stride=ex), :]
            out_ref[slot, :, c * LANES : (c + 1) * LANES] = jnp.where(q >= 0, value, jnp.zeros_like(value))
        return carry

    over_slots(slots, body, 0)


def shards(train_grads, query_grads, in_precond, out_precond, pair_blocks):
    ex = lax.axis_size("ex")
    layer = lax.axis_size("layer")
    train_rows, layers, features = train_grads.shape
    assert layers == 1
    held = query_grads.shape[0] // QBLK
    slots = pair_blocks.shape[0] // ex
    rows = QBLK // layer
    train = train_grads.reshape(train_rows, features)
    query = query_grads.reshape(query_grads.shape[0], features)
    in_factor = in_precond.reshape(in_precond.shape[1:])
    out_factor = out_precond.reshape(out_precond.shape[1:])
    limit = pltpu.CompilerParams(vmem_limit_bytes=48 * 2**20)

    picked = pl.pallas_call(
        functools.partial(pick_kernel, ex, held, slots),
        out_shape=[jax.ShapeDtypeStruct((QBLK, features), BF16)] * ex,
        in_specs=[SMEM, ANY],
        out_specs=[ANY] * ex,
        scratch_shapes=[pltpu.SemaphoreType.DMA((ex,))],
        name="pick",
    )(pair_blocks, query)

    blocks = [None] * ex
    blocks[0] = picked[0]
    for k in reversed(range(1, ex)):
        blocks[k] = lax.ppermute(picked[k], "ex", [(i, i ^ k) for i in range(ex)])

    stack = features // LANES * QBLK
    span = 2 * LANES
    left, right = pl.pallas_call(
        factor_kernel,
        out_shape=[
            jax.ShapeDtypeStruct((2, 2, stack, 2 * stack), BF16),
            jax.ShapeDtypeStruct((2, span, span), BF16),
        ],
        in_specs=[VMEM, VMEM],
        out_specs=[VMEM, VMEM],
        compiler_params=limit,
        name="factors",
    )(out_factor, in_factor)

    parts = pl.pallas_call(
        functools.partial(tile_kernel, ex, layer),
        out_shape=[jax.ShapeDtypeStruct((rows * ex, train_rows), F32)]
        + [jax.ShapeDtypeStruct((rows * ex, train_rows), BF16)] * (layer - 1),
        in_specs=[VMEM] * (ex + 3),
        out_specs=[VMEM] * layer,
        scratch_shapes=[
            pltpu.VMEM((ex * QBLK, features), BF16),
            pltpu.VMEM((train_rows // LANES, ex * QBLK, LANES), F32),
        ],
        compiler_params=limit,
        name="tiles",
    )(*blocks, train, left, right)

    terms = [parts[0]] + [
        lax.ppermute(parts[m], "layer", [(i, i ^ m) for i in range(layer)]) for m in range(1, layer)
    ]
    out = pl.pallas_call(
        functools.partial(finish_kernel, ex, layer, held, slots),
        out_shape=jax.ShapeDtypeStruct((slots, rows, train_rows), F32),
        in_specs=[SMEM] + [VMEM] * layer,
        out_specs=VMEM,
        scratch_shapes=[pltpu.VMEM((train_rows // LANES, rows * ex, LANES), F32)],
        name="finish",
    )(pair_blocks, *terms)
    return jnp.transpose(out, (1, 0, 2))


def solution(mesh):
    in_specs = (
        P("ex", "layer", None),
        P("ex", "layer", None),
        P("layer", None, None),
        P("layer", None, None),
        P(),
    )
    out_specs = P("layer", "ex", None)
    return jax.shard_map(shards, mesh=mesh, in_specs=in_specs, out_specs=out_specs, check_vma=False)
```

```python
import functools

import jax
import jax.numpy as jnp
from jax import lax
from jax.experimental import pallas as pl
from jax.experimental.pallas import tpu as pltpu
from jax.sharding import PartitionSpec as P

QBLK = 16
LANES = 128
F32 = jnp.float32
BF16 = jnp.bfloat16

VMEM = pl.BlockSpec(memory_space=pltpu.VMEM)
SMEM = pl.BlockSpec(memory_space=pltpu.SMEM)


def split_bf16(x):
    high = x.astype(BF16)
    return high, (x - high.astype(F32)).astype(BF16)


def over_slots(slots, body, init):
    if slots > 8:
        return lax.fori_loop(0, slots, body, init)
    for slot in range(slots):
        init = body(slot, init)
    return init


def pick_kernel(ex, held, slots, pairs_ref, query_ref, *outs):
    me = lax.axis_index("ex")
    for k in range(ex):
        first = (me ^ k) * slots

        def body(slot, block):
            local = pairs_ref[first + slot] - me * held
            return jnp.where((local >= 0) & (local < held), local, block)

        block = over_slots(slots, body, jnp.int32(0))
        outs[k][...] = query_ref[pl.ds(pl.multiple_of(block * QBLK, QBLK), QBLK), :]


def factor_kernel(rows, out_ref, in_ref, left_ref, right_ref):
    width = out_ref.shape[0]
    in_width = in_ref.shape[0]
    half = left_ref.shape[2]
    span = right_ref.shape[1]
    outs = split_bf16(out_ref[...])
    ins = split_bf16(in_ref[...])
    row = lax.broadcasted_iota(jnp.int32, (half, width), 0) // QBLK
    row_o = lax.broadcasted_iota(jnp.int32, (half, width), 1)
    col = lax.broadcasted_iota(jnp.int32, (width, half), 1) // QBLK
    col_o = lax.broadcasted_iota(jnp.int32, (width, half), 0)
    a = lax.broadcasted_iota(jnp.int32, (half, half), 0) % QBLK
    a = ((a // rows) ^ lax.axis_index("layer")) * rows + a % rows
    same = a == (lax.broadcasted_iota(jnp.int32, (half, half), 1) % QBLK)
    for h in range(2):
        for s in range(2):
            pick_rows = (row * 2 + s == row_o).astype(BF16)
            rows = jnp.dot(pick_rows, outs[h], preferred_element_type=F32).astype(BF16)
            for t in range(2):
                pick_cols = (col * 2 + (s ^ t) == col_o).astype(BF16)
                spread = jnp.dot(rows, pick_cols, preferred_element_type=F32)
                left_ref[h, s, :, t * half : (t + 1) * half] = jnp.where(same, spread, 0.0).astype(BF16)
        up = (
            lax.broadcasted_iota(jnp.int32, (span, in_width), 0) % in_width
            == lax.broadcasted_iota(jnp.int32, (span, in_width), 1)
        ).astype(BF16)
        down = (
            lax.broadcasted_iota(jnp.int32, (in_width, span), 1) % in_width
            == lax.broadcasted_iota(jnp.int32, (in_width, span), 0)
        ).astype(BF16)
        wide = jnp.dot(
            jnp.dot(up, ins[h], preferred_element_type=F32).astype(BF16), down, preferred_element_type=F32
        )
        block = (lax.broadcasted_iota(jnp.int32, (span, span), 0) // in_width) == (
            lax.broadcasted_iota(jnp.int32, (span, span), 1) // in_width
        )
        right_ref[h] = jnp.where(block, wide, 0.0).astype(BF16)


def prepare(blocks, left_ref, right_ref, prep_ref):
    chunks = blocks[0].shape[1] // LANES
    half = LANES // 2
    stacked = []
    for block in blocks:
        tall = jnp.concatenate([block[:, c * LANES : (c + 1) * LANES] for c in range(chunks)], axis=0)
        turned = jnp.concatenate([tall[:, half:], tall[:, :half]], axis=1)
        stacked.append(jnp.concatenate([tall, turned], axis=0))
    stacked = jnp.concatenate(stacked, axis=1)
    parts = [
        jnp.dot(left_ref[0, s], stacked, preferred_element_type=F32)
        + jnp.dot(left_ref[1, s], stacked, preferred_element_type=F32)
        for s in range(2)
    ]
    lane = lax.broadcasted_iota(jnp.int32, parts[0].shape, 1) % LANES
    high, low = split_bf16(jnp.where(lane < half, parts[0], parts[1]))
    done = (
        jnp.dot(high, right_ref[0], preferred_element_type=F32)
        + jnp.dot(low, right_ref[0], preferred_element_type=F32)
        + jnp.dot(high, right_ref[1], preferred_element_type=F32)
    ).astype(BF16)
    for b in range(len(blocks)):
        for c in range(chunks):
            prep_ref[b * QBLK : (b + 1) * QBLK, c * LANES : (c + 1) * LANES] = done[
                c * QBLK : (c + 1) * QBLK, b * LANES : (b + 1) * LANES
            ]


def group_tile(blocks, train_ref, left_ref, right_ref, prep_ref):
    for pair in range(len(blocks) // 2):
        prepare(
            [blocks[2 * pair][...], blocks[2 * pair + 1][...]],
            left_ref,
            right_ref,
            prep_ref.at[pl.ds(pair * 2 * QBLK, 2 * QBLK)],
        )
    return lax.dot_general(
        prep_ref[...], train_ref[...], (((1,), (1,)), ((), ())), preferred_element_type=F32
    )


def tile_kernel(count, *refs):
    blocks, consts = refs[:count], refs[count : count + 3]
    early, (out_ref, prep_ref) = refs[count + 3 : -2], refs[-2:]
    start = 0
    for ref in early:
        start = ref.shape[0]
        out_ref[:start] = ref[...]
    out_ref[start:] = group_tile(blocks, *consts, prep_ref)


def last_kernel(count, order, layer, held, slots, pairs_ref, *refs):
    blocks, consts, early_ref = refs[:count], refs[count : count + 3], refs[count + 3]
    refs = refs[count + 4 :]
    outs, prep_ref, tile_ref = refs[:layer], refs[layer], refs[layer + 1]
    place = 0
    for tile in (early_ref[...], group_tile(blocks, *consts, prep_ref)):
        for i in range(tile.shape[0] // QBLK):
            tile_ref[place] = tile[i * QBLK : (i + 1) * QBLK]
            place += 1
    rows = QBLK // layer
    me = lax.axis_index("ex")
    chosen = []
    for slot in range(slots):
        q = pairs_ref[me * slots + slot]
        k = (jnp.maximum(q, 0) // held) ^ me
        place = jnp.int32(0)
        for index, offset in enumerate(order):
            place = jnp.where(k == offset, index, place)
        value = tile_ref[place]
        chosen.append(jnp.where(q >= 0, value, jnp.zeros_like(value)))
    for m in range(layer):
        part = jnp.concatenate([value[m * rows : (m + 1) * rows] for value in chosen], axis=0)
        outs[m][...] = part.astype(outs[m].dtype)


def finish_kernel(layer, *refs):
    parts, out_ref = refs[:layer], refs[layer]
    total = parts[0][...]
    for part in parts[1:]:
        total = total + part[...].astype(F32)
    rows = out_ref.shape[1]
    for slot in range(out_ref.shape[0]):
        out_ref[slot] = total[slot * rows : (slot + 1) * rows]


def shards(train_grads, query_grads, in_precond, out_precond, pair_blocks):
    ex = lax.axis_size("ex")
    layer = lax.axis_size("layer")
    train_rows, layers, features = train_grads.shape
    assert layers == 1
    held = query_grads.shape[0] // QBLK
    slots = pair_blocks.shape[0] // ex
    rows = QBLK // layer
    train = train_grads.reshape(train_rows, features)
    query = query_grads.reshape(query_grads.shape[0], features)
    in_factor = in_precond.reshape(in_precond.shape[1:])
    out_factor = out_precond.reshape(out_precond.shape[1:])
    limit = pltpu.CompilerParams(vmem_limit_bytes=24 * 2**20)

    picked = pl.pallas_call(
        functools.partial(pick_kernel, ex, held, slots),
        out_shape=[jax.ShapeDtypeStruct((QBLK, features), BF16)] * ex,
        in_specs=[SMEM, VMEM],
        out_specs=[VMEM] * ex,
        compiler_params=limit,
        name="pick",
    )(pair_blocks, query)

    far = lambda k: (-bin(k >> 1).count("1"), -(k & 1), -k)
    order = [0, 1] + sorted(range(2, ex), key=far)
    blocks = [picked[0]] + [
        lax.ppermute(picked[k], "ex", [(i, i ^ k) for i in range(ex)]) for k in order[1:]
    ]

    stack = features // LANES * QBLK
    span = 2 * LANES
    left, right = pl.pallas_call(
        functools.partial(factor_kernel, rows),
        out_shape=[
            jax.ShapeDtypeStruct((2, 2, stack, 2 * stack), BF16),
            jax.ShapeDtypeStruct((2, span, span), BF16),
        ],
        in_specs=[VMEM, VMEM],
        out_specs=[VMEM, VMEM],
        compiler_params=limit,
        name="factors",
    )(out_factor, in_factor)

    early = []
    for group in (blocks[:-4], blocks[-4:-2]):
        done = sum(tile.shape[0] for tile in early)
        early = [
            pl.pallas_call(
                functools.partial(tile_kernel, len(group)),
                out_shape=jax.ShapeDtypeStruct((done + len(group) * QBLK, train_rows), F32),
                in_specs=[VMEM] * (len(group) + 3 + len(early)),
                out_specs=VMEM,
                scratch_shapes=[pltpu.VMEM((len(group) * QBLK, features), BF16)],
                compiler_params=limit,
                name=f"tiles_{len(early)}",
            )(*group, train, left, right, *early)
        ]
    parts = pl.pallas_call(
        functools.partial(last_kernel, 2, order, layer, held, slots),
        out_shape=[jax.ShapeDtypeStruct((slots * rows, train_rows), F32)]
        + [jax.ShapeDtypeStruct((slots * rows, train_rows), BF16)] * (layer - 1),
        in_specs=[SMEM] + [VMEM] * (2 + 3 + len(early)),
        out_specs=[VMEM] * layer,
        scratch_shapes=[
            pltpu.VMEM((2 * QBLK, features), BF16),
            pltpu.VMEM((ex, QBLK, train_rows), F32),
        ],
        compiler_params=limit,
        name="last",
    )(pair_blocks, *blocks[-2:], train, left, right, *early)

    terms = [parts[0]] + [
        lax.ppermute(parts[m], "layer", [(i, i ^ m) for i in range(layer)]) for m in range(1, layer)
    ]
    out = pl.pallas_call(
        functools.partial(finish_kernel, layer),
        out_shape=jax.ShapeDtypeStruct((slots, rows, train_rows), F32),
        in_specs=[VMEM] * layer,
        out_specs=VMEM,
        name="finish",
    )(*terms)
    return jnp.transpose(out, (1, 0, 2))


def solution(mesh):
    in_specs = (
        P("ex", "layer", None),
        P("ex", "layer", None),
        P("layer", None, None),
        P("layer", None, None),
        P(),
    )
    out_specs = P("layer", "ex", None)
    return jax.shard_map(shards, mesh=mesh, in_specs=in_specs, out_specs=out_specs, check_vma=False)
```

```python
import functools

import jax
import jax.numpy as jnp
from jax import lax
from jax.experimental import pallas as pl
from jax.experimental.pallas import tpu as pltpu
from jax.sharding import PartitionSpec as P

QBLK = 16
LANES = 128
F32 = jnp.float32
BF16 = jnp.bfloat16

VMEM = pl.BlockSpec(memory_space=pltpu.VMEM)
SMEM = pl.BlockSpec(memory_space=pltpu.SMEM)


def split_bf16(x):
    high = x.astype(BF16)
    return high, (x - high.astype(F32)).astype(BF16)


def over_slots(slots, body, init):
    if slots > 8:
        return lax.fori_loop(0, slots, body, init)
    for slot in range(slots):
        init = body(slot, init)
    return init


def pick_kernel(ex, held, slots, pairs_ref, own_ref, other_ref, *outs):
    me = lax.axis_index("ex")
    for group in range(ex // 2):
        first = (me ^ (2 * group)) * slots
        for side, source in enumerate((own_ref, other_ref)):
            base = (me ^ side) * held

            def body(slot, block):
                local = pairs_ref[first + slot] - base
                return jnp.where((local >= 0) & (local < held), local, block)

            block = over_slots(slots, body, jnp.int32(0))
            start = pl.multiple_of(block * QBLK, QBLK)
            outs[group][side * QBLK : (side + 1) * QBLK, :] = source[pl.ds(start, QBLK), :]


def make_factors(rows, out_ref, in_ref, left_ref, right_ref):
    width = out_ref.shape[0]
    in_width = in_ref.shape[0]
    half = left_ref.shape[2]
    span = right_ref.shape[1]
    outs = split_bf16(out_ref[...])
    ins = split_bf16(in_ref[...])
    row = lax.broadcasted_iota(jnp.int32, (half, width), 0) // QBLK
    row_o = lax.broadcasted_iota(jnp.int32, (half, width), 1)
    col = lax.broadcasted_iota(jnp.int32, (width, half), 1) // QBLK
    col_o = lax.broadcasted_iota(jnp.int32, (width, half), 0)
    a = lax.broadcasted_iota(jnp.int32, (half, half), 0) % QBLK
    a = ((a // rows) ^ lax.axis_index("layer")) * rows + a % rows
    same = a == (lax.broadcasted_iota(jnp.int32, (half, half), 1) % QBLK)
    for h in range(2):
        for s in range(2):
            pick_rows = (row * 2 + s == row_o).astype(BF16)
            rows = jnp.dot(pick_rows, outs[h], preferred_element_type=F32).astype(BF16)
            for t in range(2):
                pick_cols = (col * 2 + (s ^ t) == col_o).astype(BF16)
                spread = jnp.dot(rows, pick_cols, preferred_element_type=F32)
                left_ref[h, s, :, t * half : (t + 1) * half] = jnp.where(same, spread, 0.0).astype(BF16)
        up = (
            lax.broadcasted_iota(jnp.int32, (span, in_width), 0) % in_width
            == lax.broadcasted_iota(jnp.int32, (span, in_width), 1)
        ).astype(BF16)
        down = (
            lax.broadcasted_iota(jnp.int32, (in_width, span), 1) % in_width
            == lax.broadcasted_iota(jnp.int32, (in_width, span), 0)
        ).astype(BF16)
        wide = jnp.dot(
            jnp.dot(up, ins[h], preferred_element_type=F32).astype(BF16), down, preferred_element_type=F32
        )
        block = (lax.broadcasted_iota(jnp.int32, (span, span), 0) // in_width) == (
            lax.broadcasted_iota(jnp.int32, (span, span), 1) // in_width
        )
        right_ref[h] = jnp.where(block, wide, 0.0).astype(BF16)


def prepare(pair_ref, left_ref, right_ref, prep_ref):
    chunks = pair_ref.shape[1] // LANES
    half = LANES // 2
    stacked = []
    for side in range(2):
        block = pair_ref[side * QBLK : (side + 1) * QBLK, :]
        tall = jnp.concatenate([block[:, c * LANES : (c + 1) * LANES] for c in range(chunks)], axis=0)
        turned = jnp.concatenate([tall[:, half:], tall[:, :half]], axis=1)
        stacked.append(jnp.concatenate([tall, turned], axis=0))
    stacked = jnp.concatenate(stacked, axis=1)
    parts = [
        jnp.dot(left_ref[0, s], stacked, preferred_element_type=F32)
        + jnp.dot(left_ref[1, s], stacked, preferred_element_type=F32)
        for s in range(2)
    ]
    lane = lax.broadcasted_iota(jnp.int32, parts[0].shape, 1) % LANES
    high, low = split_bf16(jnp.where(lane < half, parts[0], parts[1]))
    done = (
        jnp.dot(high, right_ref[0], preferred_element_type=F32)
        + jnp.dot(low, right_ref[0], preferred_element_type=F32)
        + jnp.dot(high, right_ref[1], preferred_element_type=F32)
    ).astype(BF16)
    for side in range(2):
        for c in range(chunks):
            prep_ref[side, :, c * LANES : (c + 1) * LANES] = done[
                c * QBLK : (c + 1) * QBLK, side * LANES : (side + 1) * LANES
            ]


def first_kernel(rows, out_ref, in_ref, pair_ref, left_ref, right_ref, prep_ref):
    make_factors(rows, out_ref, in_ref, left_ref, right_ref)
    prepare(pair_ref, left_ref, right_ref, prep_ref)


def middle_kernel(*refs):
    early_ref, left_ref, right_ref = refs[:3]
    pairs, prep_ref = refs[3:-1], refs[-1]
    prep_ref[:2] = early_ref[...]
    for index, pair_ref in enumerate(pairs):
        prepare(pair_ref, left_ref, right_ref, prep_ref.at[pl.ds(2 + 2 * index, 2)])


def last_kernel(order, layer, held, slots, pairs_ref, pair_ref, early_ref, train_ref, left_ref, right_ref, *refs):
    outs, late_ref, rows_ref = refs[:layer], refs[layer], refs[layer + 1]
    ready = early_ref.shape[0]
    prepare(pair_ref, left_ref, right_ref, late_ref)
    me = lax.axis_index("ex")
    wanted = [pairs_ref[me * slots + slot] for slot in range(slots)]
    for slot, q in enumerate(wanted):
        k = (jnp.maximum(q, 0) // held) ^ me
        place = jnp.int32(0)
        for index, group in enumerate(order):
            place = jnp.where(k // 2 == group, 2 * index + k % 2, place)

        @pl.when(place < ready)
        def _():
            rows_ref[slot * QBLK : (slot + 1) * QBLK, :] = early_ref[jnp.minimum(place, ready - 1)]

        @pl.when(place >= ready)
        def _():
            rows_ref[slot * QBLK : (slot + 1) * QBLK, :] = late_ref[jnp.maximum(place - ready, 0)]

    tile = lax.dot_general(
        rows_ref[...], train_ref[...], (((1,), (1,)), ((), ())), preferred_element_type=F32
    )
    rows = QBLK // layer
    chosen = []
    for slot, q in enumerate(wanted):
        value = tile[slot * QBLK : (slot + 1) * QBLK]
        chosen.append(jnp.where(q >= 0, value, jnp.zeros_like(value)))
    for m in range(layer):
        part = jnp.concatenate([value[m * rows : (m + 1) * rows] for value in chosen], axis=0)
        outs[m][...] = part.astype(outs[m].dtype)


def finish_kernel(layer, *refs):
    parts, out_ref = refs[:layer], refs[layer]
    total = parts[0][...]
    for part in parts[1:]:
        total = total + part[...].astype(F32)
    rows = out_ref.shape[1]
    for slot in range(out_ref.shape[0]):
        out_ref[slot] = total[slot * rows : (slot + 1) * rows]


def shards(train_grads, query_grads, in_precond, out_precond, pair_blocks):
    ex = lax.axis_size("ex")
    layer = lax.axis_size("layer")
    train_rows, layers, features = train_grads.shape
    assert layers == 1
    held = query_grads.shape[0] // QBLK
    slots = pair_blocks.shape[0] // ex
    rows = QBLK // layer
    train = train_grads.reshape(train_rows, features)
    query = query_grads.reshape(query_grads.shape[0], features)
    in_factor = in_precond.reshape(in_precond.shape[1:])
    out_factor = out_precond.reshape(out_precond.shape[1:])
    limit = pltpu.CompilerParams(vmem_limit_bytes=24 * 2**20)

    def from_index(array, k):
        return lax.ppermute(array, "ex", [(i, i ^ k) for i in range(ex)])

    picked = pl.pallas_call(
        functools.partial(pick_kernel, ex, held, slots),
        out_shape=[jax.ShapeDtypeStruct((2 * QBLK, features), BF16)] * (ex // 2),
        in_specs=[SMEM, VMEM, VMEM],
        out_specs=[VMEM] * (ex // 2),
        compiler_params=limit,
        name="pick",
    )(pair_blocks, query, from_index(query, 1))

    order = sorted(range(ex // 2), key=lambda group: (bin(group).count("1"), group))
    blocks = [picked[0]] + [from_index(picked[group], 2 * group) for group in order[1:]]

    stack = features // LANES * QBLK
    span = 2 * LANES
    left, right, early = pl.pallas_call(
        functools.partial(first_kernel, rows),
        out_shape=[
            jax.ShapeDtypeStruct((2, 2, stack, 2 * stack), BF16),
            jax.ShapeDtypeStruct((2, span, span), BF16),
            jax.ShapeDtypeStruct((2, QBLK, features), BF16),
        ],
        in_specs=[VMEM] * 3,
        out_specs=[VMEM] * 3,
        compiler_params=limit,
        name="first",
    )(out_factor, in_factor, blocks[0])
    early = pl.pallas_call(
        middle_kernel,
        out_shape=jax.ShapeDtypeStruct((ex - 2, QBLK, features), BF16),
        in_specs=[VMEM] * (3 + len(order) - 2),
        out_specs=VMEM,
        compiler_params=limit,
        name="middle",
    )(early, left, right, *blocks[1:-1])
    parts = pl.pallas_call(
        functools.partial(last_kernel, order, layer, held, slots),
        out_shape=[jax.ShapeDtypeStruct((slots * rows, train_rows), F32)]
        + [jax.ShapeDtypeStruct((slots * rows, train_rows), BF16)] * (layer - 1),
        in_specs=[SMEM] + [VMEM] * 5,
        out_specs=[VMEM] * layer,
        scratch_shapes=[
            pltpu.VMEM((2, QBLK, features), BF16),
            pltpu.VMEM((slots * QBLK, features), BF16),
        ],
        compiler_params=limit,
        name="last",
    )(pair_blocks, blocks[-1], early, train, left, right)

    terms = [parts[0]] + [
        lax.ppermute(parts[m], "layer", [(i, i ^ m) for i in range(layer)]) for m in range(1, layer)
    ]
    out = pl.pallas_call(
        functools.partial(finish_kernel, layer),
        out_shape=jax.ShapeDtypeStruct((slots, rows, train_rows), F32),
        in_specs=[VMEM] * layer,
        out_specs=VMEM,
        compiler_params=limit,
        name="finish",
    )(*terms)
    return jnp.transpose(out, (1, 0, 2))


def solution(mesh):
    in_specs = (
        P("ex", "layer", None),
        P("ex", "layer", None),
        P("layer", None, None),
        P("layer", None, None),
        P(),
    )
    out_specs = P("layer", "ex", None)
    return jax.shard_map(shards, mesh=mesh, in_specs=in_specs, out_specs=out_specs, check_vma=False)
```

```python
import functools

import jax
import jax.numpy as jnp
from jax import lax
from jax.experimental import pallas as pl
from jax.experimental.pallas import tpu as pltpu
from jax.sharding import PartitionSpec as P

QBLK = 16
LANES = 128
F32 = jnp.float32
BF16 = jnp.bfloat16

VMEM = pl.BlockSpec(memory_space=pltpu.VMEM)
SMEM = pl.BlockSpec(memory_space=pltpu.SMEM)


def split_bf16(x):
    high = x.astype(BF16)
    return high, (x - high.astype(F32)).astype(BF16)


def over_slots(slots, body, init):
    if slots > 8:
        return lax.fori_loop(0, slots, body, init)
    for slot in range(slots):
        init = body(slot, init)
    return init


def wanted_block(ex, held, slots, pairs_ref, group, side):
    me = lax.axis_index("ex")
    first = (me ^ (2 * group)) * slots
    base = (me ^ side) * held

    def body(slot, block):
        local = pairs_ref[first + slot] - base
        return jnp.where((local >= 0) & (local < held), local, block)

    return pl.multiple_of(over_slots(slots, body, jnp.int32(0)) * QBLK, QBLK)


def own_kernel(find, pairs_ref, query_ref, *outs):
    for group, out_ref in enumerate(outs):
        out_ref[...] = query_ref[pl.ds(find(pairs_ref, group, 0), QBLK), :]


def pick_kernel(find, groups, pairs_ref, other_ref, *refs):
    for group in range(groups):
        out_ref = refs[groups + group]
        out_ref[:QBLK] = refs[group][...]
        out_ref[QBLK:] = other_ref[pl.ds(find(pairs_ref, group, 1), QBLK), :]


def make_factors(rows, out_ref, in_ref, left_ref, right_ref):
    width = out_ref.shape[0]
    in_width = in_ref.shape[0]
    half = left_ref.shape[2]
    span = right_ref.shape[1]
    outs = split_bf16(out_ref[...])
    ins = split_bf16(in_ref[...])
    row = lax.broadcasted_iota(jnp.int32, (half, width), 0) // QBLK
    row_o = lax.broadcasted_iota(jnp.int32, (half, width), 1)
    col = lax.broadcasted_iota(jnp.int32, (width, half), 1) // QBLK
    col_o = lax.broadcasted_iota(jnp.int32, (width, half), 0)
    a = lax.broadcasted_iota(jnp.int32, (half, half), 0) ^ lax.broadcasted_iota(jnp.int32, (half, half), 1)
    same = (a & (QBLK - 1)) == lax.axis_index("layer") * rows
    for h in range(2):
        for s in range(2):
            pick_rows = (row * 2 + s == row_o).astype(BF16)
            rows = jnp.dot(pick_rows, outs[h], preferred_element_type=F32).astype(BF16)
            for t in range(2):
                pick_cols = (col * 2 + (s ^ t) == col_o).astype(BF16)
                spread = jnp.dot(rows, pick_cols, preferred_element_type=F32)
                left_ref[h, s, :, t * half : (t + 1) * half] = jnp.where(same, spread, 0.0).astype(BF16)
        up = (
            lax.broadcasted_iota(jnp.int32, (span, in_width), 0) % in_width
            == lax.broadcasted_iota(jnp.int32, (span, in_width), 1)
        ).astype(BF16)
        down = (
            lax.broadcasted_iota(jnp.int32, (in_width, span), 1) % in_width
            == lax.broadcasted_iota(jnp.int32, (in_width, span), 0)
        ).astype(BF16)
        wide = jnp.dot(
            jnp.dot(up, ins[h], preferred_element_type=F32).astype(BF16), down, preferred_element_type=F32
        )
        block = (lax.broadcasted_iota(jnp.int32, (span, span), 0) // in_width) == (
            lax.broadcasted_iota(jnp.int32, (span, span), 1) // in_width
        )
        right_ref[h] = jnp.where(block, wide, 0.0).astype(BF16)


def prepare(pair_ref, left_ref, right_ref, prep_ref):
    chunks = pair_ref.shape[1] // LANES
    half = LANES // 2
    stacked = []
    for side in range(2):
        block = pair_ref[side * QBLK : (side + 1) * QBLK, :]
        tall = jnp.concatenate([block[:, c * LANES : (c + 1) * LANES] for c in range(chunks)], axis=0)
        turned = jnp.concatenate([tall[:, half:], tall[:, :half]], axis=1)
        stacked.append(jnp.concatenate([tall, turned], axis=0))
    stacked = jnp.concatenate(stacked, axis=1)
    parts = [
        jnp.dot(left_ref[0, s], stacked, preferred_element_type=F32)
        + jnp.dot(left_ref[1, s], stacked, preferred_element_type=F32)
        for s in range(2)
    ]
    lane = lax.broadcasted_iota(jnp.int32, parts[0].shape, 1) % LANES
    high, low = split_bf16(jnp.where(lane < half, parts[0], parts[1]))
    done = (
        jnp.dot(high, right_ref[0], preferred_element_type=F32)
        + jnp.dot(low, right_ref[0], preferred_element_type=F32)
        + jnp.dot(high, right_ref[1], preferred_element_type=F32)
    ).astype(BF16)
    for side in range(2):
        for c in range(chunks):
            prep_ref[side, :, c * LANES : (c + 1) * LANES] = done[
                c * QBLK : (c + 1) * QBLK, side * LANES : (side + 1) * LANES
            ]


def first_kernel(rows, out_ref, in_ref, pair_ref, left_ref, right_ref, prep_ref):
    make_factors(rows, out_ref, in_ref, left_ref, right_ref)
    prepare(pair_ref, left_ref, right_ref, prep_ref)


def near_kernel(done, left_ref, right_ref, *refs):
    prep_ref = refs[-1]
    if done:
        prep_ref[:done] = refs[0][...]
    for index, pair_ref in enumerate(refs[min(done, 1) : -1]):
        prepare(pair_ref, left_ref, right_ref, prep_ref.at[pl.ds(done + 2 * index, 2)])


def last_kernel(order, layer, held, slots, pairs_ref, late_ref, early_ref, train_ref, *refs):
    outs, rows_ref = refs[:layer], refs[layer]
    ready = early_ref.shape[0]
    me = lax.axis_index("ex")
    wanted = [pairs_ref[me * slots + slot] for slot in range(slots)]
    for slot, q in enumerate(wanted):
        k = (jnp.maximum(q, 0) // held) ^ me
        place = jnp.int32(0)
        for index, group in enumerate(order):
            place = jnp.where(k // 2 == group, 2 * index + k % 2, place)

        @pl.when(place < ready)
        def _():
            rows_ref[slot * QBLK : (slot + 1) * QBLK, :] = early_ref[jnp.minimum(place, ready - 1)]

        @pl.when(place >= ready)
        def _():
            rows_ref[slot * QBLK : (slot + 1) * QBLK, :] = late_ref[jnp.maximum(place - ready, 0)]

    tile = lax.dot_general(
        rows_ref[...], train_ref[...], (((1,), (1,)), ((), ())), preferred_element_type=F32
    )
    rows = QBLK // layer
    chosen = []
    for slot, q in enumerate(wanted):
        value = tile[slot * QBLK : (slot + 1) * QBLK]
        chosen.append(jnp.where(q >= 0, value, jnp.zeros_like(value)))
    for m in range(layer):
        part = jnp.concatenate([value[m * rows : (m + 1) * rows] for value in chosen], axis=0)
        outs[m][...] = part.astype(outs[m].dtype)


def finish_kernel(layer, *refs):
    parts, out_ref = refs[:layer], refs[layer]
    total = parts[0][...]
    for part in parts[1:]:
        total = total + part[...].astype(F32)
    rows = out_ref.shape[1]
    for slot in range(out_ref.shape[0]):
        out_ref[slot] = total[slot * rows : (slot + 1) * rows]


def shards(train_grads, query_grads, in_precond, out_precond, pair_blocks):
    ex = lax.axis_size("ex")
    layer = lax.axis_size("layer")
    train_rows, layers, features = train_grads.shape
    assert layers == 1
    held = query_grads.shape[0] // QBLK
    slots = pair_blocks.shape[0] // ex
    rows = QBLK // layer
    train = train_grads.reshape(train_rows, features)
    query = query_grads.reshape(query_grads.shape[0], features)
    in_factor = in_precond.reshape(in_precond.shape[1:])
    out_factor = out_precond.reshape(out_precond.shape[1:])
    limit = pltpu.CompilerParams(vmem_limit_bytes=24 * 2**20)

    def from_index(array, k):
        return lax.ppermute(array, "ex", [(i, i ^ k) for i in range(ex)])

    groups = ex // 2
    find = functools.partial(wanted_block, ex, held, slots)
    other = from_index(query, 1)
    own = pl.pallas_call(
        functools.partial(own_kernel, find),
        out_shape=[jax.ShapeDtypeStruct((QBLK, features), BF16)] * groups,
        in_specs=[SMEM, VMEM],
        out_specs=[VMEM] * groups,
        compiler_params=limit,
        name="own",
    )(pair_blocks, query)
    picked = pl.pallas_call(
        functools.partial(pick_kernel, find, groups),
        out_shape=[jax.ShapeDtypeStruct((2 * QBLK, features), BF16)] * groups,
        in_specs=[SMEM] + [VMEM] * (1 + groups),
        out_specs=[VMEM] * groups,
        compiler_params=limit,
        name="pick",
    )(pair_blocks, other, *own)

    order = sorted(range(groups), key=lambda group: (bin(group).count("1"), group))
    raw = [from_index(picked[group], 2 * group) for group in order[1:-1]]

    stack = features // LANES * QBLK
    span = 2 * LANES
    left, right, far = pl.pallas_call(
        functools.partial(first_kernel, rows),
        out_shape=[
            jax.ShapeDtypeStruct((2, 2, stack, 2 * stack), BF16),
            jax.ShapeDtypeStruct((2, span, span), BF16),
            jax.ShapeDtypeStruct((2, QBLK, features), BF16),
        ],
        in_specs=[VMEM] * 3,
        out_specs=[VMEM] * 3,
        compiler_params=limit,
        name="first",
    )(out_factor, in_factor, picked[order[-1]])
    far = from_index(far, 2 * order[-1])

    early, done = [], 0
    half = len(raw) // 2
    for index, pairs in enumerate(([picked[0]], raw[:half], raw[half:])):
        early = [
            pl.pallas_call(
                functools.partial(near_kernel, done),
                out_shape=jax.ShapeDtypeStruct((done + 2 * len(pairs), QBLK, features), BF16),
                in_specs=[VMEM] * (2 + len(early) + len(pairs)),
                out_specs=VMEM,
                compiler_params=limit,
                name=f"near{index}",
            )(left, right, *early, *pairs)
        ]
        done += 2 * len(pairs)
    parts = pl.pallas_call(
        functools.partial(last_kernel, order, layer, held, slots),
        out_shape=[jax.ShapeDtypeStruct((slots * rows, train_rows), F32)]
        + [jax.ShapeDtypeStruct((slots * rows, train_rows), BF16)] * (layer - 1),
        in_specs=[SMEM] + [VMEM] * 3,
        out_specs=[VMEM] * layer,
        scratch_shapes=[pltpu.VMEM((slots * QBLK, features), BF16)],
        compiler_params=limit,
        name="last",
    )(pair_blocks, far, *early, train)

    terms = [parts[0]] + [
        lax.ppermute(parts[m], "layer", [(i, i ^ m) for i in range(layer)]) for m in range(1, layer)
    ]
    out = pl.pallas_call(
        functools.partial(finish_kernel, layer),
        out_shape=jax.ShapeDtypeStruct((slots, rows, train_rows), F32),
        in_specs=[VMEM] * layer,
        out_specs=VMEM,
        compiler_params=limit,
        name="finish",
    )(*terms)
    return jnp.transpose(out, (1, 0, 2))


def solution(mesh):
    in_specs = (
        P("ex", "layer", None),
        P("ex", "layer", None),
        P("layer", None, None),
        P("layer", None, None),
        P(),
    )
    out_specs = P("layer", "ex", None)
    return jax.shard_map(shards, mesh=mesh, in_specs=in_specs, out_specs=out_specs, check_vma=False)
```

```python
import functools

import jax
import jax.numpy as jnp
from jax import lax
from jax.experimental import pallas as pl
from jax.experimental.pallas import tpu as pltpu
from jax.sharding import PartitionSpec as P

QBLK = 16
LANES = 128
F32 = jnp.float32
BF16 = jnp.bfloat16

VMEM = pl.BlockSpec(memory_space=pltpu.VMEM)
SMEM = pl.BlockSpec(memory_space=pltpu.SMEM)


def split_bf16(x):
    high = x.astype(BF16)
    return high, (x - high.astype(F32)).astype(BF16)


def over_slots(slots, body, init):
    if slots > 8:
        return lax.fori_loop(0, slots, body, init)
    for slot in range(slots):
        init = body(slot, init)
    return init


def wanted_block(ex, held, slots, pairs_ref, group, side):
    me = lax.axis_index("ex")
    first = (me ^ (2 * group)) * slots
    base = (me ^ side) * held

    def body(slot, block):
        local = pairs_ref[first + slot] - base
        return jnp.where((local >= 0) & (local < held), local, block)

    return pl.multiple_of(over_slots(slots, body, jnp.int32(0)) * QBLK, QBLK)


def own_kernel(find, pairs_ref, query_ref, *outs):
    for group, out_ref in enumerate(outs):
        out_ref[...] = query_ref[pl.ds(find(pairs_ref, group, 0), QBLK), :]


def pick_kernel(find, groups, pairs_ref, other_ref, *refs):
    for group in range(groups):
        out_ref = refs[groups + group]
        out_ref[:QBLK] = refs[group][...]
        out_ref[QBLK:] = other_ref[pl.ds(find(pairs_ref, group, 1), QBLK), :]


def make_factors(rows, width, factors_ref, left_ref, right_ref):
    in_width = factors_ref.shape[0] - width
    half = left_ref.shape[2]
    span = right_ref.shape[1]
    outs = split_bf16(factors_ref[:width])
    ins = split_bf16(factors_ref[width:])
    row = lax.broadcasted_iota(jnp.int32, (half, width), 0) // QBLK
    row_o = lax.broadcasted_iota(jnp.int32, (half, width), 1)
    col = lax.broadcasted_iota(jnp.int32, (width, half), 1) // QBLK
    col_o = lax.broadcasted_iota(jnp.int32, (width, half), 0)
    a = lax.broadcasted_iota(jnp.int32, (half, half), 0) ^ lax.broadcasted_iota(jnp.int32, (half, half), 1)
    same = (a & (QBLK - 1)) == lax.axis_index("layer") * rows
    zero = jnp.zeros((), BF16)
    for h in range(2):
        for s in range(2):
            pick_rows = (row * 2 + s == row_o).astype(BF16)
            rows = jnp.dot(pick_rows, outs[h], preferred_element_type=F32).astype(BF16)
            for t in range(2):
                pick_cols = (col * 2 + (s ^ t) == col_o).astype(BF16)
                spread = jnp.dot(rows, pick_cols, preferred_element_type=F32)
                left_ref[h, s, :, t * half : (t + 1) * half] = jnp.where(same, spread.astype(BF16), zero)
        up = (
            lax.broadcasted_iota(jnp.int32, (span, in_width), 0) % in_width
            == lax.broadcasted_iota(jnp.int32, (span, in_width), 1)
        ).astype(BF16)
        down = (
            lax.broadcasted_iota(jnp.int32, (in_width, span), 1) % in_width
            == lax.broadcasted_iota(jnp.int32, (in_width, span), 0)
        ).astype(BF16)
        wide = jnp.dot(
            jnp.dot(up, ins[h], preferred_element_type=F32).astype(BF16), down, preferred_element_type=F32
        )
        block = (lax.broadcasted_iota(jnp.int32, (span, span), 0) // in_width) == (
            lax.broadcasted_iota(jnp.int32, (span, span), 1) // in_width
        )
        right_ref[h] = jnp.where(block, wide, 0.0).astype(BF16)


def prepare(pair_ref, left_ref, right_ref, prep_ref):
    chunks = pair_ref.shape[1] // LANES
    half = LANES // 2
    stacked = []
    for side in range(2):
        block = pair_ref[side * QBLK : (side + 1) * QBLK, :]
        tall = jnp.concatenate([block[:, c * LANES : (c + 1) * LANES] for c in range(chunks)], axis=0)
        turned = jnp.concatenate([tall[:, half:], tall[:, :half]], axis=1)
        stacked.append(jnp.concatenate([tall, turned], axis=0))
    stacked = jnp.concatenate(stacked, axis=1)
    parts = [
        jnp.dot(left_ref[0, s], stacked, preferred_element_type=F32)
        + jnp.dot(left_ref[1, s], stacked, preferred_element_type=F32)
        for s in range(2)
    ]
    lane = lax.broadcasted_iota(jnp.int32, parts[0].shape, 1) % LANES
    high, low = split_bf16(jnp.where(lane < half, parts[0], parts[1]))
    done = (
        jnp.dot(high, right_ref[0], preferred_element_type=F32)
        + jnp.dot(low, right_ref[0], preferred_element_type=F32)
        + jnp.dot(high, right_ref[1], preferred_element_type=F32)
    ).astype(BF16)
    for side in range(2):
        for c in range(chunks):
            prep_ref[side, :, c * LANES : (c + 1) * LANES] = done[
                c * QBLK : (c + 1) * QBLK, side * LANES : (side + 1) * LANES
            ]


def first_kernel(rows, width, factors_ref, pair_ref, left_ref, right_ref, prep_ref):
    make_factors(rows, width, factors_ref, left_ref, right_ref)
    prepare(pair_ref, left_ref, right_ref, prep_ref)


def near_kernel(done, left_ref, right_ref, *refs):
    prep_ref = refs[-1]
    if done:
        prep_ref[:done] = refs[0][...]
    for index, pair_ref in enumerate(refs[min(done, 1) : -1]):
        prepare(pair_ref, left_ref, right_ref, prep_ref.at[pl.ds(done + 2 * index, 2)])


def last_kernel(order, layer, held, slots, pairs_ref, late_ref, early_ref, train_ref, *refs):
    mine_ref, send_ref, rows_ref = refs
    ready = early_ref.shape[0]
    me = lax.axis_index("ex")
    wanted = [pairs_ref[me * slots + slot] for slot in range(slots)]
    for slot, q in enumerate(wanted):
        k = (jnp.maximum(q, 0) // held) ^ me
        place = jnp.int32(0)
        for index, group in enumerate(order):
            place = jnp.where(k // 2 == group, 2 * index + k % 2, place)

        @pl.when(place < ready)
        def _():
            rows_ref[slot * QBLK : (slot + 1) * QBLK, :] = early_ref[jnp.minimum(place, ready - 1)]

        @pl.when(place >= ready)
        def _():
            rows_ref[slot * QBLK : (slot + 1) * QBLK, :] = late_ref[jnp.maximum(place - ready, 0)]

    tile = lax.dot_general(
        rows_ref[...], train_ref[...], (((1,), (1,)), ((), ())), preferred_element_type=F32
    )
    rows = QBLK // layer
    chosen = []
    for slot, q in enumerate(wanted):
        value = tile[slot * QBLK : (slot + 1) * QBLK]
        chosen.append(jnp.where(q >= 0, value, jnp.zeros_like(value)))
    for m in range(layer):
        part = jnp.concatenate([value[m * rows : (m + 1) * rows] for value in chosen], axis=0)
        if m == 0:
            mine_ref[...] = part
        send_ref[lax.axis_index("layer") ^ m] = part.astype(BF16)


def finish_kernel(layer, mine_ref, parts_ref, out_ref):
    total = mine_ref[...]
    for m in range(1, layer):
        total = total + parts_ref[lax.axis_index("layer") ^ m].astype(F32)
    rows = out_ref.shape[1]
    for slot in range(out_ref.shape[0]):
        out_ref[slot] = total[slot * rows : (slot + 1) * rows]


def shards(train_grads, query_grads, in_precond, out_precond, pair_blocks):
    ex = lax.axis_size("ex")
    layer = lax.axis_size("layer")
    train_rows, layers, features = train_grads.shape
    assert layers == 1
    held = query_grads.shape[0] // QBLK
    slots = pair_blocks.shape[0] // ex
    rows = QBLK // layer
    train = train_grads.reshape(train_rows, features)
    query = query_grads.reshape(query_grads.shape[0], features)
    in_factor = in_precond.reshape(in_precond.shape[1:])
    out_factor = out_precond.reshape(out_precond.shape[1:])
    limit = pltpu.CompilerParams(vmem_limit_bytes=24 * 2**20)

    def from_index(array, k):
        return lax.ppermute(array, "ex", [(i, i ^ k) for i in range(ex)])

    groups = ex // 2
    find = functools.partial(wanted_block, ex, held, slots)
    other = from_index(query, 1)
    own = pl.pallas_call(
        functools.partial(own_kernel, find),
        out_shape=[jax.ShapeDtypeStruct((QBLK, features), BF16)] * groups,
        in_specs=[SMEM, VMEM],
        out_specs=[VMEM] * groups,
        compiler_params=limit,
        name="own",
    )(pair_blocks, query)
    picked = pl.pallas_call(
        functools.partial(pick_kernel, find, groups),
        out_shape=[jax.ShapeDtypeStruct((2 * QBLK, features), BF16)] * groups,
        in_specs=[SMEM] + [VMEM] * (1 + groups),
        out_specs=[VMEM] * groups,
        compiler_params=limit,
        name="pick",
    )(pair_blocks, other, *own)

    order = sorted(range(groups), key=lambda group: (bin(group).count("1"), group))
    raw = [from_index(picked[group], 2 * group) for group in order[1:-1]]

    stack = features // LANES * QBLK
    span = 2 * LANES
    out_factor, in_factor, far_pick = lax.optimization_barrier((out_factor, in_factor, picked[order[-1]]))
    left, right, far = pl.pallas_call(
        functools.partial(first_kernel, rows, out_factor.shape[0]),
        out_shape=[
            jax.ShapeDtypeStruct((2, 2, stack, 2 * stack), BF16),
            jax.ShapeDtypeStruct((2, span, span), BF16),
            jax.ShapeDtypeStruct((2, QBLK, features), BF16),
        ],
        in_specs=[VMEM] * 2,
        out_specs=[VMEM] * 3,
        compiler_params=limit,
        name="first",
    )(jnp.concatenate([out_factor, in_factor], axis=0), far_pick)
    far = from_index(far, 2 * order[-1])

    early, done = [], 0
    half = len(raw) // 2
    for index, pairs in enumerate(([picked[0]], raw[:half], raw[half:])):
        early = [
            pl.pallas_call(
                functools.partial(near_kernel, done),
                out_shape=jax.ShapeDtypeStruct((done + 2 * len(pairs), QBLK, features), BF16),
                in_specs=[VMEM] * (2 + len(early) + len(pairs)),
                out_specs=VMEM,
                compiler_params=limit,
                name=f"near{index}",
            )(left, right, *early, *pairs)
        ]
        done += 2 * len(pairs)
    mine, parts = pl.pallas_call(
        functools.partial(last_kernel, order, layer, held, slots),
        out_shape=[
            jax.ShapeDtypeStruct((slots * rows, train_rows), F32),
            jax.ShapeDtypeStruct((layer, slots * rows, train_rows), BF16),
        ],
        in_specs=[SMEM] + [VMEM] * 3,
        out_specs=[VMEM] * 2,
        scratch_shapes=[pltpu.VMEM((slots * QBLK, features), BF16)],
        compiler_params=limit,
        name="last",
    )(pair_blocks, far, *early, train)

    parts = lax.all_to_all(parts, "layer", split_axis=0, concat_axis=0, tiled=True)
    out = pl.pallas_call(
        functools.partial(finish_kernel, layer),
        out_shape=jax.ShapeDtypeStruct((slots, rows, train_rows), F32),
        in_specs=[VMEM] * 2,
        out_specs=VMEM,
        compiler_params=limit,
        name="finish",
    )(mine, parts)
    return jnp.transpose(out, (1, 0, 2))


def solution(mesh):
    in_specs = (
        P("ex", "layer", None),
        P("ex", "layer", None),
        P("layer", None, None),
        P("layer", None, None),
        P(),
    )
    out_specs = P("layer", "ex", None)
    return jax.shard_map(shards, mesh=mesh, in_specs=in_specs, out_specs=out_specs, check_vma=False)
```

```python
import functools

import jax
import jax.numpy as jnp
from jax import lax
from jax.experimental import pallas as pl
from jax.experimental.pallas import tpu as pltpu
from jax.sharding import PartitionSpec as P

QBLK = 16
LANES = 128
F32 = jnp.float32
BF16 = jnp.bfloat16

VMEM = pl.BlockSpec(memory_space=pltpu.VMEM)
SMEM = pl.BlockSpec(memory_space=pltpu.SMEM)


def split_bf16(x):
    high = x.astype(BF16)
    return high, (x - high.astype(F32)).astype(BF16)


def over_slots(slots, body, init):
    if slots > 8:
        return lax.fori_loop(0, slots, body, init)
    for slot in range(slots):
        init = body(slot, init)
    return init


def ring_chip(place):
    return place ^ (place >> 1)


def ring_place(chip, chips):
    place, shift = chip, 1
    while shift < chips:
        place, shift = place ^ (place >> shift), 2 * shift
    return place


def wanted_block(ex, held, slots, pairs_ref, step, side):
    me = lax.axis_index("ex")
    chips = ex // 2
    target = ring_chip((ring_place(me >> 1, chips) + step) & (chips - 1))
    first = (2 * target + (me & 1)) * slots
    base = (me ^ side) * held

    def body(slot, block):
        local = pairs_ref[first + slot] - base
        return jnp.where((local >= 0) & (local < held), local, block)

    return pl.multiple_of(over_slots(slots, body, jnp.int32(0)) * QBLK, QBLK)


def own_kernel(find, pairs_ref, query_ref, *outs):
    for group, out_ref in enumerate(outs):
        out_ref[...] = query_ref[pl.ds(find(pairs_ref, group, 0), QBLK), :]


def pick_kernel(find, groups, pairs_ref, other_ref, *refs):
    for group in range(groups):
        out_ref = refs[groups + group]
        out_ref[:QBLK] = refs[group][...]
        out_ref[QBLK:] = other_ref[pl.ds(find(pairs_ref, group, 1), QBLK), :]


def make_factors(rows, width, factors_ref, left_ref, right_ref):
    in_width = factors_ref.shape[0] - width
    half = left_ref.shape[2]
    span = right_ref.shape[1]
    outs = split_bf16(factors_ref[:width])
    ins = split_bf16(factors_ref[width:])
    row = lax.broadcasted_iota(jnp.int32, (half, width), 0) // QBLK
    row_o = lax.broadcasted_iota(jnp.int32, (half, width), 1)
    col = lax.broadcasted_iota(jnp.int32, (width, half), 1) // QBLK
    col_o = lax.broadcasted_iota(jnp.int32, (width, half), 0)
    a = lax.broadcasted_iota(jnp.int32, (half, half), 1) - lax.broadcasted_iota(jnp.int32, (half, half), 0)
    same = (a & (QBLK - 1)) == lax.axis_index("layer") * rows
    zero = jnp.zeros((), BF16)
    for h in range(2):
        for s in range(2):
            pick_rows = (row * 2 + s == row_o).astype(BF16)
            rows = jnp.dot(pick_rows, outs[h], preferred_element_type=F32).astype(BF16)
            for t in range(2):
                pick_cols = (col * 2 + (s ^ t) == col_o).astype(BF16)
                spread = jnp.dot(rows, pick_cols, preferred_element_type=F32)
                left_ref[h, s, :, t * half : (t + 1) * half] = jnp.where(same, spread.astype(BF16), zero)
        up = (
            lax.broadcasted_iota(jnp.int32, (span, in_width), 0) % in_width
            == lax.broadcasted_iota(jnp.int32, (span, in_width), 1)
        ).astype(BF16)
        down = (
            lax.broadcasted_iota(jnp.int32, (in_width, span), 1) % in_width
            == lax.broadcasted_iota(jnp.int32, (in_width, span), 0)
        ).astype(BF16)
        wide = jnp.dot(
            jnp.dot(up, ins[h], preferred_element_type=F32).astype(BF16), down, preferred_element_type=F32
        )
        block = (lax.broadcasted_iota(jnp.int32, (span, span), 0) // in_width) == (
            lax.broadcasted_iota(jnp.int32, (span, span), 1) // in_width
        )
        right_ref[h] = jnp.where(block, wide, 0.0).astype(BF16)


def prepare(pair_ref, left_ref, right_ref, prep_ref):
    chunks = pair_ref.shape[1] // LANES
    half = LANES // 2
    stacked = []
    for side in range(2):
        block = pair_ref[side * QBLK : (side + 1) * QBLK, :]
        tall = jnp.concatenate([block[:, c * LANES : (c + 1) * LANES] for c in range(chunks)], axis=0)
        turned = jnp.concatenate([tall[:, half:], tall[:, :half]], axis=1)
        stacked.append(jnp.concatenate([tall, turned], axis=0))
    stacked = jnp.concatenate(stacked, axis=1)
    parts = [
        jnp.dot(left_ref[0, s], stacked, preferred_element_type=F32)
        + jnp.dot(left_ref[1, s], stacked, preferred_element_type=F32)
        for s in range(2)
    ]
    lane = lax.broadcasted_iota(jnp.int32, parts[0].shape, 1) % LANES
    high, low = split_bf16(jnp.where(lane < half, parts[0], parts[1]))
    done = (
        jnp.dot(high, right_ref[0], preferred_element_type=F32)
        + jnp.dot(low, right_ref[0], preferred_element_type=F32)
        + jnp.dot(high, right_ref[1], preferred_element_type=F32)
    ).astype(BF16)
    for side in range(2):
        for c in range(chunks):
            prep_ref[side, :, c * LANES : (c + 1) * LANES] = done[
                c * QBLK : (c + 1) * QBLK, side * LANES : (side + 1) * LANES
            ]


def first_kernel(rows, width, factors_ref, pair_ref, left_ref, right_ref, prep_ref):
    make_factors(rows, width, factors_ref, left_ref, right_ref)
    prepare(pair_ref, left_ref, right_ref, prep_ref)


def near_kernel(done, left_ref, right_ref, *refs):
    prep_ref = refs[-1]
    if done:
        prep_ref[:done] = refs[0][...]
    for index, pair_ref in enumerate(refs[min(done, 1) : -1]):
        prepare(pair_ref, left_ref, right_ref, prep_ref.at[pl.ds(done + 2 * index, 2)])


def last_kernel(order, layer, held, slots, pairs_ref, late_ref, early_ref, train_ref, *refs):
    outs, rows_ref = refs[:-1], refs[-1]
    chips = len(order)
    ready = early_ref.shape[0]
    me = lax.axis_index("ex")
    wanted = [pairs_ref[me * slots + slot] for slot in range(slots)]
    for slot, q in enumerate(wanted):
        source = jnp.maximum(q, 0) // held
        step = (ring_place(me >> 1, chips) - ring_place(source >> 1, chips)) & (chips - 1)
        place = (source ^ me) & 1
        for index, taken in enumerate(order):
            place = jnp.where(step == taken, 2 * index, 0) + place

        @pl.when(place < ready)
        def _():
            rows_ref[slot * QBLK : (slot + 1) * QBLK, :] = early_ref[jnp.minimum(place, ready - 1)]

        @pl.when(place >= ready)
        def _():
            rows_ref[slot * QBLK : (slot + 1) * QBLK, :] = late_ref[jnp.maximum(place - ready, 0)]

    tile = lax.dot_general(
        rows_ref[...], train_ref[...], (((1,), (1,)), ((), ())), preferred_element_type=F32
    )
    rows = QBLK // layer
    chosen = []
    for slot, q in enumerate(wanted):
        value = tile[slot * QBLK : (slot + 1) * QBLK]
        chosen.append(jnp.where(q >= 0, value, jnp.zeros_like(value)))
    for m in range(layer):
        part = jnp.concatenate([value[m * rows : (m + 1) * rows] for value in chosen], axis=0)
        outs[m][...] = part.astype(outs[m].dtype)


def finish_kernel(layer, *refs):
    parts, out_ref = refs[:layer], refs[layer]
    total = parts[0][...]
    for part in parts[1:]:
        total = total + part[...].astype(F32)
    rows = out_ref.shape[1]
    for slot in range(out_ref.shape[0]):
        out_ref[slot] = total[slot * rows : (slot + 1) * rows]


def shards(train_grads, query_grads, in_precond, out_precond, pair_blocks):
    ex = lax.axis_size("ex")
    layer = lax.axis_size("layer")
    train_rows, layers, features = train_grads.shape
    assert layers == 1
    held = query_grads.shape[0] // QBLK
    slots = pair_blocks.shape[0] // ex
    rows = QBLK // layer
    train = train_grads.reshape(train_rows, features)
    query = query_grads.reshape(query_grads.shape[0], features)
    in_factor = in_precond.reshape(in_precond.shape[1:])
    out_factor = out_precond.reshape(out_precond.shape[1:])
    limit = pltpu.CompilerParams(vmem_limit_bytes=24 * 2**20)

    def pass_on(array, step):
        ring = [ring_chip(place) for place in range(ex // 2)]
        moves = zip(ring, ring[step:] + ring[:step])
        return lax.ppermute(array, "ex", [(2 * a + c, 2 * b + c) for a, b in moves for c in range(2)])

    groups = ex // 2
    find = functools.partial(wanted_block, ex, held, slots)
    other = lax.ppermute(query, "ex", [(i, i ^ 1) for i in range(ex)])
    own = pl.pallas_call(
        functools.partial(own_kernel, find),
        out_shape=[jax.ShapeDtypeStruct((QBLK, features), BF16)] * groups,
        in_specs=[SMEM, VMEM],
        out_specs=[VMEM] * groups,
        compiler_params=limit,
        name="own",
    )(pair_blocks, query)
    picked = pl.pallas_call(
        functools.partial(pick_kernel, find, groups),
        out_shape=[jax.ShapeDtypeStruct((2 * QBLK, features), BF16)] * groups,
        in_specs=[SMEM] + [VMEM] * (1 + groups),
        out_specs=[VMEM] * groups,
        compiler_params=limit,
        name="pick",
    )(pair_blocks, other, *own)

    order = sorted(range(groups), key=lambda step: min(step, groups - step))
    raw = [pass_on(picked[step], step) for step in order[1:-1]]

    stack = features // LANES * QBLK
    span = 2 * LANES
    out_factor, in_factor, far_pick = lax.optimization_barrier((out_factor, in_factor, picked[order[-1]]))
    left, right, far = pl.pallas_call(
        functools.partial(first_kernel, rows, out_factor.shape[0]),
        out_shape=[
            jax.ShapeDtypeStruct((2, 2, stack, 2 * stack), BF16),
            jax.ShapeDtypeStruct((2, span, span), BF16),
            jax.ShapeDtypeStruct((2, QBLK, features), BF16),
        ],
        in_specs=[VMEM] * 2,
        out_specs=[VMEM] * 3,
        compiler_params=limit,
        name="first",
    )(jnp.concatenate([out_factor, in_factor], axis=0), far_pick)
    far = pass_on(far, order[-1])

    early, done = [], 0
    half = len(raw) // 2
    for index, pairs in enumerate(([picked[0]], raw[:half], raw[half:])):
        early = [
            pl.pallas_call(
                functools.partial(near_kernel, done),
                out_shape=jax.ShapeDtypeStruct((done + 2 * len(pairs), QBLK, features), BF16),
                in_specs=[VMEM] * (2 + len(early) + len(pairs)),
                out_specs=VMEM,
                compiler_params=limit,
                name=f"near{index}",
            )(left, right, *early, *pairs)
        ]
        done += 2 * len(pairs)
    parts = pl.pallas_call(
        functools.partial(last_kernel, order, layer, held, slots),
        out_shape=[jax.ShapeDtypeStruct((slots * rows, train_rows), F32)]
        + [jax.ShapeDtypeStruct((slots * rows, train_rows), BF16)] * (layer - 1),
        in_specs=[SMEM] + [VMEM] * 3,
        out_specs=[VMEM] * layer,
        scratch_shapes=[pltpu.VMEM((slots * QBLK, features), BF16)],
        compiler_params=limit,
        name="last",
    )(pair_blocks, far, *early, train)

    terms = [parts[0]] + [
        lax.ppermute(parts[m], "layer", [(i, (i + m) % layer) for i in range(layer)]) for m in range(1, layer)
    ]
    out = pl.pallas_call(
        functools.partial(finish_kernel, layer),
        out_shape=jax.ShapeDtypeStruct((slots, rows, train_rows), F32),
        in_specs=[VMEM] * layer,
        out_specs=VMEM,
        compiler_params=limit,
        name="finish",
    )(*terms)
    return jnp.transpose(out, (1, 0, 2))


def solution(mesh):
    in_specs = (
        P("ex", "layer", None),
        P("ex", "layer", None),
        P("layer", None, None),
        P("layer", None, None),
        P(),
    )
    out_specs = P("layer", "ex", None)
    return jax.shard_map(shards, mesh=mesh, in_specs=in_specs, out_specs=out_specs, check_vma=False)
```

```python
import functools

import jax
import jax.numpy as jnp
from jax import lax
from jax.experimental import pallas as pl
from jax.experimental.pallas import tpu as pltpu
from jax.sharding import PartitionSpec as P

QBLK = 16
LANES = 128
F32 = jnp.float32
BF16 = jnp.bfloat16

VMEM = pl.BlockSpec(memory_space=pltpu.VMEM)
SMEM = pl.BlockSpec(memory_space=pltpu.SMEM)


def split_bf16(x):
    high = x.astype(BF16)
    return high, (x - high.astype(F32)).astype(BF16)


def over_slots(slots, body, init):
    if slots > 8:
        return lax.fori_loop(0, slots, body, init)
    for slot in range(slots):
        init = body(slot, init)
    return init


def ring_chip(place):
    return place ^ (place >> 1)


def ring_place(chip, chips):
    place, shift = chip, 1
    while shift < chips:
        place, shift = place ^ (place >> shift), 2 * shift
    return place


def pick_kernel(ex, held, slots, order, pairs_ref, query_ref, *outs):
    me = lax.axis_index("ex")
    chips = ex // 2
    place = ring_place(me >> 1, chips)
    self_ref, near_refs, far_ref, swap_ref = outs[0], outs[1:-2], outs[-2], outs[-1]
    targets = [self_ref, swap_ref.at[pl.ds(0, QBLK)], *near_refs, far_ref, swap_ref.at[pl.ds(QBLK, QBLK)]]
    for index, out_ref in enumerate(targets):
        target = 2 * ring_chip((place + order[index // 2]) & (chips - 1)) + ((me & 1) ^ (index % 2))

        def body(slot, block):
            local = pairs_ref[target * slots + slot] - me * held
            return jnp.where((local >= 0) & (local < held), local, block)

        block = over_slots(slots, body, jnp.int32(0))
        out_ref[...] = query_ref[pl.ds(pl.multiple_of(block * QBLK, QBLK), QBLK), :]


def make_factors(rows, width, factors_ref, left_ref, right_ref):
    in_width = factors_ref.shape[0] - width
    half = left_ref.shape[2]
    span = right_ref.shape[1]
    outs = split_bf16(factors_ref[:width])
    ins = split_bf16(factors_ref[width:])
    row = lax.broadcasted_iota(jnp.int32, (half // QBLK, width), 0)
    row_o = lax.broadcasted_iota(jnp.int32, (half // QBLK, width), 1)
    col = lax.broadcasted_iota(jnp.int32, (width, half), 1) // QBLK
    col_o = lax.broadcasted_iota(jnp.int32, (width, half), 0)
    a = lax.broadcasted_iota(jnp.int32, (half, half), 1) - lax.broadcasted_iota(jnp.int32, (half, half), 0)
    same = (a & (QBLK - 1)) == lax.axis_index("layer") * rows
    for h in range(2):
        for s in range(2):
            pick_rows = (row * 2 + s == row_o).astype(BF16)
            rows = jnp.dot(pick_rows, outs[h], preferred_element_type=F32).astype(BF16)
            for t in range(2):
                pick_cols = (col * 2 + (s ^ t) == col_o).astype(BF16)
                spread = jnp.dot(rows, pick_cols, preferred_element_type=F32)
                tall = jnp.broadcast_to(spread[:, None, :], (half // QBLK, QBLK, half)).reshape(half, half)
                left_ref[h, s, :, t * half : (t + 1) * half] = jnp.where(same, tall, 0.0).astype(BF16)
        up = (
            lax.broadcasted_iota(jnp.int32, (span, in_width), 0) % in_width
            == lax.broadcasted_iota(jnp.int32, (span, in_width), 1)
        ).astype(BF16)
        down = (
            lax.broadcasted_iota(jnp.int32, (in_width, span), 1) % in_width
            == lax.broadcasted_iota(jnp.int32, (in_width, span), 0)
        ).astype(BF16)
        wide = jnp.dot(
            jnp.dot(up, ins[h], preferred_element_type=F32).astype(BF16), down, preferred_element_type=F32
        )
        block = (lax.broadcasted_iota(jnp.int32, (span, span), 0) // in_width) == (
            lax.broadcasted_iota(jnp.int32, (span, span), 1) // in_width
        )
        right_ref[h] = jnp.where(block, wide, 0.0).astype(BF16)


def prepare(blocks, left_ref, right_ref, prep_ref):
    chunks = blocks[0].shape[1] // LANES
    half = LANES // 2
    stacked = []
    for block in blocks:
        tall = jnp.concatenate([block[:, c * LANES : (c + 1) * LANES] for c in range(chunks)], axis=0)
        turned = jnp.concatenate([tall[:, half:], tall[:, :half]], axis=1)
        stacked.append(jnp.concatenate([tall, turned], axis=0))
    stacked = jnp.concatenate(stacked, axis=1)
    parts = [
        jnp.dot(left_ref[0, s], stacked, preferred_element_type=F32)
        + jnp.dot(left_ref[1, s], stacked, preferred_element_type=F32)
        for s in range(2)
    ]
    lane = lax.broadcasted_iota(jnp.int32, parts[0].shape, 1) % LANES
    high, low = split_bf16(jnp.where(lane < half, parts[0], parts[1]))
    done = (
        jnp.dot(high, right_ref[0], preferred_element_type=F32)
        + jnp.dot(low, right_ref[0], preferred_element_type=F32)
        + jnp.dot(high, right_ref[1], preferred_element_type=F32)
    ).astype(BF16)
    for side in range(2):
        for c in range(chunks):
            prep_ref[side, :, c * LANES : (c + 1) * LANES] = done[
                c * QBLK : (c + 1) * QBLK, side * LANES : (side + 1) * LANES
            ]


def first_kernel(rows, width, factors_ref, far_ref, swap_ref, left_ref, right_ref, prep_ref):
    make_factors(rows, width, factors_ref, left_ref, right_ref)
    prepare((far_ref[...], swap_ref[QBLK:]), left_ref, right_ref, prep_ref)


def near_kernel(done, left_ref, right_ref, *refs):
    prep_ref = refs[-1]
    if done:
        prep_ref[:done] = refs[0][...]
    blocks = [ref[:QBLK] for ref in refs[min(done, 1) : -1]]
    for index in range(0, len(blocks), 2):
        prepare(blocks[index : index + 2], left_ref, right_ref, prep_ref.at[pl.ds(done + index, 2)])


def last_kernel(order, layer, held, slots, pairs_ref, late_ref, early_ref, train_ref, *refs):
    outs, rows_ref = refs[:-1], refs[-1]
    chips = len(order)
    ready = early_ref.shape[0]
    me = lax.axis_index("ex")
    wanted = [pairs_ref[me * slots + slot] for slot in range(slots)]
    for slot, q in enumerate(wanted):
        source = jnp.maximum(q, 0) // held
        step = (ring_place(me >> 1, chips) - ring_place(source >> 1, chips)) & (chips - 1)
        place = (source ^ me) & 1
        for index, taken in enumerate(order):
            place = jnp.where(step == taken, 2 * index, 0) + place

        @pl.when(place < ready)
        def _():
            rows_ref[slot * QBLK : (slot + 1) * QBLK, :] = early_ref[jnp.minimum(place, ready - 1)]

        @pl.when(place >= ready)
        def _():
            rows_ref[slot * QBLK : (slot + 1) * QBLK, :] = late_ref[jnp.maximum(place - ready, 0)]

    tile = lax.dot_general(
        rows_ref[...], train_ref[...], (((1,), (1,)), ((), ())), preferred_element_type=F32
    )
    rows = QBLK // layer
    chosen = []
    for slot, q in enumerate(wanted):
        value = tile[slot * QBLK : (slot + 1) * QBLK]
        chosen.append(jnp.where(q >= 0, value, jnp.zeros_like(value)))
    for m in range(layer):
        part = jnp.concatenate([value[m * rows : (m + 1) * rows] for value in chosen], axis=0)
        outs[m][...] = part.astype(outs[m].dtype)


def finish_kernel(layer, *refs):
    parts, out_ref = refs[:layer], refs[layer]
    total = parts[0][...]
    for part in parts[1:]:
        total = total + part[...].astype(F32)
    rows = out_ref.shape[1]
    for slot in range(out_ref.shape[0]):
        out_ref[slot] = total[slot * rows : (slot + 1) * rows]


def shards(train_grads, query_grads, in_precond, out_precond, pair_blocks):
    ex = lax.axis_size("ex")
    layer = lax.axis_size("layer")
    train_rows, layers, features = train_grads.shape
    assert layers == 1
    held = query_grads.shape[0] // QBLK
    slots = pair_blocks.shape[0] // ex
    rows = QBLK // layer
    train = train_grads.reshape(train_rows, features)
    query = query_grads.reshape(query_grads.shape[0], features)
    in_factor = in_precond.reshape(in_precond.shape[1:])
    out_factor = out_precond.reshape(out_precond.shape[1:])
    limit = pltpu.CompilerParams(vmem_limit_bytes=24 * 2**20)

    work = pl.CostEstimate(flops=2 * 10**9, bytes_accessed=1000, transcendentals=0)
    groups = ex // 2
    order = sorted(range(groups), key=lambda step: min(step, groups - step))

    def pass_on(array, step, flip=0):
        ring = [ring_chip(place) for place in range(groups)]
        moves = zip(ring, ring[step:] + ring[:step])
        return lax.ppermute(array, "ex", [(2 * a + c, 2 * b + (c ^ flip)) for a, b in moves for c in range(2)])

    block = jax.ShapeDtypeStruct((QBLK, features), BF16)
    picked = pl.pallas_call(
        functools.partial(pick_kernel, ex, held, slots, order),
        out_shape=[block] * (ex - 2) + [jax.ShapeDtypeStruct((2 * QBLK, features), BF16)],
        in_specs=[SMEM, VMEM],
        out_specs=[VMEM] * (ex - 1),
        compiler_params=limit,
        name="pick",
    )(pair_blocks, query)
    near = picked[1:-2]
    raw = [None] * len(near)
    for flip in range(2):
        for index in range(flip, len(near), 2):
            raw[index] = pass_on(near[index], order[1 + index // 2], flip)
        if flip == 0:
            swapped = pass_on(picked[-1], 0, 1)

    stack = features // LANES * QBLK
    span = 2 * LANES
    out_factor, in_factor, far_pick = lax.optimization_barrier((out_factor, in_factor, picked[-2]))
    left, right, far = pl.pallas_call(
        functools.partial(first_kernel, rows, out_factor.shape[0]),
        out_shape=[
            jax.ShapeDtypeStruct((2, 2, stack, 2 * stack), BF16),
            jax.ShapeDtypeStruct((2, span, span), BF16),
            jax.ShapeDtypeStruct((2, QBLK, features), BF16),
        ],
        in_specs=[VMEM] * 3,
        out_specs=[VMEM] * 3,
        compiler_params=limit,
        name="first",
        cost_estimate=work,
    )(jnp.concatenate([out_factor, in_factor], axis=0), far_pick, swapped)
    far = pass_on(far, order[-1])

    early, done = [], 0
    half = len(raw) // 4 * 2
    for index, blocks in enumerate(([picked[0], swapped], raw[:half], raw[half:])):
        early = [
            pl.pallas_call(
                functools.partial(near_kernel, done),
                out_shape=jax.ShapeDtypeStruct((done + len(blocks), QBLK, features), BF16),
                in_specs=[VMEM] * (2 + len(early) + len(blocks)),
                out_specs=VMEM,
                compiler_params=limit,
                name=f"near{index}",
                cost_estimate=work,
            )(left, right, *early, *blocks)
        ]
        done += len(blocks)
    parts = pl.pallas_call(
        functools.partial(last_kernel, order, layer, held, slots),
        out_shape=[jax.ShapeDtypeStruct((slots * rows, train_rows), F32)]
        + [jax.ShapeDtypeStruct((slots * rows, train_rows), BF16)] * (layer - 1),
        in_specs=[SMEM] + [VMEM] * 3,
        out_specs=[VMEM] * layer,
        scratch_shapes=[pltpu.VMEM((slots * QBLK, features), BF16)],
        compiler_params=limit,
        name="last",
    )(pair_blocks, far, *early, train)

    terms = [parts[0]] + [
        lax.ppermute(parts[m], "layer", [(i, (i + m) % layer) for i in range(layer)]) for m in range(1, layer)
    ]
    out = pl.pallas_call(
        functools.partial(finish_kernel, layer),
        out_shape=jax.ShapeDtypeStruct((slots, rows, train_rows), F32),
        in_specs=[VMEM] * layer,
        out_specs=VMEM,
        compiler_params=limit,
        name="finish",
    )(*terms)
    return jnp.transpose(out, (1, 0, 2))


def solution(mesh):
    in_specs = (
        P("ex", "layer", None),
        P("ex", "layer", None),
        P("layer", None, None),
        P("layer", None, None),
        P(),
    )
    out_specs = P("layer", "ex", None)
    return jax.shard_map(shards, mesh=mesh, in_specs=in_specs, out_specs=out_specs, check_vma=False)
```

```python
import functools

import jax
import jax.numpy as jnp
from jax import lax
from jax.experimental import pallas as pl
from jax.experimental.pallas import tpu as pltpu
from jax.sharding import PartitionSpec as P

QBLK = 16
LANES = 128
F32 = jnp.float32
BF16 = jnp.bfloat16

VMEM = pl.BlockSpec(memory_space=pltpu.VMEM)
SMEM = pl.BlockSpec(memory_space=pltpu.SMEM)


def split_bf16(x):
    high = x.astype(BF16)
    return high, (x - high.astype(F32)).astype(BF16)


def over_slots(slots, body, init):
    if slots > 8:
        return lax.fori_loop(0, slots, body, init)
    for slot in range(slots):
        init = body(slot, init)
    return init


def ring_chip(place):
    return place ^ (place >> 1)


def ring_place(chip, chips):
    place, shift = chip, 1
    while shift < chips:
        place, shift = place ^ (place >> shift), 2 * shift
    return place


def wanted_block(ex, held, slots, pairs_ref, step, side):
    me = lax.axis_index("ex")
    chips = ex // 2
    target = ring_chip((ring_place(me >> 1, chips) + step) & (chips - 1))
    first = (2 * target + (me & 1)) * slots
    base = (me ^ side) * held

    def body(slot, block):
        local = pairs_ref[first + slot] - base
        return jnp.where((local >= 0) & (local < held), local, block)

    return pl.multiple_of(over_slots(slots, body, jnp.int32(0)) * QBLK, QBLK)


def own_kernel(find, pairs_ref, query_ref, *outs):
    for group, out_ref in enumerate(outs):
        out_ref[...] = query_ref[pl.ds(find(pairs_ref, group, 0), QBLK), :]


def pick_kernel(find, groups, pairs_ref, other_ref, *refs):
    for group in range(groups):
        out_ref = refs[groups + group]
        out_ref[:QBLK] = refs[group][...]
        out_ref[QBLK:] = other_ref[pl.ds(find(pairs_ref, group, 1), QBLK), :]


def make_factors(rows, width, factors_ref, left_ref, right_ref):
    in_width = factors_ref.shape[0] - width
    half = left_ref.shape[1] // 2
    span = right_ref.shape[1]
    outs = split_bf16(factors_ref[:width])
    ins = split_bf16(factors_ref[width:])
    row = lax.broadcasted_iota(jnp.int32, (half // QBLK, width), 0)
    row_o = lax.broadcasted_iota(jnp.int32, (half // QBLK, width), 1)
    col = lax.broadcasted_iota(jnp.int32, (width, half), 1) // QBLK
    col_o = lax.broadcasted_iota(jnp.int32, (width, half), 0)
    a = lax.broadcasted_iota(jnp.int32, (half, half), 1) - lax.broadcasted_iota(jnp.int32, (half, half), 0)
    same = (a & (QBLK - 1)) == lax.axis_index("layer") * rows
    for h in range(2):
        for s in range(2):
            pick_rows = (row * 2 + s == row_o).astype(BF16)
            part = jnp.dot(pick_rows, outs[h], preferred_element_type=F32).astype(BF16)
            start = (2 * h + s) * half
            for t in range(2):
                pick_cols = (col * 2 + (s ^ t) == col_o).astype(BF16)
                spread = jnp.dot(part, pick_cols, preferred_element_type=F32)
                tall = jnp.broadcast_to(spread[:, None, :], (half // QBLK, QBLK, half)).reshape(half, half)
                left_ref[start : start + half, t * half : (t + 1) * half] = jnp.where(same, tall, 0.0).astype(BF16)
    up = (
        lax.broadcasted_iota(jnp.int32, (span, in_width), 0) % in_width
        == lax.broadcasted_iota(jnp.int32, (span, in_width), 1)
    ).astype(BF16)
    down = (
        lax.broadcasted_iota(jnp.int32, (in_width, span), 1) % in_width
        == lax.broadcasted_iota(jnp.int32, (in_width, span), 0)
    ).astype(BF16)
    block = (lax.broadcasted_iota(jnp.int32, (span, span), 0) // in_width) == (
        lax.broadcasted_iota(jnp.int32, (span, span), 1) // in_width
    )
    for h in range(2):
        wide = jnp.dot(
            jnp.dot(up, ins[h], preferred_element_type=F32).astype(BF16), down, preferred_element_type=F32
        )
        wide = jnp.where(block, wide, 0.0).astype(BF16)
        right_ref[h * span : (h + 1) * span] = wide
        if h == 0:
            right_ref[2 * span :] = wide


def prepare(pair_ref, left_ref, right_ref, prep_ref):
    chunks = pair_ref.shape[1] // LANES
    half = LANES // 2
    stacked = []
    for side in range(2):
        block = pair_ref[side * QBLK : (side + 1) * QBLK, :]
        tall = jnp.concatenate([block[:, c * LANES : (c + 1) * LANES] for c in range(chunks)], axis=0)
        turned = jnp.concatenate([tall[:, half:], tall[:, :half]], axis=1)
        stacked.append(jnp.concatenate([tall, turned], axis=0))
    stacked = jnp.concatenate(stacked, axis=1)
    tall = jnp.dot(left_ref[...], stacked, preferred_element_type=F32)
    quarter = tall.shape[0] // 4
    parts = [tall[s * quarter : (s + 1) * quarter] + tall[(2 + s) * quarter : (3 + s) * quarter] for s in range(2)]
    lane = lax.broadcasted_iota(jnp.int32, parts[0].shape, 1) % LANES
    high, low = split_bf16(jnp.where(lane < half, parts[0], parts[1]))
    done = jnp.dot(
        jnp.concatenate([high, high, low], axis=1), right_ref[...], preferred_element_type=F32
    ).astype(BF16)
    for side in range(2):
        for c in range(chunks):
            prep_ref[side, :, c * LANES : (c + 1) * LANES] = done[
                c * QBLK : (c + 1) * QBLK, side * LANES : (side + 1) * LANES
            ]


def first_kernel(rows, width, factors_ref, pair_ref, left_ref, right_ref, prep_ref):
    make_factors(rows, width, factors_ref, left_ref, right_ref)
    prepare(pair_ref, left_ref, right_ref, prep_ref)


def near_kernel(done, left_ref, right_ref, *refs):
    prep_ref = refs[-1]
    if done:
        prep_ref[:done] = refs[0][...]
    for index, pair_ref in enumerate(refs[min(done, 1) : -1]):
        prepare(pair_ref, left_ref, right_ref, prep_ref.at[pl.ds(done + 2 * index, 2)])


def last_kernel(order, layer, held, slots, pairs_ref, late_ref, early_ref, train_ref, *refs):
    outs, rows_ref = refs[:-1], refs[-1]
    chips = len(order)
    ready = early_ref.shape[0]
    me = lax.axis_index("ex")
    wanted = [pairs_ref[me * slots + slot] for slot in range(slots)]
    for slot, q in enumerate(wanted):
        source = jnp.maximum(q, 0) // held
        step = (ring_place(me >> 1, chips) - ring_place(source >> 1, chips)) & (chips - 1)
        place = (source ^ me) & 1
        for index, taken in enumerate(order):
            place = jnp.where(step == taken, 2 * index, 0) + place

        @pl.when(place < ready)
        def _():
            rows_ref[slot * QBLK : (slot + 1) * QBLK, :] = early_ref[jnp.minimum(place, ready - 1)]

        @pl.when(place >= ready)
        def _():
            rows_ref[slot * QBLK : (slot + 1) * QBLK, :] = late_ref[jnp.maximum(place - ready, 0)]

    tile = lax.dot_general(
        rows_ref[...], train_ref[...], (((1,), (1,)), ((), ())), preferred_element_type=F32
    )
    rows = QBLK // layer
    chosen = []
    for slot, q in enumerate(wanted):
        value = tile[slot * QBLK : (slot + 1) * QBLK]
        chosen.append(jnp.where(q >= 0, value, jnp.zeros_like(value)))
    for m in range(layer):
        part = jnp.concatenate([value[m * rows : (m + 1) * rows] for value in chosen], axis=0)
        outs[m][...] = part.astype(outs[m].dtype)


def finish_kernel(layer, *refs):
    parts, out_ref = refs[:layer], refs[layer]
    total = parts[0][...]
    for part in parts[1:]:
        total = total + part[...].astype(F32)
    rows = out_ref.shape[1]
    for slot in range(out_ref.shape[0]):
        out_ref[slot] = total[slot * rows : (slot + 1) * rows]


def shards(train_grads, query_grads, in_precond, out_precond, pair_blocks):
    ex = lax.axis_size("ex")
    layer = lax.axis_size("layer")
    train_rows, layers, features = train_grads.shape
    assert layers == 1
    held = query_grads.shape[0] // QBLK
    slots = pair_blocks.shape[0] // ex
    rows = QBLK // layer
    train = train_grads.reshape(train_rows, features)
    query = query_grads.reshape(query_grads.shape[0], features)
    in_factor = in_precond.reshape(in_precond.shape[1:])
    out_factor = out_precond.reshape(out_precond.shape[1:])
    limit = pltpu.CompilerParams(vmem_limit_bytes=24 * 2**20)

    def pass_on(array, step):
        ring = [ring_chip(place) for place in range(ex // 2)]
        moves = zip(ring, ring[step:] + ring[:step])
        return lax.ppermute(array, "ex", [(2 * a + c, 2 * b + c) for a, b in moves for c in range(2)])

    groups = ex // 2
    find = functools.partial(wanted_block, ex, held, slots)
    other = lax.ppermute(query, "ex", [(i, i ^ 1) for i in range(ex)])
    own = pl.pallas_call(
        functools.partial(own_kernel, find),
        out_shape=[jax.ShapeDtypeStruct((QBLK, features), BF16)] * groups,
        in_specs=[SMEM, VMEM],
        out_specs=[VMEM] * groups,
        compiler_params=limit,
        name="own",
    )(pair_blocks, query)
    picked = pl.pallas_call(
        functools.partial(pick_kernel, find, groups),
        out_shape=[jax.ShapeDtypeStruct((2 * QBLK, features), BF16)] * groups,
        in_specs=[SMEM] + [VMEM] * (1 + groups),
        out_specs=[VMEM] * groups,
        compiler_params=limit,
        name="pick",
    )(pair_blocks, other, *own)

    order = sorted(range(groups), key=lambda step: min(step, groups - step))
    raw = [pass_on(picked[step], step) for step in order[1:-1]]

    stack = features // LANES * QBLK
    span = 2 * LANES
    out_factor, in_factor, far_pick = lax.optimization_barrier((out_factor, in_factor, picked[order[-1]]))
    left, right, far = pl.pallas_call(
        functools.partial(first_kernel, rows, out_precond.shape[-1]),
        out_shape=[
            jax.ShapeDtypeStruct((4 * stack, 2 * stack), BF16),
            jax.ShapeDtypeStruct((3 * span, span), BF16),
            jax.ShapeDtypeStruct((2, QBLK, features), BF16),
        ],
        in_specs=[VMEM] * 2,
        out_specs=[VMEM] * 3,
        compiler_params=limit,
        name="first",
    )(jnp.concatenate([out_factor, in_factor], axis=0), far_pick)
    far = pass_on(far, order[-1])

    early, done = [], 0
    half = len(raw) // 2
    for index, pairs in enumerate(([picked[0]], raw[:half], raw[half:])):
        early = [
            pl.pallas_call(
                functools.partial(near_kernel, done),
                out_shape=jax.ShapeDtypeStruct((done + 2 * len(pairs), QBLK, features), BF16),
                in_specs=[VMEM] * (2 + len(early) + len(pairs)),
                out_specs=VMEM,
                compiler_params=limit,
                name=f"near{index}",
            )(left, right, *early, *pairs)
        ]
        done += 2 * len(pairs)
    parts = pl.pallas_call(
        functools.partial(last_kernel, order, layer, held, slots),
        out_shape=[jax.ShapeDtypeStruct((slots * rows, train_rows), F32)]
        + [jax.ShapeDtypeStruct((slots * rows, train_rows), BF16)] * (layer - 1),
        in_specs=[SMEM] + [VMEM] * 3,
        out_specs=[VMEM] * layer,
        scratch_shapes=[pltpu.VMEM((slots * QBLK, features), BF16)],
        compiler_params=limit,
        name="last",
    )(pair_blocks, far, *early, train)

    terms = [parts[0]] + [
        lax.ppermute(parts[m], "layer", [(i, (i + m) % layer) for i in range(layer)]) for m in range(1, layer)
    ]
    out = pl.pallas_call(
        functools.partial(finish_kernel, layer),
        out_shape=jax.ShapeDtypeStruct((slots, rows, train_rows), F32),
        in_specs=[VMEM] * layer,
        out_specs=VMEM,
        compiler_params=limit,
        name="finish",
    )(*terms)
    return jnp.transpose(out, (1, 0, 2))


def solution(mesh):
    in_specs = (
        P("ex", "layer", None),
        P("ex", "layer", None),
        P("layer", None, None),
        P("layer", None, None),
        P(),
    )
    out_specs = P("layer", "ex", None)
    return jax.shard_map(shards, mesh=mesh, in_specs=in_specs, out_specs=out_specs, check_vma=False)
```

```python
import functools

import jax
import jax.numpy as jnp
from jax import lax
from jax.experimental import pallas as pl
from jax.experimental.pallas import tpu as pltpu
from jax.sharding import PartitionSpec as P

QBLK = 16
LANES = 128
F32 = jnp.float32
BF16 = jnp.bfloat16

VMEM = pl.BlockSpec(memory_space=pltpu.VMEM)
SMEM = pl.BlockSpec(memory_space=pltpu.SMEM)


def split_bf16(x):
    high = x.astype(BF16)
    return high, (x - high.astype(F32)).astype(BF16)


def over_slots(slots, body, init):
    if slots > 8:
        return lax.fori_loop(0, slots, body, init)
    for slot in range(slots):
        init = body(slot, init)
    return init


def ring_chip(place):
    return place ^ (place >> 1)


def ring_place(chip, chips):
    place, shift = chip, 1
    while shift < chips:
        place, shift = place ^ (place >> shift), 2 * shift
    return place


def wanted_block(ex, held, slots, pairs_ref, step, side):
    me = lax.axis_index("ex")
    chips = ex // 2
    target = ring_chip((ring_place(me >> 1, chips) + step) & (chips - 1))
    first = (2 * target + (me & 1)) * slots
    base = (me ^ side) * held

    def body(slot, block):
        local = pairs_ref[first + slot] - base
        return jnp.where((local >= 0) & (local < held), local, block)

    return pl.multiple_of(over_slots(slots, body, jnp.int32(0)) * QBLK, QBLK)


def own_kernel(find, pairs_ref, query_ref, *outs):
    for group, out_ref in enumerate(outs):
        out_ref[...] = query_ref[pl.ds(find(pairs_ref, group, 0), QBLK), :]


def pick_kernel(find, groups, pairs_ref, other_ref, *refs):
    for group in range(groups):
        out_ref = refs[groups + group]
        out_ref[:QBLK] = refs[group][...]
        out_ref[QBLK:] = other_ref[pl.ds(find(pairs_ref, group, 1), QBLK), :]


def make_factors(rows, width, factors_ref, left_ref, right_ref):
    in_width = factors_ref.shape[0] - width
    half = left_ref.shape[0] // 2
    span = right_ref.shape[1]
    outs = split_bf16(factors_ref[:width])
    ins = split_bf16(factors_ref[width:])
    row = lax.broadcasted_iota(jnp.int32, (half // QBLK, width), 0)
    row_o = lax.broadcasted_iota(jnp.int32, (half // QBLK, width), 1)
    col = lax.broadcasted_iota(jnp.int32, (width, half), 1) // QBLK
    col_o = lax.broadcasted_iota(jnp.int32, (width, half), 0)
    a = lax.broadcasted_iota(jnp.int32, (half, half), 1) - lax.broadcasted_iota(jnp.int32, (half, half), 0)
    same = (a & (QBLK - 1)) == lax.axis_index("layer") * rows
    for h in range(2):
        for s in range(2):
            pick_rows = (row * 2 + s == row_o).astype(BF16)
            part = jnp.dot(pick_rows, outs[h], preferred_element_type=F32).astype(BF16)
            for t in range(2):
                pick_cols = (col * 2 + t == col_o).astype(BF16)
                spread = jnp.dot(part, pick_cols, preferred_element_type=F32)
                tall = jnp.broadcast_to(spread[:, None, :], (half // QBLK, QBLK, half)).reshape(half, half)
                start = (2 * h + t) * half
                left_ref[s * half : (s + 1) * half, start : start + half] = jnp.where(same, tall, 0.0).astype(BF16)
    up = (
        lax.broadcasted_iota(jnp.int32, (span, in_width), 0) % in_width
        == lax.broadcasted_iota(jnp.int32, (span, in_width), 1)
    ).astype(BF16)
    down = (
        lax.broadcasted_iota(jnp.int32, (in_width, span), 1) % in_width
        == lax.broadcasted_iota(jnp.int32, (in_width, span), 0)
    ).astype(BF16)
    block = (lax.broadcasted_iota(jnp.int32, (span, span), 0) // in_width) == (
        lax.broadcasted_iota(jnp.int32, (span, span), 1) // in_width
    )
    for h in range(2):
        wide = jnp.dot(
            jnp.dot(up, ins[h], preferred_element_type=F32).astype(BF16), down, preferred_element_type=F32
        )
        wide = jnp.where(block, wide, 0.0).astype(BF16)
        right_ref[h * span : (h + 1) * span] = wide
        if h == 0:
            right_ref[2 * span :] = wide


def swap_halves(x):
    half = x.shape[1] // 2
    return jnp.concatenate([x[:, half:], x[:, :half]], axis=1)


def prepare(blocks, left_ref, right_ref, targets):
    chunks = blocks[0].shape[1] // LANES
    half = chunks * QBLK
    lower = lax.broadcasted_iota(jnp.int32, (half, LANES), 1) < LANES // 2
    talls = [
        jnp.concatenate([block[:, c * LANES : (c + 1) * LANES] for c in range(chunks)], axis=0) for block in blocks
    ]
    stacked = []
    for one, two in (talls[:2], talls[2:]):
        stacked.append(
            jnp.concatenate(
                [jnp.where(lower, one, swap_halves(two)), jnp.where(lower, swap_halves(one), two)], axis=0
            )
        )
    stacked = jnp.concatenate(stacked, axis=1)
    high, low = split_bf16(
        jnp.dot(left_ref[...], jnp.concatenate([stacked, stacked], axis=0), preferred_element_type=F32)
    )
    done = jnp.dot(
        jnp.concatenate([high, high, low], axis=1), right_ref[...], preferred_element_type=F32
    ).astype(BF16)
    for pair in range(2):
        even = done[:half, pair * LANES : (pair + 1) * LANES]
        odd = done[half:, pair * LANES : (pair + 1) * LANES]
        for value, (ref, index) in zip(
            (jnp.where(lower, even, swap_halves(odd)), jnp.where(lower, swap_halves(even), odd)),
            targets[2 * pair : 2 * pair + 2],
        ):
            for c in range(chunks):
                ref[index, :, c * LANES : (c + 1) * LANES] = value[c * QBLK : (c + 1) * QBLK]


def halves(refs):
    return [ref[side * QBLK : (side + 1) * QBLK] for ref in refs for side in range(2)]


def first_kernel(rows, width, factors_ref, far_pair_ref, self_pair_ref, left_ref, right_ref, far_ref, self_ref):
    make_factors(rows, width, factors_ref, left_ref, right_ref)
    targets = [(far_ref, 0), (far_ref, 1), (self_ref, 0), (self_ref, 1)]
    prepare(halves((far_pair_ref, self_pair_ref)), left_ref, right_ref, targets)


def near_kernel(left_ref, right_ref, self_ref, *refs):
    prep_ref = refs[-1]
    prep_ref[:2] = self_ref[...]
    blocks = halves(refs[:-1])
    targets = [(prep_ref, 2 + index) for index in range(len(blocks))]
    for start in range(0, len(blocks), 4):
        pick = slice(start, start + 4) if start + 4 <= len(blocks) else slice(-2, None)
        times = 1 if start + 4 <= len(blocks) else 2
        prepare(blocks[pick] * times, left_ref, right_ref, targets[pick] * times)


def last_kernel(order, layer, held, slots, pairs_ref, late_ref, early_ref, train_ref, *refs):
    outs, rows_ref = refs[:-1], refs[-1]
    chips = len(order)
    ready = early_ref.shape[0]
    me = lax.axis_index("ex")
    wanted = [pairs_ref[me * slots + slot] for slot in range(slots)]
    for slot, q in enumerate(wanted):
        source = jnp.maximum(q, 0) // held
        step = (ring_place(me >> 1, chips) - ring_place(source >> 1, chips)) & (chips - 1)
        place = (source ^ me) & 1
        for index, taken in enumerate(order):
            place = jnp.where(step == taken, 2 * index, 0) + place

        @pl.when(place < ready)
        def _():
            rows_ref[slot * QBLK : (slot + 1) * QBLK, :] = early_ref[jnp.minimum(place, ready - 1)]

        @pl.when(place >= ready)
        def _():
            rows_ref[slot * QBLK : (slot + 1) * QBLK, :] = late_ref[jnp.maximum(place - ready, 0)]

    tile = lax.dot_general(
        rows_ref[...], train_ref[...], (((1,), (1,)), ((), ())), preferred_element_type=F32
    )
    rows = QBLK // layer
    chosen = []
    for slot, q in enumerate(wanted):
        value = tile[slot * QBLK : (slot + 1) * QBLK]
        chosen.append(jnp.where(q >= 0, value, jnp.zeros_like(value)))
    for m in range(layer):
        part = jnp.concatenate([value[m * rows : (m + 1) * rows] for value in chosen], axis=0)
        outs[m][...] = part.astype(outs[m].dtype)


def finish_kernel(layer, *refs):
    parts, out_ref = refs[:layer], refs[layer]
    total = parts[0][...]
    for part in parts[1:]:
        total = total + part[...].astype(F32)
    rows = out_ref.shape[1]
    for slot in range(out_ref.shape[0]):
        out_ref[slot] = total[slot * rows : (slot + 1) * rows]


def shards(train_grads, query_grads, in_precond, out_precond, pair_blocks):
    ex = lax.axis_size("ex")
    layer = lax.axis_size("layer")
    train_rows, layers, features = train_grads.shape
    assert layers == 1
    held = query_grads.shape[0] // QBLK
    slots = pair_blocks.shape[0] // ex
    rows = QBLK // layer
    train = train_grads.reshape(train_rows, features)
    query = query_grads.reshape(query_grads.shape[0], features)
    in_factor = in_precond.reshape(in_precond.shape[1:])
    out_factor = out_precond.reshape(out_precond.shape[1:])
    limit = pltpu.CompilerParams(vmem_limit_bytes=24 * 2**20)

    def pass_on(array, step):
        ring = [ring_chip(place) for place in range(ex // 2)]
        moves = zip(ring, ring[step:] + ring[:step])
        return lax.ppermute(array, "ex", [(2 * a + c, 2 * b + c) for a, b in moves for c in range(2)])

    groups = ex // 2
    find = functools.partial(wanted_block, ex, held, slots)
    other = lax.ppermute(query, "ex", [(i, i ^ 1) for i in range(ex)])
    own = pl.pallas_call(
        functools.partial(own_kernel, find),
        out_shape=[jax.ShapeDtypeStruct((QBLK, features), BF16)] * groups,
        in_specs=[SMEM, VMEM],
        out_specs=[VMEM] * groups,
        compiler_params=limit,
        name="own",
    )(pair_blocks, query)
    picked = pl.pallas_call(
        functools.partial(pick_kernel, find, groups),
        out_shape=[jax.ShapeDtypeStruct((2 * QBLK, features), BF16)] * groups,
        in_specs=[SMEM] + [VMEM] * (1 + groups),
        out_specs=[VMEM] * groups,
        compiler_params=limit,
        name="pick",
    )(pair_blocks, other, *own)

    order = sorted(range(groups), key=lambda step: min(step, groups - step))
    raw = [pass_on(picked[step], step) for step in order[1:-1]]

    stack = features // LANES * QBLK
    span = 2 * LANES
    out_factor, in_factor, far_pick = lax.optimization_barrier((out_factor, in_factor, picked[order[-1]]))
    left, right, far, self_pair = pl.pallas_call(
        functools.partial(first_kernel, rows, out_precond.shape[-1]),
        out_shape=[
            jax.ShapeDtypeStruct((2 * stack, 4 * stack), BF16),
            jax.ShapeDtypeStruct((3 * span, span), BF16),
            jax.ShapeDtypeStruct((2, QBLK, features), BF16),
            jax.ShapeDtypeStruct((2, QBLK, features), BF16),
        ],
        in_specs=[VMEM] * 3,
        out_specs=[VMEM] * 4,
        compiler_params=limit,
        name="first",
    )(jnp.concatenate([out_factor, in_factor], axis=0), far_pick, picked[0])
    far = pass_on(far, order[-1])

    early = pl.pallas_call(
        near_kernel,
        out_shape=jax.ShapeDtypeStruct((ex - 2, QBLK, features), BF16),
        in_specs=[VMEM] * (3 + len(raw)),
        out_specs=VMEM,
        compiler_params=limit,
        name="near",
    )(left, right, self_pair, *raw)
    parts = pl.pallas_call(
        functools.partial(last_kernel, order, layer, held, slots),
        out_shape=[jax.ShapeDtypeStruct((slots * rows, train_rows), F32)]
        + [jax.ShapeDtypeStruct((slots * rows, train_rows), BF16)] * (layer - 1),
        in_specs=[SMEM] + [VMEM] * 3,
        out_specs=[VMEM] * layer,
        scratch_shapes=[pltpu.VMEM((slots * QBLK, features), BF16)],
        compiler_params=limit,
        name="last",
    )(pair_blocks, far, early, train)

    terms = [parts[0]] + [
        lax.ppermute(parts[m], "layer", [(i, (i + m) % layer) for i in range(layer)]) for m in range(1, layer)
    ]
    out = pl.pallas_call(
        functools.partial(finish_kernel, layer),
        out_shape=jax.ShapeDtypeStruct((slots, rows, train_rows), F32),
        in_specs=[VMEM] * layer,
        out_specs=VMEM,
        compiler_params=limit,
        name="finish",
    )(*terms)
    return jnp.transpose(out, (1, 0, 2))


def solution(mesh):
    in_specs = (
        P("ex", "layer", None),
        P("ex", "layer", None),
        P("layer", None, None),
        P("layer", None, None),
        P(),
    )
    out_specs = P("layer", "ex", None)
    return jax.shard_map(shards, mesh=mesh, in_specs=in_specs, out_specs=out_specs, check_vma=False)
```

```python
import functools

import jax
import jax.numpy as jnp
from jax import lax
from jax.experimental import pallas as pl
from jax.experimental.pallas import tpu as pltpu
from jax.sharding import PartitionSpec as P

QBLK = 16
LANES = 128
F32 = jnp.float32
BF16 = jnp.bfloat16

VMEM = pl.BlockSpec(memory_space=pltpu.VMEM)
SMEM = pl.BlockSpec(memory_space=pltpu.SMEM)


def split_bf16(x):
    high = x.astype(BF16)
    return high, (x - high.astype(F32)).astype(BF16)


def over_slots(slots, body, init):
    if slots > 8:
        return lax.fori_loop(0, slots, body, init)
    for slot in range(slots):
        init = body(slot, init)
    return init


def ring_chip(place):
    return place ^ (place >> 1)


def ring_place(chip, chips):
    place, shift = chip, 1
    while shift < chips:
        place, shift = place ^ (place >> shift), 2 * shift
    return place


def pick_kernel(ex, held, slots, order, pairs_ref, query_ref, self_ref, far_ref, swap_ref, *near_refs):
    me = lax.axis_index("ex")
    chips = ex // 2
    place = ring_place(me >> 1, chips)
    targets = [self_ref, swap_ref.at[pl.ds(0, QBLK)]]
    for ref in near_refs:
        targets += [ref.at[pl.ds(0, QBLK)], ref.at[pl.ds(QBLK, QBLK)]]
    targets += [far_ref, swap_ref.at[pl.ds(QBLK, QBLK)]]
    for index, out_ref in enumerate(targets):
        target = 2 * ring_chip((place + order[index // 2]) & (chips - 1)) + ((me & 1) ^ (index % 2))

        def body(slot, block):
            local = pairs_ref[target * slots + slot] - me * held
            return jnp.where((local >= 0) & (local < held), local, block)

        block = over_slots(slots, body, jnp.int32(0))
        out_ref[...] = query_ref[pl.ds(pl.multiple_of(block * QBLK, QBLK), QBLK), :]


def cross_kernel(*refs):
    count = len(refs) // 2
    for ref, out_ref in zip(refs[:count], refs[count:]):
        out_ref[...] = ref[QBLK:]


def make_factors(rows, width, factors_ref, left_ref, right_ref):
    in_width = factors_ref.shape[0] - width
    half = left_ref.shape[1] // 2
    span = right_ref.shape[1]
    outs = split_bf16(factors_ref[:width])
    ins = split_bf16(factors_ref[width:])
    row = lax.broadcasted_iota(jnp.int32, (half // QBLK, width), 0)
    row_o = lax.broadcasted_iota(jnp.int32, (half // QBLK, width), 1)
    col = lax.broadcasted_iota(jnp.int32, (width, half), 1) // QBLK
    col_o = lax.broadcasted_iota(jnp.int32, (width, half), 0)
    a = lax.broadcasted_iota(jnp.int32, (half, half), 1) - lax.broadcasted_iota(jnp.int32, (half, half), 0)
    same = (a & (QBLK - 1)) == lax.axis_index("layer") * rows
    for h in range(2):
        for s in range(2):
            pick_rows = (row * 2 + s == row_o).astype(BF16)
            part = jnp.dot(pick_rows, outs[h], preferred_element_type=F32).astype(BF16)
            start = (2 * h + s) * half
            for t in range(2):
                pick_cols = (col * 2 + (s ^ t) == col_o).astype(BF16)
                spread = jnp.dot(part, pick_cols, preferred_element_type=F32)
                tall = jnp.broadcast_to(spread[:, None, :], (half // QBLK, QBLK, half)).reshape(half, half)
                left_ref[start : start + half, t * half : (t + 1) * half] = jnp.where(same, tall, 0.0).astype(BF16)
    up = (
        lax.broadcasted_iota(jnp.int32, (span, in_width), 0) % in_width
        == lax.broadcasted_iota(jnp.int32, (span, in_width), 1)
    ).astype(BF16)
    down = (
        lax.broadcasted_iota(jnp.int32, (in_width, span), 1) % in_width
        == lax.broadcasted_iota(jnp.int32, (in_width, span), 0)
    ).astype(BF16)
    block = (lax.broadcasted_iota(jnp.int32, (span, span), 0) // in_width) == (
        lax.broadcasted_iota(jnp.int32, (span, span), 1) // in_width
    )
    for h in range(2):
        wide = jnp.dot(
            jnp.dot(up, ins[h], preferred_element_type=F32).astype(BF16), down, preferred_element_type=F32
        )
        wide = jnp.where(block, wide, 0.0).astype(BF16)
        right_ref[h * span : (h + 1) * span] = wide
        if h == 0:
            right_ref[2 * span :] = wide


def prepare(blocks, left_ref, right_ref, prep_ref):
    chunks = blocks[0].shape[1] // LANES
    half = LANES // 2
    stacked = []
    for block in blocks:
        tall = jnp.concatenate([block[:, c * LANES : (c + 1) * LANES] for c in range(chunks)], axis=0)
        turned = jnp.concatenate([tall[:, half:], tall[:, :half]], axis=1)
        stacked.append(jnp.concatenate([tall, turned], axis=0))
    stacked = jnp.concatenate(stacked, axis=1)
    tall = jnp.dot(left_ref[...], stacked, preferred_element_type=F32)
    quarter = tall.shape[0] // 4
    parts = [tall[s * quarter : (s + 1) * quarter] + tall[(2 + s) * quarter : (3 + s) * quarter] for s in range(2)]
    lane = lax.broadcasted_iota(jnp.int32, parts[0].shape, 1) % LANES
    high, low = split_bf16(jnp.where(lane < half, parts[0], parts[1]))
    done = jnp.dot(
        jnp.concatenate([high, high, low], axis=1), right_ref[...], preferred_element_type=F32
    ).astype(BF16)
    for side in range(2):
        for c in range(chunks):
            prep_ref[side, :, c * LANES : (c + 1) * LANES] = done[
                c * QBLK : (c + 1) * QBLK, side * LANES : (side + 1) * LANES
            ]


def first_kernel(rows, width, factors_ref, far_ref, swap_ref, left_ref, right_ref, prep_ref):
    make_factors(rows, width, factors_ref, left_ref, right_ref)
    prepare((far_ref[...], swap_ref[QBLK:]), left_ref, right_ref, prep_ref)


def self_kernel(left_ref, right_ref, self_ref, swap_ref, prep_ref):
    prepare((self_ref[...], swap_ref[:QBLK]), left_ref, right_ref, prep_ref)


def near_kernel(left_ref, right_ref, done_ref, *refs):
    prep_ref = refs[-1]
    done = done_ref.shape[0]
    prep_ref[:done] = done_ref[...]
    blocks = [ref[:QBLK] for ref in refs[:-1]]
    for index in range(0, len(blocks), 2):
        prepare(blocks[index : index + 2], left_ref, right_ref, prep_ref.at[pl.ds(done + index, 2)])


def last_kernel(order, layer, held, slots, pairs_ref, late_ref, early_ref, train_ref, *refs):
    outs, rows_ref = refs[:-1], refs[-1]
    chips = len(order)
    ready = early_ref.shape[0]
    me = lax.axis_index("ex")
    wanted = [pairs_ref[me * slots + slot] for slot in range(slots)]
    for slot, q in enumerate(wanted):
        source = jnp.maximum(q, 0) // held
        step = (ring_place(me >> 1, chips) - ring_place(source >> 1, chips)) & (chips - 1)
        side = (source ^ me) & 1
        place = jnp.where(step == order[-1], ready, 0) + side
        for index, taken in enumerate(order[1:-1]):
            place = jnp.where(step == taken, 2 + side * (chips - 2) + index, place)

        @pl.when(place < ready)
        def _():
            rows_ref[slot * QBLK : (slot + 1) * QBLK, :] = early_ref[jnp.minimum(place, ready - 1)]

        @pl.when(place >= ready)
        def _():
            rows_ref[slot * QBLK : (slot + 1) * QBLK, :] = late_ref[jnp.maximum(place - ready, 0)]

    tile = lax.dot_general(
        rows_ref[...], train_ref[...], (((1,), (1,)), ((), ())), preferred_element_type=F32
    )
    rows = QBLK // layer
    chosen = []
    for slot, q in enumerate(wanted):
        value = tile[slot * QBLK : (slot + 1) * QBLK]
        chosen.append(jnp.where(q >= 0, value, jnp.zeros_like(value)))
    for m in range(layer):
        part = jnp.concatenate([value[m * rows : (m + 1) * rows] for value in chosen], axis=0)
        outs[m][...] = part.astype(outs[m].dtype)


def finish_kernel(layer, *refs):
    parts, out_ref = refs[:layer], refs[layer]
    total = parts[0][...]
    for part in parts[1:]:
        total = total + part[...].astype(F32)
    rows = out_ref.shape[1]
    for slot in range(out_ref.shape[0]):
        out_ref[slot] = total[slot * rows : (slot + 1) * rows]


def shards(train_grads, query_grads, in_precond, out_precond, pair_blocks):
    ex = lax.axis_size("ex")
    layer = lax.axis_size("layer")
    train_rows, layers, features = train_grads.shape
    assert layers == 1
    held = query_grads.shape[0] // QBLK
    slots = pair_blocks.shape[0] // ex
    rows = QBLK // layer
    train = train_grads.reshape(train_rows, features)
    query = query_grads.reshape(query_grads.shape[0], features)
    in_factor = in_precond.reshape(in_precond.shape[1:])
    out_factor = out_precond.reshape(out_precond.shape[1:])
    limit = pltpu.CompilerParams(vmem_limit_bytes=24 * 2**20)

    groups = ex // 2
    order = sorted(range(groups), key=lambda step: min(step, groups - step))

    def pass_on(array, step, flip=0):
        ring = [ring_chip(place) for place in range(groups)]
        moves = zip(ring, ring[step:] + ring[:step])
        return lax.ppermute(array, "ex", [(2 * a + c, 2 * b + (c ^ flip)) for a, b in moves for c in range(2)])

    one = jax.ShapeDtypeStruct((QBLK, features), BF16)
    two = jax.ShapeDtypeStruct((2 * QBLK, features), BF16)
    self_block, far_block, swap, *near = pl.pallas_call(
        functools.partial(pick_kernel, ex, held, slots, order),
        out_shape=[one, one, two] + [two] * (groups - 2),
        in_specs=[SMEM, VMEM],
        out_specs=[VMEM] * (groups + 1),
        compiler_params=limit,
        name="pick",
    )(pair_blocks, query)
    raw = [pass_on(array, step) for array, step in zip(near, order[1:])]
    swap = pass_on(swap, 0, 1)

    brief = pl.CostEstimate(flops=1000, bytes_accessed=1000, transcendentals=0)
    stack = features // LANES * QBLK
    span = 2 * LANES
    out_factor, in_factor, far_pick = lax.optimization_barrier((out_factor, in_factor, far_block))
    left, right, far = pl.pallas_call(
        functools.partial(first_kernel, rows, out_precond.shape[-1]),
        out_shape=[
            jax.ShapeDtypeStruct((4 * stack, 2 * stack), BF16),
            jax.ShapeDtypeStruct((3 * span, span), BF16),
            jax.ShapeDtypeStruct((2, QBLK, features), BF16),
        ],
        in_specs=[VMEM] * 3,
        out_specs=[VMEM] * 3,
        compiler_params=limit,
        name="first",
        cost_estimate=brief,
    )(jnp.concatenate([out_factor, in_factor], axis=0), far_pick, swap)
    far = pass_on(far, order[-1])

    def prepared(count):
        return jax.ShapeDtypeStruct((count, QBLK, features), BF16)

    early = pl.pallas_call(
        self_kernel,
        out_shape=prepared(2),
        in_specs=[VMEM] * 4,
        out_specs=VMEM,
        compiler_params=limit,
        name="self",
        cost_estimate=brief,
    )(left, right, self_block, swap)
    _, *ready = lax.optimization_barrier((early, *raw))
    crossed = pl.pallas_call(
        cross_kernel,
        out_shape=[one] * len(raw),
        in_specs=[VMEM] * len(raw),
        out_specs=[VMEM] * len(raw),
        compiler_params=limit,
        name="cross",
    )(*ready)
    crossed = [pass_on(array, 0, 1) for array in crossed]
    for name, blocks in (("near", raw), ("crossed", crossed)):
        early = pl.pallas_call(
            near_kernel,
            out_shape=prepared(early.shape[0] + len(raw)),
            in_specs=[VMEM] * (3 + len(blocks)),
            out_specs=VMEM,
            compiler_params=limit,
            name=name,
            cost_estimate=brief,
        )(left, right, early, *blocks)
    parts = pl.pallas_call(
        functools.partial(last_kernel, order, layer, held, slots),
        out_shape=[jax.ShapeDtypeStruct((slots * rows, train_rows), F32)]
        + [jax.ShapeDtypeStruct((slots * rows, train_rows), BF16)] * (layer - 1),
        in_specs=[SMEM] + [VMEM] * 3,
        out_specs=[VMEM] * layer,
        scratch_shapes=[pltpu.VMEM((slots * QBLK, features), BF16)],
        compiler_params=limit,
        name="last",
    )(pair_blocks, far, early, train)

    terms = [parts[0]] + [
        lax.ppermute(parts[m], "layer", [(i, (i + m) % layer) for i in range(layer)]) for m in range(1, layer)
    ]
    out = pl.pallas_call(
        functools.partial(finish_kernel, layer),
        out_shape=jax.ShapeDtypeStruct((slots, rows, train_rows), F32),
        in_specs=[VMEM] * layer,
        out_specs=VMEM,
        compiler_params=limit,
        name="finish",
    )(*terms)
    return jnp.transpose(out, (1, 0, 2))


def solution(mesh):
    in_specs = (
        P("ex", "layer", None),
        P("ex", "layer", None),
        P("layer", None, None),
        P("layer", None, None),
        P(),
    )
    out_specs = P("layer", "ex", None)
    return jax.shard_map(shards, mesh=mesh, in_specs=in_specs, out_specs=out_specs, check_vma=False)
```

```python
import functools

import jax
import jax.numpy as jnp
from jax import lax
from jax.experimental import pallas as pl
from jax.experimental.pallas import tpu as pltpu
from jax.sharding import PartitionSpec as P

QBLK = 16
LANES = 128
F32 = jnp.float32
BF16 = jnp.bfloat16

VMEM = pl.BlockSpec(memory_space=pltpu.VMEM)
SMEM = pl.BlockSpec(memory_space=pltpu.SMEM)


def split_bf16(x):
    high = x.astype(BF16)
    return high, (x - high.astype(F32)).astype(BF16)


def over_slots(slots, body, init):
    if slots > 8:
        return lax.fori_loop(0, slots, body, init)
    for slot in range(slots):
        init = body(slot, init)
    return init


def ring_chip(place):
    return place ^ (place >> 1)


def ring_place(chip, chips):
    place, shift = chip, 1
    while shift < chips:
        place, shift = place ^ (place >> shift), 2 * shift
    return place


def pick_kernel(ex, held, slots, order, pairs_ref, query_ref, self_ref, far_ref, swap_ref, *near_refs):
    me = lax.axis_index("ex")
    chips = ex // 2
    place = ring_place(me >> 1, chips)
    targets = [self_ref, swap_ref.at[pl.ds(0, QBLK)]]
    for ref in near_refs:
        targets += [ref.at[pl.ds(0, QBLK)], ref.at[pl.ds(QBLK, QBLK)]]
    targets += [far_ref, swap_ref.at[pl.ds(QBLK, QBLK)]]
    for index, out_ref in enumerate(targets):
        target = 2 * ring_chip((place + order[index // 2]) & (chips - 1)) + ((me & 1) ^ (index % 2))

        def body(slot, block):
            local = pairs_ref[target * slots + slot] - me * held
            return jnp.where((local >= 0) & (local < held), local, block)

        block = over_slots(slots, body, jnp.int32(0))
        out_ref[...] = query_ref[pl.ds(pl.multiple_of(block * QBLK, QBLK), QBLK), :]


def cross_kernel(*refs):
    count = len(refs) // 2
    for ref, out_ref in zip(refs[:count], refs[count:]):
        out_ref[...] = ref[QBLK:]


def make_factors(rows, width, factors_ref, left_ref, right_ref):
    in_width = factors_ref.shape[0] - width
    half = left_ref.shape[1] // 2
    span = right_ref.shape[1]
    outs = split_bf16(factors_ref[:width])
    ins = split_bf16(factors_ref[width:])
    row = lax.broadcasted_iota(jnp.int32, (half // QBLK, width), 0)
    row_o = lax.broadcasted_iota(jnp.int32, (half // QBLK, width), 1)
    col = lax.broadcasted_iota(jnp.int32, (width, half), 1) // QBLK
    col_o = lax.broadcasted_iota(jnp.int32, (width, half), 0)
    a = lax.broadcasted_iota(jnp.int32, (half, half), 1) - lax.broadcasted_iota(jnp.int32, (half, half), 0)
    same = jnp.where((a & (QBLK - 1)) == lax.axis_index("layer") * rows, 1.0, 0.0).astype(BF16)
    for h in range(2):
        for s in range(2):
            pick_rows = (row * 2 + s == row_o).astype(BF16)
            part = jnp.dot(pick_rows, outs[h], preferred_element_type=F32).astype(BF16)
            start = (2 * h + s) * half
            for t in range(2):
                pick_cols = (col * 2 + (s ^ t) == col_o).astype(BF16)
                spread = jnp.dot(part, pick_cols, preferred_element_type=F32).astype(BF16)
                tall = jnp.broadcast_to(spread[:, None, :], (half // QBLK, QBLK, half)).reshape(half, half)
                left_ref[start : start + half, t * half : (t + 1) * half] = tall * same
    up = (
        lax.broadcasted_iota(jnp.int32, (span, in_width), 0) % in_width
        == lax.broadcasted_iota(jnp.int32, (span, in_width), 1)
    ).astype(BF16)
    down = (
        lax.broadcasted_iota(jnp.int32, (in_width, span), 1) % in_width
        == lax.broadcasted_iota(jnp.int32, (in_width, span), 0)
    ).astype(BF16)
    block = (lax.broadcasted_iota(jnp.int32, (span, span), 0) // in_width) == (
        lax.broadcasted_iota(jnp.int32, (span, span), 1) // in_width
    )
    for h in range(2):
        wide = jnp.dot(
            jnp.dot(up, ins[h], preferred_element_type=F32).astype(BF16), down, preferred_element_type=F32
        )
        wide = jnp.where(block, wide, 0.0).astype(BF16)
        right_ref[h * span : (h + 1) * span] = wide
        if h == 0:
            right_ref[2 * span :] = wide


def prepare(blocks, left_ref, right_ref, prep_ref):
    chunks = blocks[0].shape[1] // LANES
    half = LANES // 2
    stacked = []
    for block in blocks:
        tall = jnp.concatenate([block[:, c * LANES : (c + 1) * LANES] for c in range(chunks)], axis=0)
        turned = jnp.concatenate([tall[:, half:], tall[:, :half]], axis=1)
        stacked.append(jnp.concatenate([tall, turned], axis=0))
    stacked = jnp.concatenate(stacked, axis=1)
    tall = jnp.dot(left_ref[...], stacked, preferred_element_type=F32)
    quarter = tall.shape[0] // 4
    parts = [tall[s * quarter : (s + 1) * quarter] + tall[(2 + s) * quarter : (3 + s) * quarter] for s in range(2)]
    lane = lax.broadcasted_iota(jnp.int32, parts[0].shape, 1) % LANES
    high, low = split_bf16(jnp.where(lane < half, parts[0], parts[1]))
    done = jnp.dot(
        jnp.concatenate([high, high, low], axis=1), right_ref[...], preferred_element_type=F32
    ).astype(BF16)
    for side in range(2):
        for c in range(chunks):
            prep_ref[side, :, c * LANES : (c + 1) * LANES] = done[
                c * QBLK : (c + 1) * QBLK, side * LANES : (side + 1) * LANES
            ]


def first_kernel(rows, width, factors_ref, far_ref, swap_ref, left_ref, right_ref, prep_ref):
    make_factors(rows, width, factors_ref, left_ref, right_ref)
    prepare((far_ref[...], swap_ref[QBLK:]), left_ref, right_ref, prep_ref)


def self_kernel(left_ref, right_ref, self_ref, swap_ref, prep_ref):
    prepare((self_ref[...], swap_ref[:QBLK]), left_ref, right_ref, prep_ref)


def near_kernel(left_ref, right_ref, done_ref, *refs):
    prep_ref = refs[-1]
    done = done_ref.shape[0]
    prep_ref[:done] = done_ref[...]
    blocks = [ref[:QBLK] for ref in refs[:-1]]
    for index in range(0, len(blocks), 2):
        prepare(blocks[index : index + 2], left_ref, right_ref, prep_ref.at[pl.ds(done + index, 2)])


def last_kernel(order, layer, held, slots, pairs_ref, late_ref, early_ref, train_ref, *refs):
    outs, rows_ref = refs[:-1], refs[-1]
    chips = len(order)
    ready = early_ref.shape[0]
    me = lax.axis_index("ex")
    wanted = [pairs_ref[me * slots + slot] for slot in range(slots)]
    for slot, q in enumerate(wanted):
        source = jnp.maximum(q, 0) // held
        step = (ring_place(me >> 1, chips) - ring_place(source >> 1, chips)) & (chips - 1)
        side = (source ^ me) & 1
        place = jnp.where(step == order[-1], ready, 0) + side
        for index, taken in enumerate(order[1:-1]):
            place = jnp.where(step == taken, 2 + side * (chips - 2) + index, place)

        @pl.when(place < ready)
        def _():
            rows_ref[slot * QBLK : (slot + 1) * QBLK, :] = early_ref[jnp.minimum(place, ready - 1)]

        @pl.when(place >= ready)
        def _():
            rows_ref[slot * QBLK : (slot + 1) * QBLK, :] = late_ref[jnp.maximum(place - ready, 0)]

    tile = lax.dot_general(
        train_ref[...], rows_ref[...], (((1,), (1,)), ((), ())), preferred_element_type=F32
    ).T
    rows = QBLK // layer
    chosen = []
    for slot, q in enumerate(wanted):
        value = tile[slot * QBLK : (slot + 1) * QBLK]
        chosen.append(jnp.where(q >= 0, value, jnp.zeros_like(value)))
    for m in range(layer):
        part = jnp.concatenate([value[m * rows : (m + 1) * rows] for value in chosen], axis=0)
        outs[m][...] = part.astype(outs[m].dtype)


def finish_kernel(layer, *refs):
    parts, out_ref = refs[:layer], refs[layer]
    total = parts[0][...]
    for part in parts[1:]:
        total = total + part[...].astype(F32)
    rows = out_ref.shape[1]
    for slot in range(out_ref.shape[0]):
        out_ref[slot] = total[slot * rows : (slot + 1) * rows]


def shards(train_grads, query_grads, in_precond, out_precond, pair_blocks):
    ex = lax.axis_size("ex")
    layer = lax.axis_size("layer")
    train_rows, layers, features = train_grads.shape
    assert layers == 1
    held = query_grads.shape[0] // QBLK
    slots = pair_blocks.shape[0] // ex
    rows = QBLK // layer
    train = train_grads.reshape(train_rows, features)
    query = query_grads.reshape(query_grads.shape[0], features)
    in_factor = in_precond.reshape(in_precond.shape[1:])
    out_factor = out_precond.reshape(out_precond.shape[1:])
    limit = pltpu.CompilerParams(vmem_limit_bytes=24 * 2**20)

    groups = ex // 2
    order = sorted(range(groups), key=lambda step: min(step, groups - step))

    def pass_on(array, step, flip=0):
        ring = [ring_chip(place) for place in range(groups)]
        moves = zip(ring, ring[step:] + ring[:step])
        return lax.ppermute(array, "ex", [(2 * a + c, 2 * b + (c ^ flip)) for a, b in moves for c in range(2)])

    one = jax.ShapeDtypeStruct((QBLK, features), BF16)
    two = jax.ShapeDtypeStruct((2 * QBLK, features), BF16)
    self_block, far_block, swap, *near = pl.pallas_call(
        functools.partial(pick_kernel, ex, held, slots, order),
        out_shape=[one, one, two] + [two] * (groups - 2),
        in_specs=[SMEM, VMEM],
        out_specs=[VMEM] * (groups + 1),
        compiler_params=limit,
        name="pick",
    )(pair_blocks, query)
    raw = [pass_on(array, step) for array, step in zip(near, order[1:])]
    swap = pass_on(swap, 0, 1)

    brief = pl.CostEstimate(flops=1000, bytes_accessed=1000, transcendentals=0)
    stack = features // LANES * QBLK
    span = 2 * LANES
    out_factor, in_factor, far_pick = lax.optimization_barrier((out_factor, in_factor, far_block))
    left, right, far = pl.pallas_call(
        functools.partial(first_kernel, rows, out_precond.shape[-1]),
        out_shape=[
            jax.ShapeDtypeStruct((4 * stack, 2 * stack), BF16),
            jax.ShapeDtypeStruct((3 * span, span), BF16),
            jax.ShapeDtypeStruct((2, QBLK, features), BF16),
        ],
        in_specs=[VMEM] * 3,
        out_specs=[VMEM] * 3,
        compiler_params=limit,
        name="first",
        cost_estimate=brief,
    )(jnp.concatenate([out_factor, in_factor], axis=0), far_pick, swap)
    far = pass_on(far, order[-1])

    def prepared(count):
        return jax.ShapeDtypeStruct((count, QBLK, features), BF16)

    early = pl.pallas_call(
        self_kernel,
        out_shape=prepared(2),
        in_specs=[VMEM] * 4,
        out_specs=VMEM,
        compiler_params=limit,
        name="self",
        cost_estimate=brief,
    )(left, right, self_block, swap)
    _, *ready = lax.optimization_barrier((early, *raw))
    crossed = pl.pallas_call(
        cross_kernel,
        out_shape=[one] * len(raw),
        in_specs=[VMEM] * len(raw),
        out_specs=[VMEM] * len(raw),
        compiler_params=limit,
        name="cross",
    )(*ready)
    crossed = [pass_on(array, 0, 1) for array in crossed]
    for name, blocks in (("near", raw), ("crossed", crossed)):
        early = pl.pallas_call(
            near_kernel,
            out_shape=prepared(early.shape[0] + len(raw)),
            in_specs=[VMEM] * (3 + len(blocks)),
            out_specs=VMEM,
            compiler_params=limit,
            name=name,
            cost_estimate=brief,
        )(left, right, early, *blocks)
    parts = pl.pallas_call(
        functools.partial(last_kernel, order, layer, held, slots),
        out_shape=[jax.ShapeDtypeStruct((slots * rows, train_rows), F32)]
        + [jax.ShapeDtypeStruct((slots * rows, train_rows), BF16)] * (layer - 1),
        in_specs=[SMEM] + [VMEM] * 3,
        out_specs=[VMEM] * layer,
        scratch_shapes=[pltpu.VMEM((slots * QBLK, features), BF16)],
        compiler_params=limit,
        name="last",
    )(pair_blocks, far, early, train)

    terms = [parts[0]] + [
        lax.ppermute(parts[m], "layer", [(i, (i + m) % layer) for i in range(layer)]) for m in range(1, layer)
    ]
    out = pl.pallas_call(
        functools.partial(finish_kernel, layer),
        out_shape=jax.ShapeDtypeStruct((slots, rows, train_rows), F32),
        in_specs=[VMEM] * layer,
        out_specs=VMEM,
        compiler_params=limit,
        name="finish",
    )(*terms)
    return jnp.transpose(out, (1, 0, 2))


def solution(mesh):
    in_specs = (
        P("ex", "layer", None),
        P("ex", "layer", None),
        P("layer", None, None),
        P("layer", None, None),
        P(),
    )
    out_specs = P("layer", "ex", None)
    return jax.shard_map(shards, mesh=mesh, in_specs=in_specs, out_specs=out_specs, check_vma=False)
```

```python
import functools

import jax
import jax.numpy as jnp
from jax import lax
from jax.experimental import pallas as pl
from jax.experimental.pallas import tpu as pltpu
from jax.sharding import PartitionSpec as P

QBLK = 16
LANES = 128
F32 = jnp.float32
BF16 = jnp.bfloat16

VMEM = pl.BlockSpec(memory_space=pltpu.VMEM)
SMEM = pl.BlockSpec(memory_space=pltpu.SMEM)


def split_bf16(x):
    high = x.astype(BF16)
    return high, (x - high.astype(F32)).astype(BF16)


def over_slots(slots, body, init):
    if slots > 8:
        return lax.fori_loop(0, slots, body, init)
    for slot in range(slots):
        init = body(slot, init)
    return init


def ring_chip(place):
    return place ^ (place >> 1)


def ring_place(chip, chips):
    place, shift = chip, 1
    while shift < chips:
        place, shift = place ^ (place >> shift), 2 * shift
    return place


def pick_kernel(ex, held, slots, order, pairs_ref, query_ref, self_ref, far_ref, swap_ref, *near_refs):
    me = lax.axis_index("ex")
    chips = ex // 2
    place = ring_place(me >> 1, chips)
    targets = [self_ref, swap_ref.at[pl.ds(0, QBLK)]]
    for ref in near_refs:
        targets += [ref.at[pl.ds(0, QBLK)], ref.at[pl.ds(QBLK, QBLK)]]
    targets += [far_ref, swap_ref.at[pl.ds(QBLK, QBLK)]]
    for index, out_ref in enumerate(targets):
        target = 2 * ring_chip((place + order[index // 2]) & (chips - 1)) + ((me & 1) ^ (index % 2))

        def body(slot, block):
            local = pairs_ref[target * slots + slot] - me * held
            return jnp.where((local >= 0) & (local < held), local, block)

        block = over_slots(slots, body, jnp.int32(0))
        out_ref[...] = query_ref[pl.ds(pl.multiple_of(block * QBLK, QBLK), QBLK), :]


def cross_kernel(*refs):
    count = len(refs) // 2
    for ref, out_ref in zip(refs[:count], refs[count:]):
        out_ref[...] = ref[QBLK:]


def make_factors(rows, width, factors_ref, left_ref, right_ref):
    in_width = factors_ref.shape[0] - width
    half = left_ref.shape[1] // 2
    span = right_ref.shape[1]
    outs = split_bf16(factors_ref[:width])
    ins = split_bf16(factors_ref[width:])
    row = lax.broadcasted_iota(jnp.int32, (half // QBLK, width), 0)
    row_o = lax.broadcasted_iota(jnp.int32, (half // QBLK, width), 1)
    col = lax.broadcasted_iota(jnp.int32, (width, half), 1) // QBLK
    col_o = lax.broadcasted_iota(jnp.int32, (width, half), 0)
    a = lax.broadcasted_iota(jnp.int32, (half, half), 1) - lax.broadcasted_iota(jnp.int32, (half, half), 0)
    same = (a & (QBLK - 1)) == lax.axis_index("layer") * rows
    for h in range(2):
        for s in range(2):
            pick_rows = (row * 2 + s == row_o).astype(BF16)
            part = jnp.dot(pick_rows, outs[h], preferred_element_type=F32).astype(BF16)
            start = (2 * h + s) * half
            for t in range(2):
                pick_cols = (col * 2 + (s ^ t) == col_o).astype(BF16)
                spread = jnp.dot(part, pick_cols, preferred_element_type=F32)
                tall = jnp.broadcast_to(spread[:, None, :], (half // QBLK, QBLK, half)).reshape(half, half)
                left_ref[start : start + half, t * half : (t + 1) * half] = jnp.where(same, tall, 0.0).astype(BF16)
    up = (
        lax.broadcasted_iota(jnp.int32, (span, in_width), 0) % in_width
        == lax.broadcasted_iota(jnp.int32, (span, in_width), 1)
    ).astype(BF16)
    down = (
        lax.broadcasted_iota(jnp.int32, (in_width, span), 1) % in_width
        == lax.broadcasted_iota(jnp.int32, (in_width, span), 0)
    ).astype(BF16)
    block = (lax.broadcasted_iota(jnp.int32, (span, span), 0) // in_width) == (
        lax.broadcasted_iota(jnp.int32, (span, span), 1) // in_width
    )
    for h in range(2):
        wide = jnp.dot(
            jnp.dot(up, ins[h], preferred_element_type=F32).astype(BF16), down, preferred_element_type=F32
        )
        wide = jnp.where(block, wide, 0.0).astype(BF16)
        right_ref[h * span : (h + 1) * span] = wide
        if h == 0:
            right_ref[2 * span :] = wide


def prepare(blocks, left_ref, right_ref, prep_ref):
    chunks = blocks[0].shape[1] // LANES
    half = LANES // 2
    stacked = []
    for block in blocks:
        tall = jnp.concatenate([block[:, c * LANES : (c + 1) * LANES] for c in range(chunks)], axis=0)
        turned = jnp.concatenate([tall[:, half:], tall[:, :half]], axis=1)
        stacked.append(jnp.concatenate([tall, turned], axis=0))
    stacked = jnp.concatenate(stacked, axis=1)
    tall = jnp.dot(left_ref[...], stacked, preferred_element_type=F32)
    quarter = tall.shape[0] // 4
    parts = [tall[s * quarter : (s + 1) * quarter] + tall[(2 + s) * quarter : (3 + s) * quarter] for s in range(2)]
    lane = lax.broadcasted_iota(jnp.int32, parts[0].shape, 1) % LANES
    high, low = split_bf16(jnp.where(lane < half, parts[0], parts[1]))
    done = jnp.dot(
        jnp.concatenate([high, high, low], axis=1), right_ref[...], preferred_element_type=F32
    ).astype(BF16)
    for side in range(2):
        for c in range(chunks):
            prep_ref[side, :, c * LANES : (c + 1) * LANES] = done[
                c * QBLK : (c + 1) * QBLK, side * LANES : (side + 1) * LANES
            ]


def first_kernel(rows, width, factors_ref, far_ref, swap_ref, left_ref, right_ref, prep_ref):
    make_factors(rows, width, factors_ref, left_ref, right_ref)
    prepare((far_ref[...], swap_ref[QBLK:]), left_ref, right_ref, prep_ref)


def self_kernel(left_ref, right_ref, self_ref, swap_ref, prep_ref):
    prepare((self_ref[...], swap_ref[:QBLK]), left_ref, right_ref, prep_ref)


def near_kernel(left_ref, right_ref, done_ref, *refs):
    prep_ref = refs[-1]
    done = done_ref.shape[0]
    prep_ref[:done] = done_ref[...]
    blocks = [ref[:QBLK] for ref in refs[:-1]]
    for index in range(0, len(blocks), 2):
        prepare(blocks[index : index + 2], left_ref, right_ref, prep_ref.at[pl.ds(done + index, 2)])


def last_kernel(order, layer, held, slots, pairs_ref, late_ref, early_ref, train_ref, *refs):
    outs, rows_ref = refs[:-1], refs[-1]
    chips = len(order)
    ready = early_ref.shape[0]
    me = lax.axis_index("ex")
    wanted = [pairs_ref[me * slots + slot] for slot in range(slots)]
    for slot, q in enumerate(wanted):
        source = jnp.maximum(q, 0) // held
        step = (ring_place(me >> 1, chips) - ring_place(source >> 1, chips)) & (chips - 1)
        side = (source ^ me) & 1
        place = jnp.where(step == order[-1], ready, 0) + side
        for index, taken in enumerate(order[1:-1]):
            place = jnp.where(step == taken, 2 + side * (chips - 2) + index, place)

        @pl.when(place < ready)
        def _():
            rows_ref[slot * QBLK : (slot + 1) * QBLK, :] = early_ref[jnp.minimum(place, ready - 1)]

        @pl.when(place >= ready)
        def _():
            rows_ref[slot * QBLK : (slot + 1) * QBLK, :] = late_ref[jnp.maximum(place - ready, 0)]

    tile = lax.dot_general(
        train_ref[...], rows_ref[...], (((1,), (1,)), ((), ())), preferred_element_type=F32
    ).T
    rows = QBLK // layer
    chosen = []
    for slot, q in enumerate(wanted):
        value = tile[slot * QBLK : (slot + 1) * QBLK]
        chosen.append(jnp.where(q >= 0, value, jnp.zeros_like(value)))
    for m in range(layer):
        part = jnp.concatenate([value[m * rows : (m + 1) * rows] for value in chosen], axis=0)
        outs[m][...] = part.astype(outs[m].dtype)


def finish_kernel(layer, *refs):
    parts, out_ref = refs[:layer], refs[layer]
    total = parts[0][...]
    for part in parts[1:]:
        total = total + part[...].astype(F32)
    rows = out_ref.shape[1]
    for slot in range(out_ref.shape[0]):
        out_ref[slot] = total[slot * rows : (slot + 1) * rows]


def shards(train_grads, query_grads, in_precond, out_precond, pair_blocks):
    ex = lax.axis_size("ex")
    layer = lax.axis_size("layer")
    train_rows, layers, features = train_grads.shape
    assert layers == 1
    held = query_grads.shape[0] // QBLK
    slots = pair_blocks.shape[0] // ex
    rows = QBLK // layer
    train = train_grads.reshape(train_rows, features)
    query = query_grads.reshape(query_grads.shape[0], features)
    in_factor = in_precond.reshape(in_precond.shape[1:])
    out_factor = out_precond.reshape(out_precond.shape[1:])
    limit = pltpu.CompilerParams(vmem_limit_bytes=24 * 2**20)

    groups = ex // 2
    order = sorted(range(groups), key=lambda step: min(step, groups - step))

    def pass_on(array, step, flip=0):
        ring = [ring_chip(place) for place in range(groups)]
        moves = zip(ring, ring[step:] + ring[:step])
        return lax.ppermute(array, "ex", [(2 * a + c, 2 * b + (c ^ flip)) for a, b in moves for c in range(2)])

    one = jax.ShapeDtypeStruct((QBLK, features), BF16)
    two = jax.ShapeDtypeStruct((2 * QBLK, features), BF16)
    self_block, far_block, swap, *near = pl.pallas_call(
        functools.partial(pick_kernel, ex, held, slots, order),
        out_shape=[one, one, two] + [two] * (groups - 2),
        in_specs=[SMEM, VMEM],
        out_specs=[VMEM] * (groups + 1),
        compiler_params=limit,
        name="pick",
    )(pair_blocks, query)
    raw = [pass_on(array, step) for array, step in zip(near, order[1:])]
    swap = pass_on(swap, 0, 1)

    brief = pl.CostEstimate(flops=1000, bytes_accessed=1000, transcendentals=0)
    stack = features // LANES * QBLK
    span = 2 * LANES
    out_factor, in_factor, far_pick = lax.optimization_barrier((out_factor, in_factor, far_block))
    left, right, far = pl.pallas_call(
        functools.partial(first_kernel, rows, out_precond.shape[-1]),
        out_shape=[
            jax.ShapeDtypeStruct((4 * stack, 2 * stack), BF16),
            jax.ShapeDtypeStruct((3 * span, span), BF16),
            jax.ShapeDtypeStruct((2, QBLK, features), BF16),
        ],
        in_specs=[VMEM] * 3,
        out_specs=[VMEM] * 3,
        compiler_params=limit,
        name="first",
        cost_estimate=brief,
    )(jnp.concatenate([out_factor, in_factor], axis=0), far_pick, swap)
    far = pass_on(far, order[-1])

    def prepared(count):
        return jax.ShapeDtypeStruct((count, QBLK, features), BF16)

    early = pl.pallas_call(
        self_kernel,
        out_shape=prepared(2),
        in_specs=[VMEM] * 4,
        out_specs=VMEM,
        compiler_params=limit,
        name="self",
        cost_estimate=brief,
    )(left, right, self_block, swap)
    _, *ready = lax.optimization_barrier((early, *raw))
    crossed = pl.pallas_call(
        cross_kernel,
        out_shape=[one] * len(raw),
        in_specs=[VMEM] * len(raw),
        out_specs=[VMEM] * len(raw),
        compiler_params=limit,
        name="cross",
    )(*ready)
    crossed = [pass_on(array, 0, 1) for array in crossed]
    for name, blocks in (("near", raw), ("crossed", crossed)):
        early = pl.pallas_call(
            near_kernel,
            out_shape=prepared(early.shape[0] + len(raw)),
            in_specs=[VMEM] * (3 + len(blocks)),
            out_specs=VMEM,
            compiler_params=limit,
            name=name,
            cost_estimate=brief,
        )(left, right, early, *blocks)
    parts = pl.pallas_call(
        functools.partial(last_kernel, order, layer, held, slots),
        out_shape=[jax.ShapeDtypeStruct((slots * rows, train_rows), F32)]
        + [jax.ShapeDtypeStruct((slots * rows, train_rows), BF16)] * (layer - 1),
        in_specs=[SMEM] + [VMEM] * 3,
        out_specs=[VMEM] * layer,
        scratch_shapes=[pltpu.VMEM((slots * QBLK, features), BF16)],
        compiler_params=limit,
        name="last",
    )(pair_blocks, far, early, train)

    shifts = sorted(range(1, layer), key=lambda m: (min(m, layer - m), m))
    terms = [parts[0]] + [
        lax.ppermute(parts[m], "layer", [(i, (i + m) % layer) for i in range(layer)]) for m in shifts
    ]
    out = pl.pallas_call(
        functools.partial(finish_kernel, layer),
        out_shape=jax.ShapeDtypeStruct((slots, rows, train_rows), F32),
        in_specs=[VMEM] * layer,
        out_specs=VMEM,
        compiler_params=limit,
        name="finish",
    )(*terms)
    return jnp.transpose(out, (1, 0, 2))


def solution(mesh):
    in_specs = (
        P("ex", "layer", None),
        P("ex", "layer", None),
        P("layer", None, None),
        P("layer", None, None),
        P(),
    )
    out_specs = P("layer", "ex", None)
    return jax.shard_map(shards, mesh=mesh, in_specs=in_specs, out_specs=out_specs, check_vma=False)
```

```python
import functools

import jax
import jax.numpy as jnp
from jax import lax
from jax.experimental import pallas as pl
from jax.experimental.pallas import tpu as pltpu
from jax.sharding import PartitionSpec as P

QBLK = 16
LANES = 128
F32 = jnp.float32
BF16 = jnp.bfloat16

VMEM = pl.BlockSpec(memory_space=pltpu.VMEM)
SMEM = pl.BlockSpec(memory_space=pltpu.SMEM)


def split_bf16(x):
    high = x.astype(BF16)
    return high, (x - high.astype(F32)).astype(BF16)


def over_slots(slots, body, init):
    if slots > 8:
        return lax.fori_loop(0, slots, body, init)
    for slot in range(slots):
        init = body(slot, init)
    return init


def ring_chip(place):
    return place ^ (place >> 1)


def ring_place(chip, chips):
    place, shift = chip, 1
    while shift < chips:
        place, shift = place ^ (place >> shift), 2 * shift
    return place


def pick_kernel(ex, held, slots, order, pairs_ref, query_ref, self_ref, far_ref, swap_ref, *near_refs):
    me = lax.axis_index("ex")
    chips = ex // 2
    place = ring_place(me >> 1, chips)
    targets = [self_ref, swap_ref.at[pl.ds(0, QBLK)]]
    for ref in near_refs:
        targets += [ref.at[pl.ds(0, QBLK)], ref.at[pl.ds(QBLK, QBLK)]]
    targets += [far_ref, swap_ref.at[pl.ds(QBLK, QBLK)]]
    for index, out_ref in enumerate(targets):
        target = 2 * ring_chip((place + order[index // 2]) & (chips - 1)) + ((me & 1) ^ (index % 2))

        def body(slot, block):
            local = pairs_ref[target * slots + slot] - me * held
            return jnp.where((local >= 0) & (local < held), local, block)

        block = over_slots(slots, body, jnp.int32(0))
        out_ref[...] = query_ref[pl.ds(pl.multiple_of(block * QBLK, QBLK), QBLK), :]


def cross_kernel(*refs):
    count = len(refs) // 2
    for ref, out_ref in zip(refs[:count], refs[count:]):
        out_ref[...] = ref[QBLK:]


def make_factors(rows, out_ref, in_ref, left_ref, right_ref):
    width, in_width = out_ref.shape[0], in_ref.shape[0]
    half = left_ref.shape[1] // 2
    span = right_ref.shape[1]
    outs = split_bf16(out_ref[...])
    ins = split_bf16(in_ref[...])
    row = lax.broadcasted_iota(jnp.int32, (half // QBLK, width), 0)
    row_o = lax.broadcasted_iota(jnp.int32, (half // QBLK, width), 1)
    col = lax.broadcasted_iota(jnp.int32, (width, half), 1) // QBLK
    col_o = lax.broadcasted_iota(jnp.int32, (width, half), 0)
    a = lax.broadcasted_iota(jnp.int32, (half, half), 1) - lax.broadcasted_iota(jnp.int32, (half, half), 0)
    same = (a & (QBLK - 1)) == lax.axis_index("layer") * rows
    for h in range(2):
        for s in range(2):
            pick_rows = (row * 2 + s == row_o).astype(BF16)
            part = jnp.dot(pick_rows, outs[h], preferred_element_type=F32).astype(BF16)
            start = (2 * h + s) * half
            for t in range(2):
                pick_cols = (col * 2 + (s ^ t) == col_o).astype(BF16)
                spread = jnp.dot(part, pick_cols, preferred_element_type=F32)
                tall = jnp.broadcast_to(spread[:, None, :], (half // QBLK, QBLK, half)).reshape(half, half)
                left_ref[start : start + half, t * half : (t + 1) * half] = jnp.where(same, tall, 0.0).astype(BF16)
    up = (
        lax.broadcasted_iota(jnp.int32, (span, in_width), 0) % in_width
        == lax.broadcasted_iota(jnp.int32, (span, in_width), 1)
    ).astype(BF16)
    down = (
        lax.broadcasted_iota(jnp.int32, (in_width, span), 1) % in_width
        == lax.broadcasted_iota(jnp.int32, (in_width, span), 0)
    ).astype(BF16)
    block = (lax.broadcasted_iota(jnp.int32, (span, span), 0) // in_width) == (
        lax.broadcasted_iota(jnp.int32, (span, span), 1) // in_width
    )
    for h in range(2):
        wide = jnp.dot(
            jnp.dot(up, ins[h], preferred_element_type=F32).astype(BF16), down, preferred_element_type=F32
        )
        wide = jnp.where(block, wide, 0.0).astype(BF16)
        right_ref[h * span : (h + 1) * span] = wide
        if h == 0:
            right_ref[2 * span :] = wide


def prepare(blocks, left_ref, right_ref, prep_ref):
    chunks = blocks[0].shape[1] // LANES
    half = LANES // 2
    stacked = []
    for block in blocks:
        tall = jnp.concatenate([block[:, c * LANES : (c + 1) * LANES] for c in range(chunks)], axis=0)
        turned = jnp.concatenate([tall[:, half:], tall[:, :half]], axis=1)
        stacked.append(jnp.concatenate([tall, turned], axis=0))
    stacked = jnp.concatenate(stacked, axis=1)
    tall = jnp.dot(left_ref[...], stacked, preferred_element_type=F32)
    quarter = tall.shape[0] // 4
    parts = [tall[s * quarter : (s + 1) * quarter] + tall[(2 + s) * quarter : (3 + s) * quarter] for s in range(2)]
    lane = lax.broadcasted_iota(jnp.int32, parts[0].shape, 1) % LANES
    high, low = split_bf16(jnp.where(lane < half, parts[0], parts[1]))
    done = jnp.dot(
        jnp.concatenate([high, high, low], axis=1), right_ref[...], preferred_element_type=F32
    ).astype(BF16)
    for side in range(2):
        for c in range(chunks):
            prep_ref[side, :, c * LANES : (c + 1) * LANES] = done[
                c * QBLK : (c + 1) * QBLK, side * LANES : (side + 1) * LANES
            ]


def first_kernel(rows, out_ref, in_ref, far_ref, swap_ref, left_ref, right_ref, prep_ref):
    make_factors(rows, out_ref, in_ref, left_ref, right_ref)
    prepare((far_ref[...], swap_ref[QBLK:]), left_ref, right_ref, prep_ref)


def self_kernel(left_ref, right_ref, self_ref, swap_ref, prep_ref):
    prepare((self_ref[...], swap_ref[:QBLK]), left_ref, right_ref, prep_ref)


def near_kernel(left_ref, right_ref, done_ref, *refs):
    prep_ref = refs[-1]
    done = done_ref.shape[0]
    prep_ref[:done] = done_ref[...]
    blocks = [ref[:QBLK] for ref in refs[:-1]]
    for index in range(0, len(blocks), 2):
        prepare(blocks[index : index + 2], left_ref, right_ref, prep_ref.at[pl.ds(done + index, 2)])


def last_kernel(order, layer, held, slots, pairs_ref, late_ref, early_ref, train_ref, *refs):
    outs, rows_ref = refs[:-1], refs[-1]
    chips = len(order)
    ready = early_ref.shape[0]
    me = lax.axis_index("ex")
    wanted = [pairs_ref[me * slots + slot] for slot in range(slots)]
    for slot, q in enumerate(wanted):
        source = jnp.maximum(q, 0) // held
        step = (ring_place(me >> 1, chips) - ring_place(source >> 1, chips)) & (chips - 1)
        side = (source ^ me) & 1
        place = jnp.where(step == order[-1], ready, 0) + side
        for index, taken in enumerate(order[1:-1]):
            place = jnp.where(step == taken, 2 + side * (chips - 2) + index, place)

        @pl.when(place < ready)
        def _():
            rows_ref[slot * QBLK : (slot + 1) * QBLK, :] = early_ref[jnp.minimum(place, ready - 1)]

        @pl.when(place >= ready)
        def _():
            rows_ref[slot * QBLK : (slot + 1) * QBLK, :] = late_ref[jnp.maximum(place - ready, 0)]

    tile = lax.dot_general(
        train_ref[...], rows_ref[...], (((1,), (1,)), ((), ())), preferred_element_type=F32
    ).T
    rows = QBLK // layer
    chosen = []
    for slot, q in enumerate(wanted):
        value = tile[slot * QBLK : (slot + 1) * QBLK]
        chosen.append(jnp.where(q >= 0, value, jnp.zeros_like(value)))
    for m in range(layer):
        part = jnp.concatenate([value[m * rows : (m + 1) * rows] for value in chosen], axis=0)
        outs[m][...] = part.astype(outs[m].dtype)


def finish_kernel(layer, *refs):
    parts, out_ref = refs[:layer], refs[layer]
    total = parts[0][...]
    for part in parts[1:]:
        total = total + part[...].astype(F32)
    rows = out_ref.shape[1]
    for slot in range(out_ref.shape[0]):
        out_ref[slot] = total[slot * rows : (slot + 1) * rows]


def shards(train_grads, query_grads, in_precond, out_precond, pair_blocks):
    ex = lax.axis_size("ex")
    layer = lax.axis_size("layer")
    train_rows, layers, features = train_grads.shape
    assert layers == 1
    held = query_grads.shape[0] // QBLK
    slots = pair_blocks.shape[0] // ex
    rows = QBLK // layer
    train = train_grads.reshape(train_rows, features)
    query = query_grads.reshape(query_grads.shape[0], features)
    in_factor = in_precond.reshape(in_precond.shape[1:])
    out_factor = out_precond.reshape(out_precond.shape[1:])
    limit = pltpu.CompilerParams(vmem_limit_bytes=24 * 2**20)

    groups = ex // 2
    order = sorted(range(groups), key=lambda step: min(step, groups - step))

    def pass_on(array, step, flip=0):
        ring = [ring_chip(place) for place in range(groups)]
        moves = zip(ring, ring[step:] + ring[:step])
        return lax.ppermute(array, "ex", [(2 * a + c, 2 * b + (c ^ flip)) for a, b in moves for c in range(2)])

    one = jax.ShapeDtypeStruct((QBLK, features), BF16)
    two = jax.ShapeDtypeStruct((2 * QBLK, features), BF16)
    self_block, far_block, swap, *near = pl.pallas_call(
        functools.partial(pick_kernel, ex, held, slots, order),
        out_shape=[one, one, two] + [two] * (groups - 2),
        in_specs=[SMEM, VMEM],
        out_specs=[VMEM] * (groups + 1),
        compiler_params=limit,
        name="pick",
        cost_estimate=pl.CostEstimate(flops=2 * 10**9, bytes_accessed=1000, transcendentals=0),
    )(pair_blocks, query)
    raw = [pass_on(array, step) for array, step in zip(near, order[1:])]
    swap = pass_on(swap, 0, 1)

    brief = pl.CostEstimate(flops=1000, bytes_accessed=1000, transcendentals=0)
    stack = features // LANES * QBLK
    span = 2 * LANES
    left, right, far = pl.pallas_call(
        functools.partial(first_kernel, rows),
        out_shape=[
            jax.ShapeDtypeStruct((4 * stack, 2 * stack), BF16),
            jax.ShapeDtypeStruct((3 * span, span), BF16),
            jax.ShapeDtypeStruct((2, QBLK, features), BF16),
        ],
        in_specs=[VMEM] * 4,
        out_specs=[VMEM] * 3,
        compiler_params=limit,
        name="first",
        cost_estimate=brief,
    )(out_factor, in_factor, far_block, swap)
    far = pass_on(far, order[-1])

    def prepared(count):
        return jax.ShapeDtypeStruct((count, QBLK, features), BF16)

    early = pl.pallas_call(
        self_kernel,
        out_shape=prepared(2),
        in_specs=[VMEM] * 4,
        out_specs=VMEM,
        compiler_params=limit,
        name="self",
        cost_estimate=brief,
    )(left, right, self_block, swap)
    _, *ready = lax.optimization_barrier((early, *raw))
    crossed = pl.pallas_call(
        cross_kernel,
        out_shape=[one] * len(raw),
        in_specs=[VMEM] * len(raw),
        out_specs=[VMEM] * len(raw),
        compiler_params=limit,
        name="cross",
    )(*ready)
    crossed = [pass_on(array, 0, 1) for array in crossed]
    for name, blocks in (("near", raw), ("crossed", crossed)):
        early = pl.pallas_call(
            near_kernel,
            out_shape=prepared(early.shape[0] + len(raw)),
            in_specs=[VMEM] * (3 + len(blocks)),
            out_specs=VMEM,
            compiler_params=limit,
            name=name,
            cost_estimate=brief,
        )(left, right, early, *blocks)
    parts = pl.pallas_call(
        functools.partial(last_kernel, order, layer, held, slots),
        out_shape=[jax.ShapeDtypeStruct((slots * rows, train_rows), F32)]
        + [jax.ShapeDtypeStruct((slots * rows, train_rows), BF16)] * (layer - 1),
        in_specs=[SMEM] + [VMEM] * 3,
        out_specs=[VMEM] * layer,
        scratch_shapes=[pltpu.VMEM((slots * QBLK, features), BF16)],
        compiler_params=limit,
        name="last",
    )(pair_blocks, far, early, train)

    terms = [parts[0]] + [
        lax.ppermute(parts[m], "layer", [(i, (i + m) % layer) for i in range(layer)]) for m in range(1, layer)
    ]
    out = pl.pallas_call(
        functools.partial(finish_kernel, layer),
        out_shape=jax.ShapeDtypeStruct((slots, rows, train_rows), F32),
        in_specs=[VMEM] * layer,
        out_specs=VMEM,
        compiler_params=limit,
        name="finish",
    )(*terms)
    return jnp.transpose(out, (1, 0, 2))


def solution(mesh):
    in_specs = (
        P("ex", "layer", None),
        P("ex", "layer", None),
        P("layer", None, None),
        P("layer", None, None),
        P(),
    )
    out_specs = P("layer", "ex", None)
    return jax.shard_map(shards, mesh=mesh, in_specs=in_specs, out_specs=out_specs, check_vma=False)
```

```python
import functools

import jax
import jax.numpy as jnp
from jax import lax
from jax.experimental import pallas as pl
from jax.experimental.pallas import tpu as pltpu
from jax.sharding import PartitionSpec as P

QBLK = 16
LANES = 128
F32 = jnp.float32
BF16 = jnp.bfloat16

VMEM = pl.BlockSpec(memory_space=pltpu.VMEM)
SMEM = pl.BlockSpec(memory_space=pltpu.SMEM)


def split_bf16(x):
    high = x.astype(BF16)
    return high, (x - high.astype(F32)).astype(BF16)


def over_slots(slots, body, init):
    if slots > 8:
        return lax.fori_loop(0, slots, body, init)
    for slot in range(slots):
        init = body(slot, init)
    return init


def ring_chip(place):
    return place ^ (place >> 1)


def ring_place(chip, chips):
    place, shift = chip, 1
    while shift < chips:
        place, shift = place ^ (place >> shift), 2 * shift
    return place


def pick_kernel(ex, held, slots, order, pairs_ref, query_ref, self_ref, far_ref, swap_ref, *near_refs):
    me = lax.axis_index("ex")
    chips = ex // 2
    place = ring_place(me >> 1, chips)
    targets = [self_ref, swap_ref.at[pl.ds(0, QBLK)]]
    for ref in near_refs:
        targets += [ref.at[pl.ds(0, QBLK)], ref.at[pl.ds(QBLK, QBLK)]]
    targets += [far_ref, swap_ref.at[pl.ds(QBLK, QBLK)]]
    for index, out_ref in enumerate(targets):
        target = 2 * ring_chip((place + order[index // 2]) & (chips - 1)) + ((me & 1) ^ (index % 2))

        def body(slot, block):
            local = pairs_ref[target * slots + slot] - me * held
            return jnp.where((local >= 0) & (local < held), local, block)

        block = over_slots(slots, body, jnp.int32(0))
        out_ref[...] = query_ref[pl.ds(pl.multiple_of(block * QBLK, QBLK), QBLK), :]


def cross_kernel(*refs):
    count = len(refs) // 2
    for ref, out_ref in zip(refs[:count], refs[count:]):
        out_ref[...] = ref[QBLK:]


def make_factors(rows, out_ref, in_ref, left_ref, right_ref):
    width, in_width = out_ref.shape[0], in_ref.shape[0]
    half = left_ref.shape[0] // 2
    span = right_ref.shape[1]
    outs = split_bf16(out_ref[...])
    ins = split_bf16(in_ref[...])
    row = lax.broadcasted_iota(jnp.int32, (half // QBLK, width), 0)
    row_o = lax.broadcasted_iota(jnp.int32, (half // QBLK, width), 1)
    col = lax.broadcasted_iota(jnp.int32, (width, half), 1) // QBLK
    col_o = lax.broadcasted_iota(jnp.int32, (width, half), 0)
    a = lax.broadcasted_iota(jnp.int32, (half, half), 1) - lax.broadcasted_iota(jnp.int32, (half, half), 0)
    same = (a & (QBLK - 1)) == lax.axis_index("layer") * rows
    for h in range(2):
        for s in range(2):
            pick_rows = (row * 2 + s == row_o).astype(BF16)
            part = jnp.dot(pick_rows, outs[h], preferred_element_type=F32).astype(BF16)
            for t in range(2):
                pick_cols = (col * 2 + t == col_o).astype(BF16)
                spread = jnp.dot(part, pick_cols, preferred_element_type=F32)
                tall = jnp.broadcast_to(spread[:, None, :], (half // QBLK, QBLK, half)).reshape(half, half)
                start = (2 * h + t) * half
                left_ref[s * half : (s + 1) * half, start : start + half] = jnp.where(same, tall, 0.0).astype(BF16)
    up = (
        lax.broadcasted_iota(jnp.int32, (span, in_width), 0) % in_width
        == lax.broadcasted_iota(jnp.int32, (span, in_width), 1)
    ).astype(BF16)
    down = (
        lax.broadcasted_iota(jnp.int32, (in_width, span), 1) % in_width
        == lax.broadcasted_iota(jnp.int32, (in_width, span), 0)
    ).astype(BF16)
    block = (lax.broadcasted_iota(jnp.int32, (span, span), 0) // in_width) == (
        lax.broadcasted_iota(jnp.int32, (span, span), 1) // in_width
    )
    for h in range(2):
        wide = jnp.dot(
            jnp.dot(up, ins[h], preferred_element_type=F32).astype(BF16), down, preferred_element_type=F32
        )
        wide = jnp.where(block, wide, 0.0).astype(BF16)
        right_ref[h * span : (h + 1) * span] = wide
        if h == 0:
            right_ref[2 * span :] = wide


def swap_halves(x):
    half = x.shape[1] // 2
    return jnp.concatenate([x[:, half:], x[:, :half]], axis=1)


def prepare(blocks, left_ref, right_ref, targets):
    chunks = blocks[0].shape[1] // LANES
    half = chunks * QBLK
    lower = lax.broadcasted_iota(jnp.int32, (half, LANES), 1) < LANES // 2
    talls = [
        jnp.concatenate([block[:, c * LANES : (c + 1) * LANES] for c in range(chunks)], axis=0) for block in blocks
    ]
    stacked = []
    for one, two in (talls[:2], talls[2:]):
        stacked.append(
            jnp.concatenate(
                [jnp.where(lower, one, swap_halves(two)), jnp.where(lower, swap_halves(one), two)], axis=0
            )
        )
    stacked = jnp.concatenate(stacked, axis=1)
    high, low = split_bf16(
        jnp.dot(left_ref[...], jnp.concatenate([stacked, stacked], axis=0), preferred_element_type=F32)
    )
    done = jnp.dot(
        jnp.concatenate([high, high, low], axis=1), right_ref[...], preferred_element_type=F32
    ).astype(BF16)
    for pair in range(2):
        even = done[:half, pair * LANES : (pair + 1) * LANES]
        odd = done[half:, pair * LANES : (pair + 1) * LANES]
        for value, (ref, index) in zip(
            (jnp.where(lower, even, swap_halves(odd)), jnp.where(lower, swap_halves(even), odd)),
            targets[2 * pair : 2 * pair + 2],
        ):
            for c in range(chunks):
                ref[index, :, c * LANES : (c + 1) * LANES] = value[c * QBLK : (c + 1) * QBLK]


def first_kernel(rows, out_ref, in_ref, own_far_ref, own_ref, swap_ref, left_ref, right_ref, far_ref, self_ref):
    make_factors(rows, out_ref, in_ref, left_ref, right_ref)
    blocks = [own_far_ref[...], swap_ref[QBLK:], own_ref[...], swap_ref[:QBLK]]
    prepare(blocks, left_ref, right_ref, [(far_ref, 0), (far_ref, 1), (self_ref, 0), (self_ref, 1)])


def near_kernel(left_ref, right_ref, self_ref, *refs):
    prep_ref = refs[-1]
    prep_ref[:2] = self_ref[...]
    blocks = [ref[:QBLK] for ref in refs[:-1]]
    targets = [(prep_ref, 2 + index) for index in range(len(blocks))]
    for start in range(0, len(blocks), 4):
        pick = slice(start, start + 4) if start + 4 <= len(blocks) else slice(-2, None)
        times = 1 if start + 4 <= len(blocks) else 2
        prepare(blocks[pick] * times, left_ref, right_ref, targets[pick] * times)


def last_kernel(order, layer, held, slots, pairs_ref, late_ref, early_ref, train_ref, *refs):
    outs, rows_ref = refs[:-1], refs[-1]
    chips = len(order)
    ready = early_ref.shape[0]
    me = lax.axis_index("ex")
    wanted = [pairs_ref[me * slots + slot] for slot in range(slots)]
    for slot, q in enumerate(wanted):
        source = jnp.maximum(q, 0) // held
        step = (ring_place(me >> 1, chips) - ring_place(source >> 1, chips)) & (chips - 1)
        side = (source ^ me) & 1
        place = jnp.where(step == order[-1], ready, 0) + side
        for index, taken in enumerate(order[1:-1]):
            place = jnp.where(step == taken, 2 + side * (chips - 2) + index, place)

        @pl.when(place < ready)
        def _():
            rows_ref[slot * QBLK : (slot + 1) * QBLK, :] = early_ref[jnp.minimum(place, ready - 1)]

        @pl.when(place >= ready)
        def _():
            rows_ref[slot * QBLK : (slot + 1) * QBLK, :] = late_ref[jnp.maximum(place - ready, 0)]

    tile = lax.dot_general(
        train_ref[...], rows_ref[...], (((1,), (1,)), ((), ())), preferred_element_type=F32
    ).T
    rows = QBLK // layer
    chosen = []
    for slot, q in enumerate(wanted):
        value = tile[slot * QBLK : (slot + 1) * QBLK]
        chosen.append(jnp.where(q >= 0, value, jnp.zeros_like(value)))
    for m in range(layer):
        part = jnp.concatenate([value[m * rows : (m + 1) * rows] for value in chosen], axis=0)
        outs[m][...] = part.astype(outs[m].dtype)


def finish_kernel(layer, *refs):
    parts, out_ref = refs[:layer], refs[layer]
    total = parts[0][...]
    for part in parts[1:]:
        total = total + part[...].astype(F32)
    rows = out_ref.shape[1]
    for slot in range(out_ref.shape[0]):
        out_ref[slot] = total[slot * rows : (slot + 1) * rows]


def shards(train_grads, query_grads, in_precond, out_precond, pair_blocks):
    ex = lax.axis_size("ex")
    layer = lax.axis_size("layer")
    train_rows, layers, features = train_grads.shape
    assert layers == 1
    held = query_grads.shape[0] // QBLK
    slots = pair_blocks.shape[0] // ex
    rows = QBLK // layer
    train = train_grads.reshape(train_rows, features)
    query = query_grads.reshape(query_grads.shape[0], features)
    in_factor = in_precond.reshape(in_precond.shape[1:])
    out_factor = out_precond.reshape(out_precond.shape[1:])
    limit = pltpu.CompilerParams(vmem_limit_bytes=24 * 2**20)

    groups = ex // 2
    order = sorted(range(groups), key=lambda step: min(step, groups - step))

    def pass_on(array, step, flip=0):
        ring = [ring_chip(place) for place in range(groups)]
        moves = zip(ring, ring[step:] + ring[:step])
        return lax.ppermute(array, "ex", [(2 * a + c, 2 * b + (c ^ flip)) for a, b in moves for c in range(2)])

    one = jax.ShapeDtypeStruct((QBLK, features), BF16)
    two = jax.ShapeDtypeStruct((2 * QBLK, features), BF16)
    self_block, far_block, swap, *near = pl.pallas_call(
        functools.partial(pick_kernel, ex, held, slots, order),
        out_shape=[one, one, two] + [two] * (groups - 2),
        in_specs=[SMEM, VMEM],
        out_specs=[VMEM] * (groups + 1),
        compiler_params=limit,
        name="pick",
        cost_estimate=pl.CostEstimate(flops=2 * 10**9, bytes_accessed=1000, transcendentals=0),
    )(pair_blocks, query)
    raw = [pass_on(array, step) for array, step in zip(near, order[1:])]
    swap = pass_on(swap, 0, 1)

    brief = pl.CostEstimate(flops=1000, bytes_accessed=1000, transcendentals=0)
    stack = features // LANES * QBLK
    span = 2 * LANES
    def prepared(count):
        return jax.ShapeDtypeStruct((count, QBLK, features), BF16)

    left, right, far, early = pl.pallas_call(
        functools.partial(first_kernel, rows),
        out_shape=[
            jax.ShapeDtypeStruct((2 * stack, 4 * stack), BF16),
            jax.ShapeDtypeStruct((3 * span, span), BF16),
            prepared(2),
            prepared(2),
        ],
        in_specs=[VMEM] * 5,
        out_specs=[VMEM] * 4,
        compiler_params=limit,
        name="first",
        cost_estimate=brief,
    )(out_factor, in_factor, far_block, self_block, swap)
    far = pass_on(far, order[-1])

    _, *ready = lax.optimization_barrier((early, *raw))
    crossed = pl.pallas_call(
        cross_kernel,
        out_shape=[one] * len(raw),
        in_specs=[VMEM] * len(raw),
        out_specs=[VMEM] * len(raw),
        compiler_params=limit,
        name="cross",
    )(*ready)
    crossed = [pass_on(array, 0, 1) for array in crossed]
    early = pl.pallas_call(
        near_kernel,
        out_shape=prepared(ex - 2),
        in_specs=[VMEM] * (3 + 2 * len(raw)),
        out_specs=VMEM,
        compiler_params=limit,
        name="near",
        cost_estimate=brief,
    )(left, right, early, *raw, *crossed)
    parts = pl.pallas_call(
        functools.partial(last_kernel, order, layer, held, slots),
        out_shape=[jax.ShapeDtypeStruct((slots * rows, train_rows), F32)]
        + [jax.ShapeDtypeStruct((slots * rows, train_rows), BF16)] * (layer - 1),
        in_specs=[SMEM] + [VMEM] * 3,
        out_specs=[VMEM] * layer,
        scratch_shapes=[pltpu.VMEM((slots * QBLK, features), BF16)],
        compiler_params=limit,
        name="last",
    )(pair_blocks, far, early, train)

    terms = [parts[0]] + [
        lax.ppermute(parts[m], "layer", [(i, (i + m) % layer) for i in range(layer)]) for m in range(1, layer)
    ]
    out = pl.pallas_call(
        functools.partial(finish_kernel, layer),
        out_shape=jax.ShapeDtypeStruct((slots, rows, train_rows), F32),
        in_specs=[VMEM] * layer,
        out_specs=VMEM,
        compiler_params=limit,
        name="finish",
    )(*terms)
    return jnp.transpose(out, (1, 0, 2))


def solution(mesh):
    in_specs = (
        P("ex", "layer", None),
        P("ex", "layer", None),
        P("layer", None, None),
        P("layer", None, None),
        P(),
    )
    out_specs = P("layer", "ex", None)
    return jax.shard_map(shards, mesh=mesh, in_specs=in_specs, out_specs=out_specs, check_vma=False)
```

```python
import functools

import jax
import jax.numpy as jnp
from jax import lax
from jax.experimental import pallas as pl
from jax.experimental.pallas import tpu as pltpu
from jax.sharding import PartitionSpec as P

QBLK = 16
LANES = 128
F32 = jnp.float32
BF16 = jnp.bfloat16

VMEM = pl.BlockSpec(memory_space=pltpu.VMEM)
SMEM = pl.BlockSpec(memory_space=pltpu.SMEM)


def split_bf16(x):
    high = x.astype(BF16)
    return high, (x - high.astype(F32)).astype(BF16)


def over_slots(slots, body, init):
    if slots > 8:
        return lax.fori_loop(0, slots, body, init)
    for slot in range(slots):
        init = body(slot, init)
    return init


def ring_chip(place):
    return place ^ (place >> 1)


def ring_place(chip, chips):
    place, shift = chip, 1
    while shift < chips:
        place, shift = place ^ (place >> shift), 2 * shift
    return place


def pick_kernel(ex, held, slots, order, pairs_ref, query_ref, self_ref, far_ref, swap_ref, *near_refs):
    me = lax.axis_index("ex")
    chips = ex // 2
    place = ring_place(me >> 1, chips)
    targets = [self_ref, swap_ref.at[pl.ds(0, QBLK)]]
    for ref in near_refs:
        targets += [ref.at[pl.ds(0, QBLK)], ref.at[pl.ds(QBLK, QBLK)]]
    targets += [far_ref, swap_ref.at[pl.ds(QBLK, QBLK)]]
    for index, out_ref in enumerate(targets):
        target = 2 * ring_chip((place + order[index // 2]) & (chips - 1)) + ((me & 1) ^ (index % 2))

        def body(slot, block):
            local = pairs_ref[target * slots + slot] - me * held
            return jnp.where((local >= 0) & (local < held), local, block)

        block = over_slots(slots, body, jnp.int32(0))
        out_ref[...] = query_ref[pl.ds(pl.multiple_of(block * QBLK, QBLK), QBLK), :]


def cross_kernel(*refs):
    count = len(refs) // 2
    for ref, out_ref in zip(refs[:count], refs[count:]):
        out_ref[...] = ref[QBLK:]


def make_factors(rows, out_ref, in_ref, left_ref, right_ref):
    width, in_width = out_ref.shape[0], in_ref.shape[0]
    half = left_ref.shape[1] // 2
    span = right_ref.shape[1]
    outs = split_bf16(out_ref[...])
    ins = split_bf16(in_ref[...])
    row = lax.broadcasted_iota(jnp.int32, (half // QBLK, width), 0)
    row_o = lax.broadcasted_iota(jnp.int32, (half // QBLK, width), 1)
    col = lax.broadcasted_iota(jnp.int32, (width, half), 1) // QBLK
    col_o = lax.broadcasted_iota(jnp.int32, (width, half), 0)
    a = lax.broadcasted_iota(jnp.int32, (half, half), 1) - lax.broadcasted_iota(jnp.int32, (half, half), 0)
    same = (a & (QBLK - 1)) == lax.axis_index("layer") * rows
    for h in range(2):
        for s in range(2):
            pick_rows = (row * 2 + s == row_o).astype(BF16)
            part = jnp.dot(pick_rows, outs[h], preferred_element_type=F32).astype(BF16)
            start = (2 * h + s) * half
            for t in range(2):
                pick_cols = (col * 2 + (s ^ t) == col_o).astype(BF16)
                spread = jnp.dot(part, pick_cols, preferred_element_type=F32)
                tall = jnp.broadcast_to(spread[:, None, :], (half // QBLK, QBLK, half)).reshape(half, half)
                left_ref[start : start + half, t * half : (t + 1) * half] = jnp.where(same, tall, 0.0).astype(BF16)
    up = (
        lax.broadcasted_iota(jnp.int32, (span, in_width), 0) % in_width
        == lax.broadcasted_iota(jnp.int32, (span, in_width), 1)
    ).astype(BF16)
    down = (
        lax.broadcasted_iota(jnp.int32, (in_width, span), 1) % in_width
        == lax.broadcasted_iota(jnp.int32, (in_width, span), 0)
    ).astype(BF16)
    block = (lax.broadcasted_iota(jnp.int32, (span, span), 0) // in_width) == (
        lax.broadcasted_iota(jnp.int32, (span, span), 1) // in_width
    )
    for h in range(2):
        wide = jnp.dot(
            jnp.dot(up, ins[h], preferred_element_type=F32).astype(BF16), down, preferred_element_type=F32
        )
        wide = jnp.where(block, wide, 0.0).astype(BF16)
        right_ref[h * span : (h + 1) * span] = wide
        if h == 0:
            right_ref[2 * span :] = wide


def prepare(blocks, left_ref, right_ref, prep_ref):
    chunks = blocks[0].shape[1] // LANES
    half = LANES // 2
    stacked = []
    for block in blocks:
        tall = jnp.concatenate([block[:, c * LANES : (c + 1) * LANES] for c in range(chunks)], axis=0)
        turned = jnp.concatenate([tall[:, half:], tall[:, :half]], axis=1)
        stacked.append(jnp.concatenate([tall, turned], axis=0))
    stacked = jnp.concatenate(stacked, axis=1)
    tall = jnp.dot(left_ref[...], stacked, preferred_element_type=F32)
    quarter = tall.shape[0] // 4
    parts = [tall[s * quarter : (s + 1) * quarter] + tall[(2 + s) * quarter : (3 + s) * quarter] for s in range(2)]
    lane = lax.broadcasted_iota(jnp.int32, parts[0].shape, 1) % LANES
    high, low = split_bf16(jnp.where(lane < half, parts[0], parts[1]))
    done = jnp.dot(
        jnp.concatenate([high, high, low], axis=1), right_ref[...], preferred_element_type=F32
    ).astype(BF16)
    for side in range(2):
        for c in range(chunks):
            prep_ref[side, :, c * LANES : (c + 1) * LANES] = done[
                c * QBLK : (c + 1) * QBLK, side * LANES : (side + 1) * LANES
            ]


def first_kernel(rows, out_ref, in_ref, far_ref, swap_ref, left_ref, right_ref, prep_ref):
    make_factors(rows, out_ref, in_ref, left_ref, right_ref)
    prepare((far_ref[...], swap_ref[QBLK:]), left_ref, right_ref, prep_ref)


def self_kernel(left_ref, right_ref, self_ref, swap_ref, prep_ref):
    prepare((self_ref[...], swap_ref[:QBLK]), left_ref, right_ref, prep_ref)


def near_kernel(left_ref, right_ref, done_ref, *refs):
    prep_ref = refs[-1]
    done = done_ref.shape[0]
    prep_ref[:done] = done_ref[...]
    blocks = [ref[:QBLK] for ref in refs[:-1]]
    for index in range(0, len(blocks), 2):
        prepare(blocks[index : index + 2], left_ref, right_ref, prep_ref.at[pl.ds(done + index, 2)])


def last_kernel(order, layer, held, slots, pairs_ref, late_ref, early_ref, train_ref, *refs):
    outs, rows_ref = refs[:-1], refs[-1]
    chips = len(order)
    ready = early_ref.shape[0]
    me = lax.axis_index("ex")
    wanted = [pairs_ref[me * slots + slot] for slot in range(slots)]
    for slot, q in enumerate(wanted):
        source = jnp.maximum(q, 0) // held
        step = (ring_place(me >> 1, chips) - ring_place(source >> 1, chips)) & (chips - 1)
        side = (source ^ me) & 1
        place = jnp.where(step == order[-1], ready, 0) + side
        for index, taken in enumerate(order[1:-1]):
            place = jnp.where(step == taken, 2 + side * (chips - 2) + index, place)

        @pl.when(place < ready)
        def _():
            rows_ref[slot * QBLK : (slot + 1) * QBLK, :] = early_ref[jnp.minimum(place, ready - 1)]

        @pl.when(place >= ready)
        def _():
            rows_ref[slot * QBLK : (slot + 1) * QBLK, :] = late_ref[jnp.maximum(place - ready, 0)]

    tile = lax.dot_general(
        train_ref[...], rows_ref[...], (((1,), (1,)), ((), ())), preferred_element_type=F32
    ).T
    rows = QBLK // layer
    chosen = []
    for slot, q in enumerate(wanted):
        value = tile[slot * QBLK : (slot + 1) * QBLK]
        chosen.append(jnp.where(q >= 0, value, jnp.zeros_like(value)))
    for m in range(layer):
        part = jnp.concatenate([value[m * rows : (m + 1) * rows] for value in chosen], axis=0)
        outs[m][...] = part.astype(outs[m].dtype)


def finish_kernel(layer, *refs):
    parts, out_ref = refs[:layer], refs[layer]
    total = parts[0][...]
    for part in parts[1:]:
        total = total + part[...].astype(F32)
    rows = out_ref.shape[1]
    for slot in range(out_ref.shape[0]):
        out_ref[slot] = total[slot * rows : (slot + 1) * rows]


def shards(train_grads, query_grads, in_precond, out_precond, pair_blocks):
    ex = lax.axis_size("ex")
    layer = lax.axis_size("layer")
    train_rows, layers, features = train_grads.shape
    assert layers == 1
    held = query_grads.shape[0] // QBLK
    slots = pair_blocks.shape[0] // ex
    rows = QBLK // layer
    train = train_grads.reshape(train_rows, features)
    query = query_grads.reshape(query_grads.shape[0], features)
    in_factor = in_precond.reshape(in_precond.shape[1:])
    out_factor = out_precond.reshape(out_precond.shape[1:])
    limit = pltpu.CompilerParams(vmem_limit_bytes=24 * 2**20)

    groups = ex // 2
    order = sorted(range(groups), key=lambda step: min(step, groups - step))

    def pass_on(array, step, flip=0):
        ring = [ring_chip(place) for place in range(groups)]
        moves = zip(ring, ring[step:] + ring[:step])
        return lax.ppermute(array, "ex", [(2 * a + c, 2 * b + (c ^ flip)) for a, b in moves for c in range(2)])

    one = jax.ShapeDtypeStruct((QBLK, features), BF16)
    two = jax.ShapeDtypeStruct((2 * QBLK, features), BF16)
    self_block, far_block, swap, *near = pl.pallas_call(
        functools.partial(pick_kernel, ex, held, slots, order),
        out_shape=[one, one, two] + [two] * (groups - 2),
        in_specs=[SMEM, VMEM],
        out_specs=[VMEM] * (groups + 1),
        compiler_params=limit,
        name="pick",
        cost_estimate=pl.CostEstimate(flops=2 * 10**9, bytes_accessed=1000, transcendentals=0),
    )(pair_blocks, query)
    raw = [pass_on(array, step) for array, step in zip(near, order[1:])]
    swap = pass_on(swap, 0, 1)

    brief = pl.CostEstimate(flops=1000, bytes_accessed=1000, transcendentals=0)
    stack = features // LANES * QBLK
    span = 2 * LANES
    left, right, far = pl.pallas_call(
        functools.partial(first_kernel, rows),
        out_shape=[
            jax.ShapeDtypeStruct((4 * stack, 2 * stack), BF16),
            jax.ShapeDtypeStruct((3 * span, span), BF16),
            jax.ShapeDtypeStruct((2, QBLK, features), BF16),
        ],
        in_specs=[VMEM] * 4,
        out_specs=[VMEM] * 3,
        compiler_params=limit,
        name="first",
        cost_estimate=brief,
    )(out_factor, in_factor, far_block, swap)
    far = pass_on(far, order[-1])

    def prepared(count):
        return jax.ShapeDtypeStruct((count, QBLK, features), BF16)

    early = pl.pallas_call(
        self_kernel,
        out_shape=prepared(2),
        in_specs=[VMEM] * 4,
        out_specs=VMEM,
        compiler_params=limit,
        name="self",
        cost_estimate=brief,
    )(left, right, self_block, swap)
    def near_work(name, early, blocks):
        return pl.pallas_call(
            near_kernel,
            out_shape=prepared(early.shape[0] + len(blocks)),
            in_specs=[VMEM] * (3 + len(blocks)),
            out_specs=VMEM,
            compiler_params=limit,
            name=name,
            cost_estimate=brief,
        )(left, right, early, *blocks)

    early = near_work("near", early, raw)
    _, *ready = lax.optimization_barrier((early, *raw))
    crossed = pl.pallas_call(
        cross_kernel,
        out_shape=[one] * len(raw),
        in_specs=[VMEM] * len(raw),
        out_specs=[VMEM] * len(raw),
        compiler_params=limit,
        name="cross",
    )(*ready)
    crossed = [pass_on(array, 0, 1) for array in crossed]
    early = near_work("crossed", early, crossed)
    parts = pl.pallas_call(
        functools.partial(last_kernel, order, layer, held, slots),
        out_shape=[jax.ShapeDtypeStruct((slots * rows, train_rows), F32)]
        + [jax.ShapeDtypeStruct((slots * rows, train_rows), BF16)] * (layer - 1),
        in_specs=[SMEM] + [VMEM] * 3,
        out_specs=[VMEM] * layer,
        scratch_shapes=[pltpu.VMEM((slots * QBLK, features), BF16)],
        compiler_params=limit,
        name="last",
    )(pair_blocks, far, early, train)

    terms = [parts[0]] + [
        lax.ppermute(parts[m], "layer", [(i, (i + m) % layer) for i in range(layer)]) for m in range(1, layer)
    ]
    out = pl.pallas_call(
        functools.partial(finish_kernel, layer),
        out_shape=jax.ShapeDtypeStruct((slots, rows, train_rows), F32),
        in_specs=[VMEM] * layer,
        out_specs=VMEM,
        compiler_params=limit,
        name="finish",
    )(*terms)
    return jnp.transpose(out, (1, 0, 2))


def solution(mesh):
    in_specs = (
        P("ex", "layer", None),
        P("ex", "layer", None),
        P("layer", None, None),
        P("layer", None, None),
        P(),
    )
    out_specs = P("layer", "ex", None)
    return jax.shard_map(shards, mesh=mesh, in_specs=in_specs, out_specs=out_specs, check_vma=False)
```

```python
import functools

import jax
import jax.numpy as jnp
from jax import lax
from jax.experimental import pallas as pl
from jax.experimental.pallas import tpu as pltpu
from jax.sharding import PartitionSpec as P

QBLK = 16
LANES = 128
F32 = jnp.float32
BF16 = jnp.bfloat16

VMEM = pl.BlockSpec(memory_space=pltpu.VMEM)
SMEM = pl.BlockSpec(memory_space=pltpu.SMEM)


def split_bf16(x):
    high = x.astype(BF16)
    return high, (x - high.astype(F32)).astype(BF16)


def over_slots(slots, body, init):
    if slots > 8:
        return lax.fori_loop(0, slots, body, init)
    for slot in range(slots):
        init = body(slot, init)
    return init


def ring_chip(place):
    return place ^ (place >> 1)


def ring_place(chip, chips):
    place, shift = chip, 1
    while shift < chips:
        place, shift = place ^ (place >> shift), 2 * shift
    return place


def pick_kernel(ex, held, slots, order, pairs_ref, query_ref, self_ref, far_ref, swap_ref, *near_refs):
    me = lax.axis_index("ex")
    chips = ex // 2
    place = ring_place(me >> 1, chips)
    targets = [self_ref, swap_ref.at[pl.ds(0, QBLK)]]
    for ref in near_refs:
        targets += [ref.at[pl.ds(0, QBLK)], ref.at[pl.ds(QBLK, QBLK)]]
    targets += [far_ref, swap_ref.at[pl.ds(QBLK, QBLK)]]
    for index, out_ref in enumerate(targets):
        target = 2 * ring_chip((place + order[index // 2]) & (chips - 1)) + ((me & 1) ^ (index % 2))

        def body(slot, block):
            local = pairs_ref[target * slots + slot] - me * held
            return jnp.where((local >= 0) & (local < held), local, block)

        block = over_slots(slots, body, jnp.int32(0))
        out_ref[...] = query_ref[pl.ds(pl.multiple_of(block * QBLK, QBLK), QBLK), :]


def cross_kernel(*refs):
    count = len(refs) // 2
    for ref, out_ref in zip(refs[:count], refs[count:]):
        out_ref[...] = ref[QBLK:]


def make_factors(rows, width, factors_ref, left_ref, right_ref):
    in_width = factors_ref.shape[0] - width
    half = left_ref.shape[1] // 2
    span = right_ref.shape[1]
    outs = split_bf16(factors_ref[:width])
    ins = split_bf16(factors_ref[width:])
    row = lax.broadcasted_iota(jnp.int32, (half // QBLK, width), 0)
    row_o = lax.broadcasted_iota(jnp.int32, (half // QBLK, width), 1)
    col = lax.broadcasted_iota(jnp.int32, (width, half), 1) // QBLK
    col_o = lax.broadcasted_iota(jnp.int32, (width, half), 0)
    a = lax.broadcasted_iota(jnp.int32, (half, half), 1) - lax.broadcasted_iota(jnp.int32, (half, half), 0)
    same = (a & (QBLK - 1)) == lax.axis_index("layer") * rows
    for h in range(2):
        for s in range(2):
            pick_rows = (row * 2 + s == row_o).astype(BF16)
            part = jnp.dot(pick_rows, outs[h], preferred_element_type=F32).astype(BF16)
            start = (2 * h + s) * half
            for t in range(2):
                pick_cols = (col * 2 + (s ^ t) == col_o).astype(BF16)
                spread = jnp.dot(part, pick_cols, preferred_element_type=F32)
                tall = jnp.broadcast_to(spread[:, None, :], (half // QBLK, QBLK, half)).reshape(half, half)
                left_ref[start : start + half, t * half : (t + 1) * half] = jnp.where(same, tall, 0.0).astype(BF16)
    up = (
        lax.broadcasted_iota(jnp.int32, (span, in_width), 0) % in_width
        == lax.broadcasted_iota(jnp.int32, (span, in_width), 1)
    ).astype(BF16)
    down = (
        lax.broadcasted_iota(jnp.int32, (in_width, span), 1) % in_width
        == lax.broadcasted_iota(jnp.int32, (in_width, span), 0)
    ).astype(BF16)
    block = (lax.broadcasted_iota(jnp.int32, (span, span), 0) // in_width) == (
        lax.broadcasted_iota(jnp.int32, (span, span), 1) // in_width
    )
    for h in range(2):
        wide = jnp.dot(
            jnp.dot(up, ins[h], preferred_element_type=F32).astype(BF16), down, preferred_element_type=F32
        )
        wide = jnp.where(block, wide, 0.0).astype(BF16)
        right_ref[h * span : (h + 1) * span] = wide
        if h == 0:
            right_ref[2 * span :] = wide


def prepare(blocks, left_ref, right_ref, prep_ref):
    chunks = blocks[0].shape[1] // LANES
    half = LANES // 2
    stacked = []
    for block in blocks:
        tall = jnp.concatenate([block[:, c * LANES : (c + 1) * LANES] for c in range(chunks)], axis=0)
        turned = jnp.concatenate([tall[:, half:], tall[:, :half]], axis=1)
        stacked.append(jnp.concatenate([tall, turned], axis=0))
    stacked = jnp.concatenate(stacked, axis=1)
    tall = jnp.dot(left_ref[...], stacked, preferred_element_type=F32)
    quarter = tall.shape[0] // 4
    parts = [tall[s * quarter : (s + 1) * quarter] + tall[(2 + s) * quarter : (3 + s) * quarter] for s in range(2)]
    lane = lax.broadcasted_iota(jnp.int32, parts[0].shape, 1) % LANES
    high, low = split_bf16(jnp.where(lane < half, parts[0], parts[1]))
    done = jnp.dot(
        jnp.concatenate([high, high, low], axis=1), right_ref[...], preferred_element_type=F32
    ).astype(BF16)
    for side in range(2):
        for c in range(chunks):
            prep_ref[side, :, c * LANES : (c + 1) * LANES] = done[
                c * QBLK : (c + 1) * QBLK, side * LANES : (side + 1) * LANES
            ]


def first_kernel(rows, width, factors_ref, far_ref, swap_ref, left_ref, right_ref, prep_ref):
    make_factors(rows, width, factors_ref, left_ref, right_ref)
    prepare((far_ref[...], swap_ref[QBLK:]), left_ref, right_ref, prep_ref)


def self_kernel(left_ref, right_ref, self_ref, swap_ref, prep_ref):
    prepare((self_ref[...], swap_ref[:QBLK]), left_ref, right_ref, prep_ref)


def near_kernel(left_ref, right_ref, done_ref, *refs):
    prep_ref = refs[-1]
    done = done_ref.shape[0]
    prep_ref[:done] = done_ref[...]
    blocks = [ref[:QBLK] for ref in refs[:-1]]
    for index in range(0, len(blocks), 2):
        prepare(blocks[index : index + 2], left_ref, right_ref, prep_ref.at[pl.ds(done + index, 2)])


def last_kernel(order, layer, held, slots, pairs_ref, late_ref, early_ref, train_ref, *refs):
    outs, rows_ref = refs[:-1], refs[-1]
    chips = len(order)
    ready = early_ref.shape[0]
    me = lax.axis_index("ex")
    wanted = [pairs_ref[me * slots + slot] for slot in range(slots)]
    for slot, q in enumerate(wanted):
        source = jnp.maximum(q, 0) // held
        step = (ring_place(me >> 1, chips) - ring_place(source >> 1, chips)) & (chips - 1)
        side = (source ^ me) & 1
        place = jnp.where(step == order[-1], ready, 0) + side
        for index, taken in enumerate(order[1:-1]):
            place = jnp.where(step == taken, 2 + side * (chips - 2) + index, place)

        @pl.when(place < ready)
        def _():
            rows_ref[slot * QBLK : (slot + 1) * QBLK, :] = early_ref[jnp.minimum(place, ready - 1)]

        @pl.when(place >= ready)
        def _():
            rows_ref[slot * QBLK : (slot + 1) * QBLK, :] = late_ref[jnp.maximum(place - ready, 0)]

    tile = lax.dot_general(
        train_ref[...], rows_ref[...], (((1,), (1,)), ((), ())), preferred_element_type=F32
    ).T
    rows = QBLK // layer
    chosen = []
    for slot, q in enumerate(wanted):
        value = tile[slot * QBLK : (slot + 1) * QBLK]
        chosen.append(jnp.where(q >= 0, value, jnp.zeros_like(value)))
    for m in range(layer):
        part = jnp.concatenate([value[m * rows : (m + 1) * rows] for value in chosen], axis=0)
        outs[m][...] = part.astype(outs[m].dtype)


def finish_kernel(layer, *refs):
    parts, out_ref = refs[:layer], refs[layer]
    total = parts[0][...]
    for part in parts[1:]:
        total = total + part[...].astype(F32)
    rows = out_ref.shape[1]
    for slot in range(out_ref.shape[0]):
        out_ref[slot] = total[slot * rows : (slot + 1) * rows]


def shards(train_grads, query_grads, in_precond, out_precond, pair_blocks):
    ex = lax.axis_size("ex")
    layer = lax.axis_size("layer")
    train_rows, layers, features = train_grads.shape
    assert layers == 1
    held = query_grads.shape[0] // QBLK
    slots = pair_blocks.shape[0] // ex
    rows = QBLK // layer
    train = train_grads.reshape(train_rows, features)
    query = query_grads.reshape(query_grads.shape[0], features)
    in_factor = in_precond.reshape(in_precond.shape[1:])
    out_factor = out_precond.reshape(out_precond.shape[1:])
    limit = pltpu.CompilerParams(vmem_limit_bytes=24 * 2**20)

    groups = ex // 2
    order = sorted(range(groups), key=lambda step: min(step, groups - step))

    def pass_on(array, step, flip=0):
        ring = [ring_chip(place) for place in range(groups)]
        moves = zip(ring, ring[step:] + ring[:step])
        return lax.ppermute(array, "ex", [(2 * a + c, 2 * b + (c ^ flip)) for a, b in moves for c in range(2)])

    one = jax.ShapeDtypeStruct((QBLK, features), BF16)
    two = jax.ShapeDtypeStruct((2 * QBLK, features), BF16)
    self_block, far_block, swap, *near = pl.pallas_call(
        functools.partial(pick_kernel, ex, held, slots, order),
        out_shape=[one, one, two] + [two] * (groups - 2),
        in_specs=[SMEM, VMEM],
        out_specs=[VMEM] * (groups + 1),
        compiler_params=limit,
        name="pick",
    )(pair_blocks, query)
    raw = [pass_on(array, step) for array, step in zip(near, order[1:])]
    swap = pass_on(swap, 0, 1)

    brief = pl.CostEstimate(flops=1000, bytes_accessed=1000, transcendentals=0)
    stack = features // LANES * QBLK
    span = 2 * LANES
    out_factor, in_factor, far_pick = lax.optimization_barrier((out_factor, in_factor, far_block))
    left, right, far = pl.pallas_call(
        functools.partial(first_kernel, rows, out_precond.shape[-1]),
        out_shape=[
            jax.ShapeDtypeStruct((4 * stack, 2 * stack), BF16),
            jax.ShapeDtypeStruct((3 * span, span), BF16),
            jax.ShapeDtypeStruct((2, QBLK, features), BF16),
        ],
        in_specs=[VMEM] * 3,
        out_specs=[VMEM] * 3,
        compiler_params=limit,
        name="first",
        cost_estimate=brief,
    )(jnp.concatenate([out_factor, in_factor], axis=0), far_pick, swap)
    far = pass_on(far, order[-1])

    def prepared(count):
        return jax.ShapeDtypeStruct((count, QBLK, features), BF16)

    early = pl.pallas_call(
        self_kernel,
        out_shape=prepared(2),
        in_specs=[VMEM] * 4,
        out_specs=VMEM,
        compiler_params=limit,
        name="self",
        cost_estimate=brief,
    )(left, right, self_block, swap)
    _, *ready = lax.optimization_barrier((early, *raw))
    crossed = pl.pallas_call(
        cross_kernel,
        out_shape=[one] * len(raw),
        in_specs=[VMEM] * len(raw),
        out_specs=[VMEM] * len(raw),
        compiler_params=limit,
        name="cross",
    )(*ready)
    crossed = [pass_on(array, 0, 1) for array in crossed]
    for name, blocks in (("near", raw), ("crossed", crossed)):
        early = pl.pallas_call(
            near_kernel,
            out_shape=prepared(early.shape[0] + len(raw)),
            in_specs=[VMEM] * (3 + len(blocks)),
            out_specs=VMEM,
            compiler_params=limit,
            name=name,
            cost_estimate=brief,
        )(left, right, early, *blocks)
    parts = pl.pallas_call(
        functools.partial(last_kernel, order, layer, held, slots),
        out_shape=[jax.ShapeDtypeStruct((slots * rows, train_rows), F32)]
        + [jax.ShapeDtypeStruct((slots * rows, train_rows), BF16)] * (layer - 1),
        in_specs=[SMEM] + [VMEM] * 3,
        out_specs=[VMEM] * layer,
        scratch_shapes=[pltpu.VMEM((slots * QBLK, features), BF16)],
        compiler_params=limit,
        name="last",
    )(pair_blocks, far, early, train)

    terms = [parts[0]] + [
        lax.ppermute(parts[m], "layer", [(i, (i + m) % layer) for i in range(layer)]) for m in range(1, layer)
    ]
    out = pl.pallas_call(
        functools.partial(finish_kernel, layer),
        out_shape=jax.ShapeDtypeStruct((slots, rows, train_rows), F32),
        in_specs=[VMEM] * layer,
        out_specs=VMEM,
        compiler_params=limit,
        name="finish",
    )(*terms)
    return jnp.transpose(out, (1, 0, 2))


def solution(mesh):
    in_specs = (
        P("ex", "layer", None),
        P("ex", "layer", None),
        P("layer", None, None),
        P("layer", None, None),
        P(),
    )
    out_specs = P("layer", "ex", None)
    return jax.shard_map(shards, mesh=mesh, in_specs=in_specs, out_specs=out_specs, check_vma=False)
```

```python
import functools

import jax
import jax.numpy as jnp
from jax import lax
from jax.experimental import pallas as pl
from jax.experimental.pallas import tpu as pltpu
from jax.sharding import PartitionSpec as P

QBLK = 16
LANES = 128
F32 = jnp.float32
BF16 = jnp.bfloat16

VMEM = pl.BlockSpec(memory_space=pltpu.VMEM)
SMEM = pl.BlockSpec(memory_space=pltpu.SMEM)


def split_bf16(x):
    high = x.astype(BF16)
    return high, (x - high.astype(F32)).astype(BF16)


def over_slots(slots, body, init):
    if slots > 8:
        return lax.fori_loop(0, slots, body, init)
    for slot in range(slots):
        init = body(slot, init)
    return init


def ring_chip(place):
    return place ^ (place >> 1)


def ring_place(chip, chips):
    place, shift = chip, 1
    while shift < chips:
        place, shift = place ^ (place >> shift), 2 * shift
    return place


def pick_kernel(ex, held, slots, order, pairs_ref, query_ref, self_ref, far_ref, swap_ref, *near_refs):
    me = lax.axis_index("ex")
    chips = ex // 2
    place = ring_place(me >> 1, chips)
    targets = [self_ref, swap_ref.at[pl.ds(0, QBLK)]]
    for ref in near_refs:
        targets += [ref.at[pl.ds(0, QBLK)], ref.at[pl.ds(QBLK, QBLK)]]
    targets += [far_ref, swap_ref.at[pl.ds(QBLK, QBLK)]]
    for index, out_ref in enumerate(targets):
        target = 2 * ring_chip((place + order[index // 2]) & (chips - 1)) + ((me & 1) ^ (index % 2))

        def body(slot, block):
            local = pairs_ref[target * slots + slot] - me * held
            return jnp.where((local >= 0) & (local < held), local, block)

        block = over_slots(slots, body, jnp.int32(0))
        out_ref[...] = query_ref[pl.ds(pl.multiple_of(block * QBLK, QBLK), QBLK), :]


def cross_kernel(*refs):
    count = len(refs) // 2
    for ref, out_ref in zip(refs[:count], refs[count:]):
        out_ref[...] = ref[QBLK:]


def make_factors(rows, width, factors_ref, left_ref, right_ref):
    in_width = factors_ref.shape[0] - width
    half = left_ref.shape[1] // 2
    span = right_ref.shape[1]
    outs = split_bf16(factors_ref[:width])
    ins = split_bf16(factors_ref[width:])
    row = lax.broadcasted_iota(jnp.int32, (half // QBLK, width), 0)
    row_o = lax.broadcasted_iota(jnp.int32, (half // QBLK, width), 1)
    col = lax.broadcasted_iota(jnp.int32, (width, half), 1) // QBLK
    col_o = lax.broadcasted_iota(jnp.int32, (width, half), 0)
    a = lax.broadcasted_iota(jnp.int32, (half, half), 1) - lax.broadcasted_iota(jnp.int32, (half, half), 0)
    same = jnp.where((a & (QBLK - 1)) == lax.axis_index("layer") * rows, 1.0, 0.0).astype(BF16)
    for h in range(2):
        for s in range(2):
            pick_rows = (row * 2 + s == row_o).astype(BF16)
            part = jnp.dot(pick_rows, outs[h], preferred_element_type=F32).astype(BF16)
            start = (2 * h + s) * half
            for t in range(2):
                pick_cols = (col * 2 + (s ^ t) == col_o).astype(BF16)
                spread = jnp.dot(part, pick_cols, preferred_element_type=F32).astype(BF16)
                tall = jnp.broadcast_to(spread[:, None, :], (half // QBLK, QBLK, half)).reshape(half, half)
                left_ref[start : start + half, t * half : (t + 1) * half] = tall * same
    up = (
        lax.broadcasted_iota(jnp.int32, (span, in_width), 0) % in_width
        == lax.broadcasted_iota(jnp.int32, (span, in_width), 1)
    ).astype(BF16)
    down = (
        lax.broadcasted_iota(jnp.int32, (in_width, span), 1) % in_width
        == lax.broadcasted_iota(jnp.int32, (in_width, span), 0)
    ).astype(BF16)
    block = (lax.broadcasted_iota(jnp.int32, (span, span), 0) // in_width) == (
        lax.broadcasted_iota(jnp.int32, (span, span), 1) // in_width
    )
    for h in range(2):
        wide = jnp.dot(
            jnp.dot(up, ins[h], preferred_element_type=F32).astype(BF16), down, preferred_element_type=F32
        )
        wide = jnp.where(block, wide, 0.0).astype(BF16)
        right_ref[h * span : (h + 1) * span] = wide
        if h == 0:
            right_ref[2 * span :] = wide


def prepare(blocks, left_ref, right_ref, prep_ref):
    chunks = blocks[0].shape[1] // LANES
    half = LANES // 2
    stacked = []
    for block in blocks:
        tall = jnp.concatenate([block[:, c * LANES : (c + 1) * LANES] for c in range(chunks)], axis=0)
        turned = jnp.concatenate([tall[:, half:], tall[:, :half]], axis=1)
        stacked.append(jnp.concatenate([tall, turned], axis=0))
    stacked = jnp.concatenate(stacked, axis=1)
    tall = jnp.dot(left_ref[...], stacked, preferred_element_type=F32)
    quarter = tall.shape[0] // 4
    parts = [tall[s * quarter : (s + 1) * quarter] + tall[(2 + s) * quarter : (3 + s) * quarter] for s in range(2)]
    lane = lax.broadcasted_iota(jnp.int32, parts[0].shape, 1) % LANES
    high, low = split_bf16(jnp.where(lane < half, parts[0], parts[1]))
    done = jnp.dot(
        jnp.concatenate([high, high, low], axis=1), right_ref[...], preferred_element_type=F32
    ).astype(BF16)
    for side in range(2):
        for c in range(chunks):
            prep_ref[side, :, c * LANES : (c + 1) * LANES] = done[
                c * QBLK : (c + 1) * QBLK, side * LANES : (side + 1) * LANES
            ]


def first_kernel(rows, width, factors_ref, far_ref, swap_ref, left_ref, right_ref, prep_ref):
    make_factors(rows, width, factors_ref, left_ref, right_ref)
    prepare((far_ref[...], swap_ref[QBLK:]), left_ref, right_ref, prep_ref)


def self_kernel(left_ref, right_ref, self_ref, swap_ref, prep_ref):
    prepare((self_ref[...], swap_ref[:QBLK]), left_ref, right_ref, prep_ref)


def near_kernel(left_ref, right_ref, done_ref, *refs):
    prep_ref = refs[-1]
    done = done_ref.shape[0]
    prep_ref[:done] = done_ref[...]
    blocks = [ref[:QBLK] for ref in refs[:-1]]
    for index in range(0, len(blocks), 2):
        prepare(blocks[index : index + 2], left_ref, right_ref, prep_ref.at[pl.ds(done + index, 2)])


def last_kernel(order, layer, held, slots, pairs_ref, late_ref, early_ref, train_ref, *refs):
    outs, rows_ref = refs[:-1], refs[-1]
    chips = len(order)
    ready = early_ref.shape[0]
    me = lax.axis_index("ex")
    wanted = [pairs_ref[me * slots + slot] for slot in range(slots)]
    for slot, q in enumerate(wanted):
        source = jnp.maximum(q, 0) // held
        step = (ring_place(me >> 1, chips) - ring_place(source >> 1, chips)) & (chips - 1)
        side = (source ^ me) & 1
        place = jnp.where(step == order[-1], ready, 0) + side
        for index, taken in enumerate(order[1:-1]):
            place = jnp.where(step == taken, 2 + side * (chips - 2) + index, place)

        @pl.when(place < ready)
        def _():
            rows_ref[slot * QBLK : (slot + 1) * QBLK, :] = early_ref[jnp.minimum(place, ready - 1)]

        @pl.when(place >= ready)
        def _():
            rows_ref[slot * QBLK : (slot + 1) * QBLK, :] = late_ref[jnp.maximum(place - ready, 0)]

    tile = lax.dot_general(
        train_ref[...], rows_ref[...], (((1,), (1,)), ((), ())), preferred_element_type=F32
    ).T
    rows = QBLK // layer
    chosen = []
    for slot, q in enumerate(wanted):
        value = tile[slot * QBLK : (slot + 1) * QBLK]
        chosen.append(jnp.where(q >= 0, value, jnp.zeros_like(value)))
    for m in range(layer):
        part = jnp.concatenate([value[m * rows : (m + 1) * rows] for value in chosen], axis=0)
        outs[m][...] = part.astype(outs[m].dtype)


def finish_kernel(layer, *refs):
    parts, out_ref = refs[:layer], refs[layer]
    total = parts[0][...]
    for part in parts[1:]:
        total = total + part[...].astype(F32)
    rows = out_ref.shape[1]
    for slot in range(out_ref.shape[0]):
        out_ref[slot] = total[slot * rows : (slot + 1) * rows]


def shards(train_grads, query_grads, in_precond, out_precond, pair_blocks):
    ex = lax.axis_size("ex")
    layer = lax.axis_size("layer")
    train_rows, layers, features = train_grads.shape
    assert layers == 1
    held = query_grads.shape[0] // QBLK
    slots = pair_blocks.shape[0] // ex
    rows = QBLK // layer
    train = train_grads.reshape(train_rows, features)
    query = query_grads.reshape(query_grads.shape[0], features)
    in_factor = in_precond.reshape(in_precond.shape[1:])
    out_factor = out_precond.reshape(out_precond.shape[1:])
    limit = pltpu.CompilerParams(vmem_limit_bytes=24 * 2**20)

    groups = ex // 2
    order = sorted(range(groups), key=lambda step: (min(step, groups - step), -step))

    def pass_on(array, step, flip=0):
        ring = [ring_chip(place) for place in range(groups)]
        moves = zip(ring, ring[step:] + ring[:step])
        return lax.ppermute(array, "ex", [(2 * a + c, 2 * b + (c ^ flip)) for a, b in moves for c in range(2)])

    one = jax.ShapeDtypeStruct((QBLK, features), BF16)
    two = jax.ShapeDtypeStruct((2 * QBLK, features), BF16)
    self_block, far_block, swap, *near = pl.pallas_call(
        functools.partial(pick_kernel, ex, held, slots, order),
        out_shape=[one, one, two] + [two] * (groups - 2),
        in_specs=[SMEM, VMEM],
        out_specs=[VMEM] * (groups + 1),
        compiler_params=limit,
        name="pick",
    )(pair_blocks, query)
    raw = [pass_on(array, step) for array, step in zip(near, order[1:])]
    swap = pass_on(swap, 0, 1)

    brief = pl.CostEstimate(flops=1000, bytes_accessed=1000, transcendentals=0)
    stack = features // LANES * QBLK
    span = 2 * LANES
    out_factor, in_factor, far_pick = lax.optimization_barrier((out_factor, in_factor, far_block))
    left, right, far = pl.pallas_call(
        functools.partial(first_kernel, rows, out_precond.shape[-1]),
        out_shape=[
            jax.ShapeDtypeStruct((4 * stack, 2 * stack), BF16),
            jax.ShapeDtypeStruct((3 * span, span), BF16),
            jax.ShapeDtypeStruct((2, QBLK, features), BF16),
        ],
        in_specs=[VMEM] * 3,
        out_specs=[VMEM] * 3,
        compiler_params=limit,
        name="first",
        cost_estimate=brief,
    )(jnp.concatenate([out_factor, in_factor], axis=0), far_pick, swap)
    far = pass_on(far, order[-1])

    def prepared(count):
        return jax.ShapeDtypeStruct((count, QBLK, features), BF16)

    early = pl.pallas_call(
        self_kernel,
        out_shape=prepared(2),
        in_specs=[VMEM] * 4,
        out_specs=VMEM,
        compiler_params=limit,
        name="self",
        cost_estimate=brief,
    )(left, right, self_block, swap)
    _, *ready = lax.optimization_barrier((early, *raw))
    crossed = pl.pallas_call(
        cross_kernel,
        out_shape=[one] * len(raw),
        in_specs=[VMEM] * len(raw),
        out_specs=[VMEM] * len(raw),
        compiler_params=limit,
        name="cross",
    )(*ready)
    crossed = [pass_on(array, 0, 1) for array in crossed]
    for name, blocks in (("near", raw), ("crossed", crossed)):
        early = pl.pallas_call(
            near_kernel,
            out_shape=prepared(early.shape[0] + len(raw)),
            in_specs=[VMEM] * (3 + len(blocks)),
            out_specs=VMEM,
            compiler_params=limit,
            name=name,
            cost_estimate=brief,
        )(left, right, early, *blocks)
    parts = pl.pallas_call(
        functools.partial(last_kernel, order, layer, held, slots),
        out_shape=[jax.ShapeDtypeStruct((slots * rows, train_rows), F32)]
        + [jax.ShapeDtypeStruct((slots * rows, train_rows), BF16)] * (layer - 1),
        in_specs=[SMEM] + [VMEM] * 3,
        out_specs=[VMEM] * layer,
        scratch_shapes=[pltpu.VMEM((slots * QBLK, features), BF16)],
        compiler_params=limit,
        name="last",
    )(pair_blocks, far, early, train)

    terms = [parts[0]] + [
        lax.ppermute(parts[m], "layer", [(i, (i + m) % layer) for i in range(layer)]) for m in range(1, layer)
    ]
    out = pl.pallas_call(
        functools.partial(finish_kernel, layer),
        out_shape=jax.ShapeDtypeStruct((slots, rows, train_rows), F32),
        in_specs=[VMEM] * layer,
        out_specs=VMEM,
        compiler_params=limit,
        name="finish",
    )(*terms)
    return jnp.transpose(out, (1, 0, 2))


def solution(mesh):
    in_specs = (
        P("ex", "layer", None),
        P("ex", "layer", None),
        P("layer", None, None),
        P("layer", None, None),
        P(),
    )
    out_specs = P("layer", "ex", None)
    return jax.shard_map(shards, mesh=mesh, in_specs=in_specs, out_specs=out_specs, check_vma=False)
```
